32 devices in a mesh: rows: 8 (over z, y), zone: 4 (over x, core).
Axes of the slice: x: 2, y: 2, z: 4, core: 2. Of those that a mesh axis runs over, the one named last changes fastest.
Arguments:
- snapshots: float32 [262144, 256], P(('rows', 'zone')), may hold values from -6 to 6
- tangent: bfloat16 [262144, 512], P(('rows', 'zone')), may hold values from -0.25 to 0.25
- pattern: int32 [2048, 4], P(('rows', 'zone')), may hold values from 0 to 259, as said below
- forcing: float32 [262144], P(('rows', 'zone')), may hold values from -6 to 6
- step_index: int32 [256], replicated, may hold values from 0 to 255, each once
Outputs:
- basis: float32 [262144, 256], P(('rows', 'zone'))
- coefficients: float32 [3, 256], replicated
- residual: float32 [262144], P(('rows', 'zone'))
The draws below stay inside these ranges and needn't reach their ends.
Inputs may be any that keep to these rules, and one draw needn't show every extreme that they name: `pattern`: codes of sources 1 and 3 name one of the last 4 blocks of the neighbour, codes of sources 2 and 4 one of its first 4 blocks. `step_index`: each step index once.
All inputs are finite; a program needn't handle non-finite values.
Results may differ from the reference program's by a relative error of at most 0.0003.
Values sent between devices are 32-bit elements; how exact they have to be, the bound alone decides.
No kernel may reach another device: no remote copies, remote signals or barrier semaphores. Data moves between devices by JAX's collectives and lax.ppermute only.
A program may use at most 320 MiB of HBM per device.

```python
import math
import jax
import jax.numpy as jnp
from jax import lax

SNAPS = 256
ROWS_DEV = 8192
BLOCK = 128
COUPLED = 4
HALO = 4
STEPS = 3
BLK_DEV = 64
NDOF = 262144
N_ROWS = 8
N_ZONE = 4


smooth_waves = 4


def draw_snapshots(key, part):
    key_noise, key_amplitude = jax.random.split(jax.random.fold_in(key, 101))
    position = jnp.arange(NDOF, dtype=jnp.float32) / NDOF
    noise_part = jax.random.normal(key_noise, (NDOF, SNAPS), jnp.float32)
    amplitude = jax.random.normal(key_amplitude, (2 * smooth_waves, SNAPS), jnp.float32) * 0.6
    summed = noise_part
    for wave_index in range(smooth_waves):
        wave_phase = 2.0 * math.pi * (wave_index + 1) * position
        summed = summed + jnp.cos(wave_phase)[:, None] * amplitude[2 * wave_index][None, :]
        summed = summed + jnp.sin(wave_phase)[:, None] * amplitude[2 * wave_index + 1][None, :]
    return jnp.clip(summed, -6.0, 6.0)


def draw_tangent(key, part):
    key_noise, key_level = jax.random.split(jax.random.fold_in(key, 202))
    tile_width = COUPLED * BLOCK
    noise_scale = float(tile_width) ** (-0.5)
    noise_part = jax.random.normal(key_noise, (NDOF, tile_width), jnp.float32) * noise_scale
    coherent_level = jax.random.uniform(key_level, (NDOF // BLOCK, COUPLED), jnp.float32, 0.5, 1.5) / tile_width
    coherent_part = jnp.repeat(jnp.repeat(coherent_level, BLOCK, axis=0), BLOCK, axis=1)
    return jnp.clip(noise_part + coherent_part, -0.25, 0.25).astype(jnp.bfloat16)


def draw_pattern(key, part):
    key_source, key_local, key_edge = jax.random.split(key, 3)
    shape = (NDOF // BLOCK, COUPLED)
    picker = jax.random.randint(key_source, shape, 0, 8)
    source = jnp.maximum(picker - 3, 0)
    local_block = jax.random.randint(key_local, shape, 0, BLK_DEV)
    edge_block = jax.random.randint(key_edge, shape, 0, HALO)
    from_tail = (source == 1) | (source == 3)
    block_pick = jnp.where(source == 0, local_block, jnp.where(from_tail, BLK_DEV - HALO + edge_block, edge_block))
    codes = source * BLK_DEV + block_pick
    codes = codes.at[0, 0].set(4 * BLK_DEV + HALO - 1)
    codes = codes.at[1, 0].set(0)
    return codes.astype(jnp.int32)


def shard_levels(stream_key, shape, cuts, smallest, largest):
    loudness = 1.0
    for dim, blocks in cuts:
        heights = jax.random.uniform(jax.random.fold_in(jax.random.fold_in(stream_key, 6), dim), (blocks,), jnp.float32, smallest / len(cuts), largest / len(cuts))
        loudness = loudness * jnp.repeat(jnp.exp(heights), shape[dim] // blocks).reshape((-1,) + (1,) * (len(shape) - 1 - dim))
    return loudness


def gaussian(rng, dims, width, most, pieces=(), held_as=jnp.bfloat16):
    drawn = width * jax.random.normal(rng, dims, jnp.float32)
    if pieces:
        drawn = drawn * shard_levels(rng, dims, pieces, -0.22, 0.18)
    return jnp.clip(drawn, -most, most).astype(held_as)


def setup_inputs(seed: int = 0) -> dict:
    arg_keys = jax.random.split(jax.random.key(seed), 6)
    snapshots = draw_snapshots(jax.random.fold_in(arg_keys[5], 71), 0)
    tangent = draw_tangent(jax.random.fold_in(arg_keys[5], 71), 0)
    pattern = draw_pattern(jax.random.fold_in(arg_keys[5], 71), 0)
    forcing = gaussian(arg_keys[3], (NDOF,), 1.0, 6.0, ((0, 32),), jnp.float32)
    step_index = jax.random.permutation(arg_keys[4], SNAPS).astype(jnp.int32)
    return dict(snapshots=snapshots, tangent=tangent, pattern=pattern, forcing=forcing, step_index=step_index)


step_size = 0.25

def tangent_product(field_in, tangent, pattern):
    highest = lax.Precision.HIGHEST
    block_count = NDOF // BLOCK
    device_count = NDOF // ROWS_DEV
    block_index = jnp.arange(block_count, dtype=jnp.int32)
    device_of = (block_index // BLK_DEV)[:, None]
    row_of = device_of // N_ZONE
    zone_of = device_of % N_ZONE
    source = pattern // BLK_DEV
    block_pick = pattern % BLK_DEV
    target_row = jnp.where(source == 1, (row_of - 1) % N_ROWS, jnp.where(source == 2, (row_of + 1) % N_ROWS, row_of))
    target_zone = jnp.where(source == 3, zone_of - 1, jnp.where(source == 4, zone_of + 1, zone_of))
    present = (target_zone >= 0) & (target_zone < N_ZONE)
    col_block = ((target_row * N_ZONE + jnp.clip(target_zone, 0, N_ZONE - 1)) * BLK_DEV + block_pick).astype(jnp.int32)
    blocks = field_in.reshape(block_count, BLOCK, SNAPS)
    tile_blocks = tangent.reshape(device_count, BLK_DEV, BLOCK, COUPLED, BLOCK)
    col_block = col_block.reshape(device_count, BLK_DEV, COUPLED)
    present = present.reshape(device_count, BLK_DEV, COUPLED)

    def one_device(item):
        tiles, columns, mask_here = item
        picked = blocks[columns] * mask_here.astype(jnp.float32)[:, :, None, None]
        return jnp.einsum('gbec,gecs->gbs', tiles.astype(jnp.float32), picked, precision=highest)
    product = lax.map(one_device, (tile_blocks, col_block, present))
    return product.reshape(NDOF, SNAPS)

def reference(snapshots, tangent, pattern, forcing, step_index):
    highest = lax.Precision.HIGHEST
    inverse_count = 1.0 / NDOF
    identity = jnp.eye(SNAPS, dtype=jnp.float32)
    gram_matrix = jnp.dot(snapshots.T, snapshots, precision=highest) * inverse_count
    factor_low = jnp.linalg.cholesky(gram_matrix)
    inverse = jax.scipy.linalg.solve_triangular(factor_low, identity, lower=True).T
    basis = jnp.dot(snapshots, inverse, precision=highest)
    tangent_image = tangent_product(basis, tangent, pattern)
    trial_basis = basis + step_size * tangent_image
    normal = jnp.dot(trial_basis.T, trial_basis, precision=highest) * inverse_count
    project = jnp.dot(trial_basis.T, basis, precision=highest) * inverse_count
    load_vector = jnp.dot(trial_basis.T, forcing, precision=highest) * inverse_count
    latest = (step_index == jnp.max(step_index)).astype(jnp.float32)
    coeff_now = jnp.dot(latest, factor_low, precision=highest)
    normal_low = jnp.linalg.cholesky(normal)
    history = []
    coeff_old = coeff_now
    for iteration in range(STEPS):
        coeff_old = coeff_now
        right_side = jnp.dot(project, coeff_now, precision=highest) + step_size * load_vector
        coeff_now = jax.scipy.linalg.cho_solve((normal_low, True), right_side)
        history.append(coeff_now)
    residual = jnp.dot(trial_basis, coeff_now, precision=highest) - jnp.dot(basis, coeff_old, precision=highest) - step_size * forcing
    return (basis, jnp.stack(history), residual)
```

```python
import functools

import jax
import jax.numpy as jnp
from jax import lax
from jax.experimental import pallas as pl
from jax.experimental.pallas import tpu as pltpu
from jax.sharding import PartitionSpec as P

HALO = 4
STEPS = 3
STEP_SIZE = 0.25
CHUNK = 1024
LIMIT = 56 * 1024 * 1024
F32 = jnp.float32
BF16 = jnp.bfloat16
HIGHEST = lax.Precision.HIGHEST


def split(value):
    high = value.astype(BF16)
    low = (value - high.astype(F32)).astype(BF16)
    return high, low


def contract_rows(left, right):
    return lax.dot_general(left, right, (((0,), (0,)), ((), ())), preferred_element_type=F32)


def matmul(left, right, precision=None):
    return lax.dot_general(
        left, right, (((1,), (0,)), ((), ())), preferred_element_type=F32, precision=precision
    )


def reversed_bits(value, count):
    result = value * 0
    for bit in range(count):
        result = result | (((value >> bit) & 1) << (count - 1 - bit))
    return result


def gram_kernel(snap_ref, out_ref):
    high, low = split(snap_ref[...])
    part = contract_rows(high, jnp.concatenate([high, low], 1))

    @pl.when(pl.program_id(0) == 0)
    def _():
        out_ref[...] = part

    @pl.when(pl.program_id(0) > 0)
    def _():
        out_ref[...] += part


def gram_call(snapshots):
    rows, snaps = snapshots.shape
    return pl.pallas_call(
        gram_kernel,
        out_shape=jax.ShapeDtypeStruct((snaps, 2 * snaps), F32),
        grid=(rows // CHUNK,),
        in_specs=[pl.BlockSpec((CHUNK, snaps), lambda i: (i, 0))],
        out_specs=pl.BlockSpec((snaps, 2 * snaps), lambda i: (0, 0)),
        compiler_params=pltpu.CompilerParams(vmem_limit_bytes=LIMIT),
        cost_estimate=pl.CostEstimate(
            flops=4 * rows * snaps * snaps, bytes_accessed=4 * rows * snaps, transcendentals=0
        ),
        name="gram",
    )(snapshots)


def tangent_kernel(
    parts,
    pattern_ref,
    place_ref,
    snap_any,
    prev_any,
    next_any,
    left_any,
    right_any,
    tangent_ref,
    force_ref,
    gram_ref,
    image_ref,
    pack_ref,
    snap,
    halo,
    field,
    shared,
    acc,
    cross,
    load,
    sems,
):
    step = pl.program_id(0)
    rows, snaps = snap.shape
    block_count = pattern_ref.shape[0]
    block = rows // block_count
    edge = HALO * block
    chunks = rows // CHUNK
    per_chunk = CHUNK // block

    @pl.when(step == 0)
    def _():
        copies = []
        for i in range(chunks):
            at = pl.ds(i * CHUNK, CHUNK)
            copies.append(pltpu.make_async_copy(snap_any.at[at, :], snap.at[at, :], sems.at[i]))
        for i, ref in enumerate((prev_any, next_any, left_any, right_any)):
            at = pl.ds(i * edge, edge)
            copies.append(pltpu.make_async_copy(ref, halo.at[at, :], sems.at[chunks + i]))
        for copy in copies:
            copy.start()
        for i in range(chunks):
            copies[i].wait()
            at = pl.ds(i * CHUNK, CHUNK)
            high, low = split(snap[at, :])
            field[at, :snaps] = high
            field[at, snaps:] = low
        for i in range(4):
            copies[chunks + i].wait()
            high, low = split(halo[pl.ds(i * edge, edge), :])
            at = pl.ds(rows + i * edge, edge)
            field[at, :snaps] = high
            field[at, snaps:] = low
        shared[...] = jnp.zeros_like(shared)
        acc[...] = jnp.zeros_like(acc)
        cross[...] = jnp.zeros_like(cross)
        load[...] = jnp.zeros_like(load)

    @pl.when(step < chunks)
    def _():
        force_columns = force_ref[...].T
        load_part = jnp.zeros((1, snaps), F32)
        trial_parts = []
        for k in range(per_chunk):
            g = step * per_chunk + k
            picked = []
            for e in range(pattern_ref.shape[1]):
                code = pattern_ref[g, e]
                source = lax.div(code, block_count)
                pick = lax.rem(code, block_count)
                tail = (source == 1) | (source == 3)
                base = jnp.where(source == 0, 0, block_count + (source - 1) * HALO)
                place = base + jnp.where(tail, pick - (block_count - HALO), pick)
                picked.append(field[pl.ds(pl.multiple_of(place * block, block), block), :])
            both = matmul(tangent_ref[k * block : (k + 1) * block, :], jnp.concatenate(picked, 0))
            image = STEP_SIZE * (both[:, :snaps] + both[:, snaps:])
            image_ref[k * block : (k + 1) * block, :] = image
            start = pl.multiple_of(g * block, block)
            trial = snap[pl.ds(start, block), :] + image
            load_part += jnp.sum(trial * force_columns[:, k : k + 1], 0, keepdims=True)
            trial_parts.append(trial)
        trial_high, trial_low = split(jnp.concatenate(trial_parts, 0))
        here = field[pl.ds(pl.multiple_of(step * CHUNK, CHUNK), CHUNK), :]
        shared[...] += contract_rows(trial_high, here)
        acc[...] += contract_rows(trial_high, jnp.concatenate([trial_high, trial_low], 1))
        cross[...] += contract_rows(here[:, :snaps], trial_low)
        load[...] += load_part

    @pl.when(step == chunks)
    def _():
        gram = gram_ref[:, :snaps] + gram_ref[:, snaps:] + gram_ref[:, snaps:].T
        project = shared[:, :snaps] + shared[:, snaps:] + cross[...].T
        mixed = acc[:, snaps:]
        normal = acc[:, :snaps] + mixed + mixed.T
        row = lax.broadcasted_iota(jnp.int32, (snaps, snaps), 0)
        column = lax.broadcasted_iota(jnp.int32, (snaps, snaps), 1)
        packed = jnp.where(row <= column, gram, normal)
        diagonal = jnp.sum(jnp.where(row == column, normal, 0.0), 0, keepdims=True)
        share = snaps // parts
        extra_row = lax.broadcasted_iota(jnp.int32, (8, snaps), 0)
        extra = jnp.where(extra_row == 0, load[...], jnp.where(extra_row == 1, diagonal, 0.0))
        bits = parts.bit_length() - 1
        for c in range(parts):
            at = reversed_bits(place_ref[0] ^ c, bits)
            pack_ref[at, :share, :] = packed[c * share : (c + 1) * share]
            pack_ref[at, share : 2 * share, :] = project[c * share : (c + 1) * share]
            pack_ref[at, 2 * share :, :] = extra


def tangent_call(snapshots, halos, tangent, pattern, force, gram, place, parts):
    rows, snaps = snapshots.shape
    blocks, coupled = pattern.shape
    block = rows // blocks
    share = snaps // parts
    chunks = rows // CHUNK
    hbm = pl.BlockSpec(memory_space=pl.ANY)
    return pl.pallas_call(
        functools.partial(tangent_kernel, parts),
        out_shape=(
            jax.ShapeDtypeStruct((rows, snaps), F32),
            jax.ShapeDtypeStruct((parts, 2 * share + 8, snaps), F32),
        ),
        grid_spec=pltpu.PrefetchScalarGridSpec(
            num_scalar_prefetch=2,
            grid=(chunks + 1,),
            in_specs=[
                hbm,
                hbm,
                hbm,
                hbm,
                hbm,
                pl.BlockSpec((CHUNK, coupled * block), lambda i, *_: (jnp.minimum(i, chunks - 1), 0)),
                pl.BlockSpec((CHUNK // block, block), lambda i, *_: (jnp.minimum(i, chunks - 1), 0)),
                pl.BlockSpec((snaps, 2 * snaps), lambda i, *_: (0, 0)),
            ],
            out_specs=[
                pl.BlockSpec((CHUNK, snaps), lambda i, *_: (jnp.minimum(i, chunks - 1), 0)),
                pl.BlockSpec((parts, 2 * share + 8, snaps), lambda i, *_: (0, 0, 0)),
            ],
            scratch_shapes=[
                pltpu.VMEM((rows, snaps), F32),
                pltpu.VMEM((4 * HALO * block, snaps), F32),
                pltpu.VMEM((rows + 4 * HALO * block, 2 * snaps), BF16),
                pltpu.VMEM((snaps, 2 * snaps), F32),
                pltpu.VMEM((snaps, 2 * snaps), F32),
                pltpu.VMEM((snaps, snaps), F32),
                pltpu.VMEM((1, snaps), F32),
                pltpu.SemaphoreType.DMA((chunks + 4,)),
            ],
        ),
        compiler_params=pltpu.CompilerParams(vmem_limit_bytes=LIMIT),
        cost_estimate=pl.CostEstimate(
            flops=18 * rows * snaps * snaps, bytes_accessed=12 * rows * snaps, transcendentals=0
        ),
        name="tangent",
    )(pattern, place, snapshots, *halos, tangent, force, gram)


def inverse_factors(blocks):
    size = blocks[0].shape[0]
    groups = size // 8
    lane = lax.broadcasted_iota(jnp.int32, (8, size), 1)
    sub = lax.broadcasted_iota(jnp.int32, (8, size), 0)
    spread = lambda value: jnp.broadcast_to(value, (8, size))
    count = len(blocks)
    rows = [[value[8 * g : 8 * g + 8, :] for g in range(groups)] for value in blocks]
    done = [[] for _ in blocks]
    for g in range(groups):
        first = 8 * g
        inside = (lane >= first) & (lane < first + 8)
        unit = jnp.where(lane == sub + first, 1.0, 0.0)
        columns = [
            [spread(rows[m][g][:, first + j : first + j + 1]) for j in range(8)] for m in range(count)
        ]
        work = [jnp.where(inside, unit, rows[m][g]) for m in range(count)]
        kept = [jnp.zeros((8, size), F32) for _ in range(count)]
        for j in range(8):
            for m in range(count):
                pivot = spread(columns[m][j][j : j + 1, :])
                inverse = 1.0 / pivot
                root = lax.rsqrt(pivot)
                root = root * (1.5 - 0.5 * pivot * root * root)
                mine = sub == j
                for k in range(j + 1, 8):
                    scaled = spread(columns[m][k][j : j + 1, :]) * inverse
                    columns[m][k] = jnp.where(mine, scaled, columns[m][k] - columns[m][j] * scaled)
                row = spread(work[m][j : j + 1, :])
                kept[m] = jnp.where(mine, row * root, kept[m])
                scaled = row * inverse
                work[m] = jnp.where(mine, scaled, work[m] - columns[m][j] * scaled)
        for m in range(count):
            done[m].append(jnp.where(lane < first + 8, kept[m], 0.0))
            pivots = [spread(work[m][j : j + 1, :]) for j in range(8)]
            for i in range(g + 1, groups):
                old = rows[m][i]
                new = jnp.where(inside, 0.0, old)
                for j in range(8):
                    new = new - spread(old[:, first + j : first + j + 1]) * pivots[j]
                rows[m][i] = new
    return [jnp.concatenate(values, 0) for values in done]


def dot_last(left, right):
    return lax.dot_general(
        left, right, (((1,), (1,)), ((), ())), preferred_element_type=F32, precision=HIGHEST
    )


def reduced_kernel(parts, inverse_count, place_ref, pack_ref, index_ref, root_ref, coeff_ref, state_ref):
    snaps = pack_ref.shape[2]
    share = snaps // parts
    half = snaps // 2
    bits = parts.bit_length() - 1
    order = [reversed_bits(place_ref[0] ^ c, bits) for c in range(parts)]
    packed = jnp.concatenate([pack_ref[at, :share, :] for at in order], 0) * inverse_count
    project = jnp.concatenate([pack_ref[at, share : 2 * share, :] for at in order], 0) * inverse_count
    load = pack_ref[order[0], 2 * share : 2 * share + 1, :] * inverse_count
    diagonal = pack_ref[order[0], 2 * share + 1 : 2 * share + 2, :] * inverse_count
    row = lax.broadcasted_iota(jnp.int32, (snaps, snaps), 0)
    column = lax.broadcasted_iota(jnp.int32, (snaps, snaps), 1)
    turned = packed.T
    gram = jnp.where(row <= column, packed, turned)
    normal = jnp.where(row > column, packed, jnp.where(row == column, diagonal, turned))

    pair = (gram, normal)
    upper = inverse_factors([value[:half, :half] for value in pair])
    below = [dot_last(value[half:, :half], inv) for value, inv in zip(pair, upper)]
    rest = [value[half:, half:] - dot_last(low, low) for value, low in zip(pair, below)]
    lower = inverse_factors(rest)
    inverses = []
    for top, low, bottom in zip(upper, below, lower):
        corner = -matmul(bottom, matmul(low, top, HIGHEST), HIGHEST)
        inverses.append(
            jnp.concatenate(
                [
                    jnp.concatenate([top, jnp.zeros((half, half), F32)], 1),
                    jnp.concatenate([corner, bottom], 1),
                ],
                0,
            )
        )
    gram_inverse, normal_inverse = inverses
    root = gram_inverse.T
    high, low = split(root)
    root_ref[:, :snaps] = high
    root_ref[:, snaps:] = low

    across = lambda matrix, vector: jnp.sum(matrix * vector, 1, keepdims=True)
    down = lambda matrix, vector: jnp.sum(matrix * vector, 0, keepdims=True)
    index = index_ref[...]
    state = jnp.where(index == jnp.max(index), 1.0, 0.0)
    eye = jnp.where(row == column, 1.0, 0.0)
    for n in range(STEPS):
        old = state
        right = down(eye, across(project, state)) + STEP_SIZE * load
        state = down(normal_inverse, across(normal_inverse, right))
        coeff_ref[n : n + 1, :] = down(root, across(gram, state))
    state_ref[0:1, :] = state - old
    state_ref[1:2, :] = state


def reduced_call(packed, step_index, place, parts, inverse_count):
    snaps = packed.shape[2]
    vmem = pl.BlockSpec(memory_space=pltpu.VMEM)
    return pl.pallas_call(
        functools.partial(reduced_kernel, parts, inverse_count),
        out_shape=(
            jax.ShapeDtypeStruct((snaps, 2 * snaps), BF16),
            jax.ShapeDtypeStruct((STEPS, snaps), F32),
            jax.ShapeDtypeStruct((2, snaps), F32),
        ),
        in_specs=[pl.BlockSpec(memory_space=pltpu.SMEM), vmem, vmem],
        out_specs=[vmem, vmem, vmem],
        compiler_params=pltpu.CompilerParams(vmem_limit_bytes=LIMIT),
        name="reduced",
    )(place, packed, step_index)


def basis_kernel(snap_ref, image_ref, force_ref, root_ref, state_ref, basis_ref, residual_ref):
    rows, snaps = snap_ref.shape
    block = force_ref.shape[1]
    snap = snap_ref[...]
    high, low = split(snap)
    both = matmul(high, root_ref[...])
    basis_ref[...] = both[:, :snaps] + both[:, snaps:] + matmul(low, root_ref[:, :snaps])
    sums = jnp.sum(snap * state_ref[0:1, :] + image_ref[...] * state_ref[1:2, :], 1, keepdims=True)
    lane = lax.broadcasted_iota(jnp.int32, (block, block), 1)
    tile = jnp.zeros((block, block), F32)
    for k in range(rows // block):
        tile = jnp.where(lane == k, sums[k * block : (k + 1) * block], tile)
    residual_ref[...] = tile.T[: rows // block] - STEP_SIZE * force_ref[...]


def basis_call(snapshots, image, force, root, state):
    rows, snaps = snapshots.shape
    block = force.shape[1]
    panel = pl.BlockSpec((CHUNK, snaps), lambda i: (i, 0))
    line = pl.BlockSpec((CHUNK // block, block), lambda i: (i, 0))
    return pl.pallas_call(
        basis_kernel,
        out_shape=(
            jax.ShapeDtypeStruct((rows, snaps), F32),
            jax.ShapeDtypeStruct((rows // block, block), F32),
        ),
        grid=(rows // CHUNK,),
        in_specs=[
            panel,
            panel,
            line,
            pl.BlockSpec((snaps, 2 * snaps), lambda i: (0, 0)),
            pl.BlockSpec((2, snaps), lambda i: (0, 0)),
        ],
        out_specs=[panel, line],
        compiler_params=pltpu.CompilerParams(vmem_limit_bytes=LIMIT),
        name="basis",
    )(snapshots, image, force, root, state)


def shifted(value, axis, steps):
    count = lax.axis_size(axis)
    pairs = [(source, (source + steps) % count) for source in range(count)]
    return lax.ppermute(value, axis, pairs)


def from_behind(shard, axis, by):
    devices = lax.axis_size(axis)
    pairs = [(i, i + by) for i in range(devices) if 0 <= i + by < devices]
    return lax.ppermute(shard, axis, pairs)


def partner(value, axis, bit):
    count = lax.axis_size(axis)
    return lax.ppermute(value, axis, [(i, i ^ bit) for i in range(count)])


def reduce_packed(value):
    zone_bits = lax.axis_size("zone").bit_length() - 1
    row_bits = lax.axis_size("rows").bit_length() - 1
    for bit in range(zone_bits):
        half = value.shape[0] // 2
        value = value[:half] + partner(value[half:], "zone", 1 << bit)
    for bit in range(row_bits):
        value = value + partner(value, "rows", 1 << bit)
    for bit in reversed(range(zone_bits)):
        value = jnp.concatenate([value, partner(value, "zone", 1 << bit)], 0)
    return value


def shards(snapshots, tangent, pattern, forcing, step_index):
    rows, snaps = snapshots.shape
    blocks = pattern.shape[0]
    block = rows // blocks
    edge = HALO * block
    parts = lax.axis_size("zone")
    inverse_count = 1.0 / (rows * lax.axis_size("rows") * parts)
    place = jnp.reshape(lax.axis_index("zone"), (1,)).astype(jnp.int32)
    force = forcing.reshape(blocks, block)
    head, tail = snapshots[:edge], snapshots[rows - edge :]
    halos = (
        shifted(tail, "rows", 1),
        shifted(head, "rows", -1),
        from_behind(tail, "zone", 1),
        from_behind(head, "zone", -1),
    )
    gram = gram_call(snapshots)
    image, packed = tangent_call(snapshots, halos, tangent, pattern, force, gram, place, parts)
    packed = reduce_packed(packed)
    root, coefficients, state = reduced_call(
        packed, step_index.reshape(1, snaps), place, parts, inverse_count
    )
    basis, residual = basis_call(snapshots, image, force, root, state)
    return basis, coefficients, residual.reshape(rows)


def solution(mesh):
    in_specs = (
        P(("rows", "zone"), None),
        P(("rows", "zone"), None),
        P(("rows", "zone"), None),
        P(("rows", "zone")),
        P(),
    )
    out_specs = (P(("rows", "zone"), None), P(), P(("rows", "zone")))
    return jax.shard_map(shards, mesh=mesh, in_specs=in_specs, out_specs=out_specs, check_vma=False)
```

```python
import functools

import jax
import jax.numpy as jnp
from jax import lax
from jax.experimental import pallas as pl
from jax.experimental.pallas import tpu as pltpu
from jax.sharding import PartitionSpec as P

HALO = 4
STEPS = 3
STEP_SIZE = 0.25
CHUNK = 1024
LIMIT = 56 * 1024 * 1024
F32 = jnp.float32
BF16 = jnp.bfloat16
HIGHEST = lax.Precision.HIGHEST


def split(value):
    high = value.astype(BF16)
    low = (value - high.astype(F32)).astype(BF16)
    return high, low


def contract_rows(left, right):
    return lax.dot_general(left, right, (((0,), (0,)), ((), ())), preferred_element_type=F32)


def matmul(left, right, precision=None):
    return lax.dot_general(
        left, right, (((1,), (0,)), ((), ())), preferred_element_type=F32, precision=precision
    )


def reversed_bits(value, count):
    result = value * 0
    for bit in range(count):
        result = result | (((value >> bit) & 1) << (count - 1 - bit))
    return result


def gram_kernel(snap_ref, out_ref):
    high, low = split(snap_ref[...])
    part = contract_rows(high, jnp.concatenate([high, low], 1))

    @pl.when(pl.program_id(0) == 0)
    def _():
        out_ref[...] = part

    @pl.when(pl.program_id(0) > 0)
    def _():
        out_ref[...] += part


def gram_call(snapshots):
    rows, snaps = snapshots.shape
    return pl.pallas_call(
        gram_kernel,
        out_shape=jax.ShapeDtypeStruct((snaps, 2 * snaps), F32),
        grid=(rows // CHUNK,),
        in_specs=[pl.BlockSpec((CHUNK, snaps), lambda i: (i, 0))],
        out_specs=pl.BlockSpec((snaps, 2 * snaps), lambda i: (0, 0)),
        compiler_params=pltpu.CompilerParams(vmem_limit_bytes=LIMIT),
        cost_estimate=pl.CostEstimate(
            flops=4 * rows * snaps * snaps, bytes_accessed=4 * rows * snaps, transcendentals=0
        ),
        name="gram",
    )(snapshots)


def tangent_kernel(
    parts,
    pattern_ref,
    place_ref,
    snap_any,
    prev_any,
    next_any,
    left_any,
    right_any,
    tangent_ref,
    force_ref,
    gram_ref,
    image_ref,
    keep_ref,
    send_ref,
    snap,
    halo,
    field,
    shared,
    acc,
    cross,
    load,
    packed,
    sems,
):
    step = pl.program_id(0)
    rows, snaps = snap.shape
    block_count = pattern_ref.shape[0]
    block = rows // block_count
    edge = HALO * block
    chunks = rows // CHUNK
    per_chunk = CHUNK // block

    @pl.when(step == 0)
    def _():
        copies = []
        for i in range(chunks):
            at = pl.ds(i * CHUNK, CHUNK)
            copies.append(pltpu.make_async_copy(snap_any.at[at, :], snap.at[at, :], sems.at[i]))
        for i, ref in enumerate((prev_any, next_any, left_any, right_any)):
            at = pl.ds(i * edge, edge)
            copies.append(pltpu.make_async_copy(ref, halo.at[at, :], sems.at[chunks + i]))
        for copy in copies:
            copy.start()
        for i in range(chunks):
            copies[i].wait()
            at = pl.ds(i * CHUNK, CHUNK)
            high, low = split(snap[at, :])
            field[at, :snaps] = high
            field[at, snaps:] = low
        for i in range(4):
            copies[chunks + i].wait()
            high, low = split(halo[pl.ds(i * edge, edge), :])
            at = pl.ds(rows + i * edge, edge)
            field[at, :snaps] = high
            field[at, snaps:] = low
        shared[...] = jnp.zeros_like(shared)
        acc[...] = jnp.zeros_like(acc)
        cross[...] = jnp.zeros_like(cross)
        load[...] = jnp.zeros_like(load)

    @pl.when(step < chunks)
    def _():
        force_columns = force_ref[...].T
        load_part = jnp.zeros((1, snaps), F32)
        trial_parts = []
        for k in range(per_chunk):
            g = step * per_chunk + k
            picked = []
            for e in range(pattern_ref.shape[1]):
                code = pattern_ref[g, e]
                source = lax.div(code, block_count)
                pick = lax.rem(code, block_count)
                tail = (source == 1) | (source == 3)
                base = jnp.where(source == 0, 0, block_count + (source - 1) * HALO)
                place = base + jnp.where(tail, pick - (block_count - HALO), pick)
                picked.append(field[pl.ds(pl.multiple_of(place * block, block), block), :])
            both = matmul(tangent_ref[k * block : (k + 1) * block, :], jnp.concatenate(picked, 0))
            image = STEP_SIZE * (both[:, :snaps] + both[:, snaps:])
            image_ref[k * block : (k + 1) * block, :] = image
            start = pl.multiple_of(g * block, block)
            trial = snap[pl.ds(start, block), :] + image
            load_part += jnp.sum(trial * force_columns[:, k : k + 1], 0, keepdims=True)
            trial_parts.append(trial)
        trial_high, trial_low = split(jnp.concatenate(trial_parts, 0))
        here = field[pl.ds(pl.multiple_of(step * CHUNK, CHUNK), CHUNK), :]
        shared[...] += contract_rows(trial_high, here)
        acc[...] += contract_rows(trial_high, jnp.concatenate([trial_high, trial_low], 1))
        cross[...] += contract_rows(here[:, :snaps], trial_low)
        load[...] += load_part

    @pl.when(step == chunks)
    def _():
        gram = gram_ref[:, :snaps] + gram_ref[:, snaps:] + gram_ref[:, snaps:].T
        project = shared[:, :snaps] + shared[:, snaps:] + cross[...].T
        mixed = acc[:, snaps:]
        normal = acc[:, :snaps] + mixed + mixed.T
        row = lax.broadcasted_iota(jnp.int32, (snaps, snaps), 0)
        column = lax.broadcasted_iota(jnp.int32, (snaps, snaps), 1)
        diagonal = jnp.sum(jnp.where(row == column, normal, 0.0), 0, keepdims=True)
        packed[0] = jnp.where(row <= column, gram, normal)
        packed[1] = project
        share = snaps // parts
        extra_row = lax.broadcasted_iota(jnp.int32, (8, snaps), 0)
        extra = jnp.where(extra_row == 0, load[...], jnp.where(extra_row == 1, diagonal, 0.0))
        bits = parts.bit_length() - 1
        for at in range(parts):
            out = keep_ref if at < parts // 2 else send_ref
            slot = at % (parts // 2)
            start = pl.multiple_of((place_ref[0] ^ reversed_bits(at, bits)) * share, 8)
            out[slot, :share, :] = packed[0, pl.ds(start, share), :]
            out[slot, share : 2 * share, :] = packed[1, pl.ds(start, share), :]
            out[slot, 2 * share :, :] = extra


def tangent_call(snapshots, halos, tangent, pattern, force, gram, place, parts):
    rows, snaps = snapshots.shape
    blocks, coupled = pattern.shape
    block = rows // blocks
    share = snaps // parts
    chunks = rows // CHUNK
    hbm = pl.BlockSpec(memory_space=pl.ANY)
    return pl.pallas_call(
        functools.partial(tangent_kernel, parts),
        out_shape=(
            jax.ShapeDtypeStruct((rows, snaps), F32),
            jax.ShapeDtypeStruct((parts // 2, 2 * share + 8, snaps), F32),
            jax.ShapeDtypeStruct((parts // 2, 2 * share + 8, snaps), F32),
        ),
        grid_spec=pltpu.PrefetchScalarGridSpec(
            num_scalar_prefetch=2,
            grid=(chunks + 1,),
            in_specs=[
                hbm,
                hbm,
                hbm,
                hbm,
                hbm,
                pl.BlockSpec((CHUNK, coupled * block), lambda i, *_: (jnp.minimum(i, chunks - 1), 0)),
                pl.BlockSpec((CHUNK // block, block), lambda i, *_: (jnp.minimum(i, chunks - 1), 0)),
                pl.BlockSpec((snaps, 2 * snaps), lambda i, *_: (0, 0)),
            ],
            out_specs=[
                pl.BlockSpec((CHUNK, snaps), lambda i, *_: (jnp.minimum(i, chunks - 1), 0)),
                pl.BlockSpec((parts // 2, 2 * share + 8, snaps), lambda i, *_: (0, 0, 0)),
                pl.BlockSpec((parts // 2, 2 * share + 8, snaps), lambda i, *_: (0, 0, 0)),
            ],
            scratch_shapes=[
                pltpu.VMEM((rows, snaps), F32),
                pltpu.VMEM((4 * HALO * block, snaps), F32),
                pltpu.VMEM((rows + 4 * HALO * block, 2 * snaps), BF16),
                pltpu.VMEM((snaps, 2 * snaps), F32),
                pltpu.VMEM((snaps, 2 * snaps), F32),
                pltpu.VMEM((snaps, snaps), F32),
                pltpu.VMEM((1, snaps), F32),
                pltpu.VMEM((2, snaps, snaps), F32),
                pltpu.SemaphoreType.DMA((chunks + 4,)),
            ],
        ),
        compiler_params=pltpu.CompilerParams(vmem_limit_bytes=LIMIT),
        cost_estimate=pl.CostEstimate(
            flops=18 * rows * snaps * snaps, bytes_accessed=12 * rows * snaps, transcendentals=0
        ),
        name="tangent",
    )(pattern, place, snapshots, *halos, tangent, force, gram)


def inverse_factors(blocks):
    size = blocks[0].shape[0]
    groups = size // 8
    lane = lax.broadcasted_iota(jnp.int32, (8, size), 1)
    sub = lax.broadcasted_iota(jnp.int32, (8, size), 0)
    spread = lambda value: jnp.broadcast_to(value, (8, size))
    count = len(blocks)
    rows = [[value[8 * g : 8 * g + 8, :] for g in range(groups)] for value in blocks]
    done = [[] for _ in blocks]
    for g in range(groups):
        first = 8 * g
        inside = (lane >= first) & (lane < first + 8)
        unit = jnp.where(lane == sub + first, 1.0, 0.0)
        columns = [
            [spread(rows[m][g][:, first + j : first + j + 1]) for j in range(8)] for m in range(count)
        ]
        work = [jnp.where(inside, unit, rows[m][g]) for m in range(count)]
        kept = [jnp.zeros((8, size), F32) for _ in range(count)]
        for j in range(8):
            for m in range(count):
                pivot = spread(columns[m][j][j : j + 1, :])
                inverse = 1.0 / pivot
                root = lax.rsqrt(pivot)
                root = root * (1.5 - 0.5 * pivot * root * root)
                mine = sub == j
                for k in range(j + 1, 8):
                    scaled = spread(columns[m][k][j : j + 1, :]) * inverse
                    columns[m][k] = jnp.where(mine, scaled, columns[m][k] - columns[m][j] * scaled)
                row = spread(work[m][j : j + 1, :])
                kept[m] = jnp.where(mine, row * root, kept[m])
                scaled = row * inverse
                work[m] = jnp.where(mine, scaled, work[m] - columns[m][j] * scaled)
        for m in range(count):
            done[m].append(jnp.where(lane < first + 8, kept[m], 0.0))
            pivots = [spread(work[m][j : j + 1, :]) for j in range(8)]
            for i in range(g + 1, groups):
                old = rows[m][i]
                new = jnp.where(inside, 0.0, old)
                for j in range(8):
                    new = new - spread(old[:, first + j : first + j + 1]) * pivots[j]
                rows[m][i] = new
    return [jnp.concatenate(values, 0) for values in done]


def dot_last(left, right):
    return lax.dot_general(
        left, right, (((1,), (1,)), ((), ())), preferred_element_type=F32, precision=HIGHEST
    )


def reduced_system(parts, inverse_count, place, pack, index):
    snaps = pack.shape[2]
    share = snaps // parts
    half = snaps // 2
    bits = parts.bit_length() - 1
    order = [reversed_bits(place ^ c, bits) for c in range(parts)]
    packed = jnp.concatenate([pack[at, :share, :] for at in order], 0) * inverse_count
    project = jnp.concatenate([pack[at, share : 2 * share, :] for at in order], 0) * inverse_count
    load = pack[order[0], 2 * share : 2 * share + 1, :] * inverse_count
    diagonal = pack[order[0], 2 * share + 1 : 2 * share + 2, :] * inverse_count
    row = lax.broadcasted_iota(jnp.int32, (snaps, snaps), 0)
    column = lax.broadcasted_iota(jnp.int32, (snaps, snaps), 1)
    turned = packed.T
    gram = jnp.where(row <= column, packed, turned)
    normal = jnp.where(row > column, packed, jnp.where(row == column, diagonal, turned))

    pair = (gram, normal)
    upper = inverse_factors([value[:half, :half] for value in pair])
    below = [dot_last(value[half:, :half], inv) for value, inv in zip(pair, upper)]
    rest = [value[half:, half:] - dot_last(low, low) for value, low in zip(pair, below)]
    lower = inverse_factors(rest)
    inverses = []
    for top, low, bottom in zip(upper, below, lower):
        corner = -matmul(bottom, matmul(low, top, HIGHEST), HIGHEST)
        inverses.append(
            jnp.concatenate(
                [
                    jnp.concatenate([top, jnp.zeros((half, half), F32)], 1),
                    jnp.concatenate([corner, bottom], 1),
                ],
                0,
            )
        )
    gram_inverse, normal_inverse = inverses
    root = gram_inverse.T

    across = lambda matrix, vector: jnp.sum(matrix * vector, 1, keepdims=True)
    down = lambda matrix, vector: jnp.sum(matrix * vector, 0, keepdims=True)
    state = jnp.where(index == jnp.max(index), 1.0, 0.0)
    eye = jnp.where(row == column, 1.0, 0.0)
    history = []
    for _ in range(STEPS):
        old = state
        right = down(eye, across(project, state)) + STEP_SIZE * load
        state = down(normal_inverse, across(normal_inverse, right))
        history.append(down(root, across(gram, state)))
    return root, history, state - old, state


def final_kernel(parts, inverse_count, count, place_ref, *refs):
    pieces = refs[:count]
    index_ref, force_ref, snap_any, image_any, basis_any, coeff_ref, residual_ref = refs[count : count + 7]
    snap, image, pack, root_ref, change_ref, state_ref, sems = refs[count + 7 :]
    rows, snaps = snap.shape
    block = force_ref.shape[1]
    chunks = rows // CHUNK
    per_chunk = CHUNK // block
    copies = [
        pltpu.make_async_copy(snap_any, snap, sems.at[0]),
        pltpu.make_async_copy(image_any, image, sems.at[1]),
    ]
    for copy in copies:
        copy.start()
    first = 0
    for piece in pieces:
        pack[first : first + piece.shape[0]] = piece[...]
        first += piece.shape[0]
    root, history, change, state = reduced_system(parts, inverse_count, place_ref[0], pack, index_ref[...])
    high, low = split(root)
    root_ref[:, :snaps] = high
    root_ref[:, snaps:] = low
    for n in range(STEPS):
        coeff_ref[n : n + 1, :] = history[n]
    change_ref[...] = change
    state_ref[...] = state
    for copy in copies:
        copy.wait()

    lane = lax.broadcasted_iota(jnp.int32, (block, block), 1)

    def out_copy(i):
        at = pl.ds(pl.multiple_of(i * CHUNK, CHUNK), CHUNK)
        return pltpu.make_async_copy(snap.at[at, :], basis_any.at[at, :], sems.at[2 + i])

    @pl.loop(0, chunks)
    def _(i):
        at = pl.ds(pl.multiple_of(i * CHUNK, CHUNK), CHUNK)
        panel = snap[at, :]
        sums = jnp.sum(panel * change_ref[...] + image[at, :] * state_ref[...], 1, keepdims=True)
        tile = jnp.zeros((block, block), F32)
        for k in range(per_chunk):
            tile = jnp.where(lane == k, sums[k * block : (k + 1) * block], tile)
        line = pl.ds(pl.multiple_of(i * per_chunk, per_chunk), per_chunk)
        residual_ref[line, :] = tile.T[:per_chunk] - STEP_SIZE * force_ref[line, :]
        panel_high, panel_low = split(panel)
        both = matmul(panel_high, root_ref[...])
        snap[at, :] = both[:, :snaps] + both[:, snaps:] + matmul(panel_low, root_ref[:, :snaps])
        out_copy(i).start()

    @pl.loop(0, chunks)
    def _(i):
        out_copy(i).wait()


def final_call(pieces, step_index, place, snapshots, image, force, inverse_count):
    rows, snaps = snapshots.shape
    parts = sum(piece.shape[0] for piece in pieces)
    vmem = pl.BlockSpec(memory_space=pltpu.VMEM)
    hbm = pl.BlockSpec(memory_space=pl.ANY)
    return pl.pallas_call(
        functools.partial(final_kernel, parts, inverse_count, len(pieces)),
        out_shape=(
            jax.ShapeDtypeStruct((rows, snaps), F32),
            jax.ShapeDtypeStruct((STEPS, snaps), F32),
            jax.ShapeDtypeStruct(force.shape, F32),
        ),
        in_specs=[pl.BlockSpec(memory_space=pltpu.SMEM)] + [vmem] * (len(pieces) + 2) + [hbm, hbm],
        out_specs=[hbm, vmem, vmem],
        scratch_shapes=[
            pltpu.VMEM((rows, snaps), F32),
            pltpu.VMEM((rows, snaps), F32),
            pltpu.VMEM((parts,) + pieces[0].shape[1:], F32),
            pltpu.VMEM((snaps, 2 * snaps), BF16),
            pltpu.VMEM((1, snaps), F32),
            pltpu.VMEM((1, snaps), F32),
            pltpu.SemaphoreType.DMA((2 + rows // CHUNK,)),
        ],
        compiler_params=pltpu.CompilerParams(vmem_limit_bytes=LIMIT),
        name="final",
    )(place, *pieces, step_index, force, snapshots, image)


def shifted(value, axis, steps):
    count = lax.axis_size(axis)
    pairs = [(source, (source + steps) % count) for source in range(count)]
    return lax.ppermute(value, axis, pairs)


def from_behind(shard, axis, by):
    devices = lax.axis_size(axis)
    pairs = [(i, i + by) for i in range(devices) if 0 <= i + by < devices]
    return lax.ppermute(shard, axis, pairs)


def partner(value, axis, bit):
    count = lax.axis_size(axis)
    return lax.ppermute(value, axis, [(i, i ^ bit) for i in range(count)])


def reduce_packed(keep, send):
    zone_bits = lax.axis_size("zone").bit_length() - 1
    row_bits = lax.axis_size("rows").bit_length() - 1
    value = keep + partner(send, "zone", 1)
    for bit in range(1, zone_bits):
        half = value.shape[0] // 2
        value = value[:half] + partner(value[half:], "zone", 1 << bit)
    for bit in range(row_bits):
        value = value + partner(value, "rows", 1 << bit)
    pieces = [value]
    for bit in reversed(range(zone_bits)):
        pieces += [partner(piece, "zone", 1 << bit) for piece in pieces]
    return pieces


def shards(snapshots, tangent, pattern, forcing, step_index):
    rows, snaps = snapshots.shape
    blocks = pattern.shape[0]
    block = rows // blocks
    edge = HALO * block
    parts = lax.axis_size("zone")
    inverse_count = 1.0 / (rows * lax.axis_size("rows") * parts)
    place = jnp.reshape(lax.axis_index("zone"), (1,)).astype(jnp.int32)
    force = forcing.reshape(blocks, block)
    head, tail = snapshots[:edge], snapshots[rows - edge :]
    halos = (
        shifted(tail, "rows", 1),
        shifted(head, "rows", -1),
        from_behind(tail, "zone", 1),
        from_behind(head, "zone", -1),
    )
    gram = gram_call(snapshots)
    image, keep, send = tangent_call(snapshots, halos, tangent, pattern, force, gram, place, parts)
    pieces = reduce_packed(keep, send)
    basis, coefficients, residual = final_call(
        pieces, step_index.reshape(1, snaps), place, snapshots, image, force, inverse_count
    )
    return basis, coefficients, residual.reshape(rows)


def solution(mesh):
    in_specs = (
        P(("rows", "zone"), None),
        P(("rows", "zone"), None),
        P(("rows", "zone"), None),
        P(("rows", "zone")),
        P(),
    )
    out_specs = (P(("rows", "zone"), None), P(), P(("rows", "zone")))
    return jax.shard_map(shards, mesh=mesh, in_specs=in_specs, out_specs=out_specs, check_vma=False)
```

```python
import functools

import jax
import jax.numpy as jnp
from jax import lax
from jax.experimental import pallas as pl
from jax.experimental.pallas import tpu as pltpu
from jax.sharding import PartitionSpec as P

HALO = 4
STEPS = 3
STEP_SIZE = 0.25
CHUNK = 1024
LIMIT = 24 * 1024 * 1024
PARTS = 8
F32 = jnp.float32
BF16 = jnp.bfloat16
HIGHEST = lax.Precision.HIGHEST


def split(value):
    high = value.astype(BF16)
    low = (value - high.astype(F32)).astype(BF16)
    return high, low


def contract_rows(left, right):
    return lax.dot_general(left, right, (((0,), (0,)), ((), ())), preferred_element_type=F32)


def matmul(left, right, precision=None):
    return lax.dot_general(
        left, right, (((1,), (0,)), ((), ())), preferred_element_type=F32, precision=precision
    )


def first_piece(at):
    return ((at >> 2) & 1) | (at & 2) | ((at & 1) << 2)


def second_piece(at):
    return ((at >> 2) & 1) | ((at & 1) << 1) | ((at & 2) << 1)


def second_place(piece):
    return ((piece & 1) << 2) | ((piece >> 1) & 1) | ((piece >> 1) & 2)


def force_product(panel, force):
    columns = force.T
    block = force.shape[1]
    total = jnp.zeros((1, panel.shape[1]), F32)
    for k in range(force.shape[0]):
        total += jnp.sum(panel[k * block : (k + 1) * block] * columns[:, k : k + 1], 0, keepdims=True)
    return total


def gram_kernel(snap_ref, force_ref, field_ref, turned_ref, gram_ref, load_ref):
    panel = snap_ref[...]
    snaps = panel.shape[1]
    high, low = split(panel)
    turned = high.T
    field_ref[:, :snaps] = high
    field_ref[:, snaps:] = low
    turned_ref[:snaps, :] = turned
    turned_ref[snaps:, :] = low.T
    gram = matmul(turned, jnp.concatenate([high, low], 1))
    load = force_product(panel, force_ref[...])

    @pl.when(pl.program_id(0) == 0)
    def _():
        gram_ref[...] = gram
        load_ref[...] = load

    @pl.when(pl.program_id(0) > 0)
    def _():
        gram_ref[...] += gram
        load_ref[...] += load


def gram_call(snapshots, force):
    rows, snaps = snapshots.shape
    block = force.shape[1]
    return pl.pallas_call(
        gram_kernel,
        out_shape=(
            jax.ShapeDtypeStruct((rows, 2 * snaps), BF16),
            jax.ShapeDtypeStruct((2 * snaps, rows), BF16),
            jax.ShapeDtypeStruct((snaps, 2 * snaps), F32),
            jax.ShapeDtypeStruct((1, snaps), F32),
        ),
        grid=(rows // CHUNK,),
        in_specs=[
            pl.BlockSpec((CHUNK, snaps), lambda i: (i, 0)),
            pl.BlockSpec((CHUNK // block, block), lambda i: (i, 0)),
        ],
        out_specs=[
            pl.BlockSpec((CHUNK, 2 * snaps), lambda i: (i, 0)),
            pl.BlockSpec((2 * snaps, CHUNK), lambda i: (0, i)),
            pl.BlockSpec((snaps, 2 * snaps), lambda i: (0, 0)),
            pl.BlockSpec((1, snaps), lambda i: (0, 0)),
        ],
        compiler_params=pltpu.CompilerParams(vmem_limit_bytes=LIMIT),
        cost_estimate=pl.CostEstimate(
            flops=4 * rows * snaps * snaps, bytes_accessed=12 * rows * snaps, transcendentals=0
        ),
        name="gram",
    )(snapshots, force)


def tangent_kernel(
    pattern_ref,
    place_ref,
    field,
    turned,
    prev_ref,
    next_ref,
    left_ref,
    right_ref,
    tangent_ref,
    force_ref,
    gram_ref,
    load_ref,
    image_ref,
    keep_first,
    send_first,
    keep_second,
    send_second,
    mixed,
    rest,
    load,
    packed,
    halo,
):
    rows, snaps = image_ref.shape
    block_count, coupled = pattern_ref.shape
    block = rows // block_count
    edge = HALO * block
    chunks = rows // CHUNK
    per_chunk = CHUNK // block
    for i, ref in enumerate((prev_ref, next_ref, left_ref, right_ref)):
        high, low = split(ref[...])
        at = pl.ds(i * edge, edge)
        halo[at, :snaps] = high
        halo[at, snaps:] = low
    mixed[...] = jnp.zeros_like(mixed)
    rest[...] = jnp.zeros_like(rest)
    load[...] = load_ref[...]

    @pl.loop(0, chunks)
    def _(step):
        start = pl.multiple_of(step * CHUNK, CHUNK)
        images = []
        for k in range(per_chunk):
            g = step * per_chunk + k
            picked = []
            for e in range(coupled):
                code = pattern_ref[g, e]
                source = lax.div(code, block_count)
                pick = lax.rem(code, block_count)
                here = source == 0
                tail = (source == 1) | (source == 3)
                beyond = (source - 1) * HALO + jnp.where(tail, pick - (block_count - HALO), pick)
                beyond = jnp.where(here, 0, beyond)
                inner = field[pl.ds(pl.multiple_of(pick * block, block), block), :]
                outer = halo[pl.ds(pl.multiple_of(beyond * block, block), block), :]
                picked.append(lax.select(here, inner, outer))
            own = pl.ds(pl.multiple_of(start + k * block, block), block)
            both = matmul(tangent_ref[own, :], jnp.concatenate(picked, 0))
            image = STEP_SIZE * (both[:, :snaps] + both[:, snaps:])
            image_ref[own, :] = image
            images.append(image)
        image = jnp.concatenate(images, 0)
        load[...] += force_product(image, force_ref[pl.ds(pl.multiple_of(step * per_chunk, per_chunk), per_chunk), :])
        high, low = split(image)
        high_turned = high.T
        panels = turned[:, pl.ds(start, CHUNK)]
        mixed[...] += matmul(jnp.concatenate([panels, high_turned], 0), high)
        rest[...] += matmul(jnp.concatenate([panels[:snaps], high_turned], 0), low)

    gram = gram_ref[:, :snaps] + gram_ref[:, snaps:] + gram_ref[:, snaps:].T
    cross = mixed[:snaps] + mixed[snaps : 2 * snaps] + rest[:snaps]
    square = mixed[2 * snaps :] + rest[snaps:] + rest[snaps:].T
    row = lax.broadcasted_iota(jnp.int32, (snaps, snaps), 0)
    column = lax.broadcasted_iota(jnp.int32, (snaps, snaps), 1)
    diagonal = jnp.sum(jnp.where(row == column, square, 0.0), 0, keepdims=True)
    packed[0] = jnp.where(row <= column, gram, square)
    packed[1] = cross
    extra_row = lax.broadcasted_iota(jnp.int32, (8, snaps), 0)
    extra = jnp.where(extra_row == 0, load[...], jnp.where(extra_row == 1, diagonal, 0.0))
    share = snaps // PARTS
    for at in range(PARTS):
        first = keep_first if at < PARTS // 2 else send_first
        second = keep_second if at < PARTS // 2 else send_second
        slot = at % (PARTS // 2)
        begin = pl.multiple_of((place_ref[0] ^ first_piece(at)) * share, 8)
        first[slot, :share, :] = packed[0, pl.ds(begin, share), :]
        first[slot, share:, :] = extra
        begin = pl.multiple_of((place_ref[0] ^ second_piece(at)) * share, 8)
        second[slot] = packed[1, pl.ds(begin, share), :]


def tangent_call(field, turned, halos, tangent, pattern, force, gram, load, place):
    rows = tangent.shape[0]
    snaps = gram.shape[0]
    share = snaps // PARTS
    vmem = pl.BlockSpec(memory_space=pltpu.VMEM)
    smem = pl.BlockSpec(memory_space=pltpu.SMEM)
    first = jax.ShapeDtypeStruct((PARTS // 2, share + 8, snaps), F32)
    second = jax.ShapeDtypeStruct((PARTS // 2, share, snaps), F32)
    return pl.pallas_call(
        tangent_kernel,
        out_shape=(
            jax.ShapeDtypeStruct((rows, snaps), F32),
            first,
            first,
            second,
            second,
        ),
        in_specs=[smem, smem] + [vmem] * 10,
        out_specs=[vmem] * 5,
        scratch_shapes=[
            pltpu.VMEM((3 * snaps, snaps), F32),
            pltpu.VMEM((2 * snaps, snaps), F32),
            pltpu.VMEM((1, snaps), F32),
            pltpu.VMEM((2, snaps, snaps), F32),
            pltpu.VMEM((4 * halos[0].shape[0], 2 * snaps), BF16),
        ],
        compiler_params=pltpu.CompilerParams(vmem_limit_bytes=LIMIT),
        name="tangent",
    )(pattern, place, field, turned, *halos, tangent, force, gram, load)


def inverse_factors(blocks):
    size = blocks[0].shape[0]
    groups = size // 8
    lane = lax.broadcasted_iota(jnp.int32, (8, size), 1)
    sub = lax.broadcasted_iota(jnp.int32, (8, size), 0)
    spread = lambda value: jnp.broadcast_to(value, (8, size))
    count = len(blocks)
    rows = [[value[8 * g : 8 * g + 8, :] for g in range(groups)] for value in blocks]
    done = [[] for _ in blocks]
    for g in range(groups):
        first = 8 * g
        inside = (lane >= first) & (lane < first + 8)
        unit = jnp.where(lane == sub + first, 1.0, 0.0)
        columns = [
            [spread(rows[m][g][:, first + j : first + j + 1]) for j in range(8)] for m in range(count)
        ]
        work = [jnp.where(inside, unit, rows[m][g]) for m in range(count)]
        kept = [jnp.zeros((8, size), F32) for _ in range(count)]
        for j in range(8):
            for m in range(count):
                pivot = spread(columns[m][j][j : j + 1, :])
                inverse = 1.0 / pivot
                root = lax.rsqrt(pivot)
                root = root * (1.5 - 0.5 * pivot * root * root)
                mine = sub == j
                for k in range(j + 1, 8):
                    scaled = spread(columns[m][k][j : j + 1, :]) * inverse
                    columns[m][k] = jnp.where(mine, scaled, columns[m][k] - columns[m][j] * scaled)
                row = spread(work[m][j : j + 1, :])
                kept[m] = jnp.where(mine, row * root, kept[m])
                scaled = row * inverse
                work[m] = jnp.where(mine, scaled, work[m] - columns[m][j] * scaled)
        for m in range(count):
            done[m].append(jnp.where(lane < first + 8, kept[m], 0.0))
            pivots = [spread(work[m][j : j + 1, :]) for j in range(8)]
            for i in range(g + 1, groups):
                old = rows[m][i]
                new = jnp.where(inside, 0.0, old)
                for j in range(8):
                    new = new - spread(old[:, first + j : first + j + 1]) * pivots[j]
                rows[m][i] = new
    return [jnp.concatenate(values, 0) for values in done]


def dot_last(left, right):
    return lax.dot_general(
        left, right, (((1,), (1,)), ((), ())), preferred_element_type=F32, precision=HIGHEST
    )


def reduced_system(inverse_count, place, first, second, index):
    snaps = first.shape[2]
    share = snaps // PARTS
    half = snaps // 2
    order = [first_piece(place ^ c) for c in range(PARTS)]
    packed = jnp.concatenate([first[at, :share, :] for at in order], 0) * inverse_count
    load = first[0, share : share + 1, :] * inverse_count
    diagonal = first[0, share + 1 : share + 2, :] * inverse_count
    order = [second_place(place ^ c) for c in range(PARTS)]
    cross = jnp.concatenate([second[at] for at in order], 0) * inverse_count
    row = lax.broadcasted_iota(jnp.int32, (snaps, snaps), 0)
    column = lax.broadcasted_iota(jnp.int32, (snaps, snaps), 1)
    turned = packed.T
    gram = jnp.where(row <= column, packed, turned)
    square = jnp.where(row > column, packed, jnp.where(row == column, diagonal, turned))
    project = gram + cross.T
    normal = project + cross + square

    pair = (gram, normal)
    upper = inverse_factors([value[:half, :half] for value in pair])
    below = [dot_last(value[half:, :half], inv) for value, inv in zip(pair, upper)]
    rest = [value[half:, half:] - dot_last(low, low) for value, low in zip(pair, below)]
    lower = inverse_factors(rest)
    inverses = []
    for top, low, bottom in zip(upper, below, lower):
        corner = -matmul(bottom, matmul(low, top, HIGHEST), HIGHEST)
        inverses.append(
            jnp.concatenate(
                [
                    jnp.concatenate([top, jnp.zeros((half, half), F32)], 1),
                    jnp.concatenate([corner, bottom], 1),
                ],
                0,
            )
        )
    gram_inverse, normal_inverse = inverses
    root = gram_inverse.T

    across = lambda matrix, vector: jnp.sum(matrix * vector, 1, keepdims=True)
    down = lambda matrix, vector: jnp.sum(matrix * vector, 0, keepdims=True)
    state = jnp.where(index == jnp.max(index), 1.0, 0.0)
    eye = jnp.where(row == column, 1.0, 0.0)
    history = []
    for _ in range(STEPS):
        old = state
        right = down(eye, across(project, state)) + STEP_SIZE * load
        state = down(normal_inverse, across(normal_inverse, right))
        history.append(down(root, across(gram, state)))
    return root, history, state - old, state


def final_kernel(inverse_count, place_ref, *refs):
    pieces = refs[:4]
    index_ref, force_ref, image, snap_any, basis_any, coeff_ref, residual_ref = refs[4:11]
    snap, first, second, root_ref, change_ref, state_ref, tile, sems = refs[11:]
    rows, snaps = snap.shape
    block = force_ref.shape[1]
    chunks = rows // CHUNK
    per_chunk = CHUNK // block
    copy = pltpu.make_async_copy(snap_any, snap, sems.at[chunks])
    copy.start()
    for i, pack in enumerate((first, second)):
        pack[: PARTS // 2] = pieces[2 * i][...]
        pack[PARTS // 2 :] = pieces[2 * i + 1][...]
    root, history, change, state = reduced_system(inverse_count, place_ref[0], first, second, index_ref[...])
    high, low = split(root)
    root_ref[:, :snaps] = high
    root_ref[:, snaps:] = low
    for n in range(STEPS):
        coeff_ref[n : n + 1, :] = history[n]
    change_ref[...] = change
    state_ref[...] = state
    copy.wait()
    tile[...] = jnp.zeros_like(tile)
    lane = lax.broadcasted_iota(jnp.int32, (block, block), 1)

    def out_copy(i):
        at = pl.ds(pl.multiple_of(i * CHUNK, CHUNK), CHUNK)
        return pltpu.make_async_copy(snap.at[at, :], basis_any.at[at, :], sems.at[i])

    @pl.loop(0, chunks)
    def _(i):
        at = pl.ds(pl.multiple_of(i * CHUNK, CHUNK), CHUNK)
        panel = snap[at, :]
        sums = jnp.sum(panel * change_ref[...] + image[at, :] * state_ref[...], 1, keepdims=True)
        gathered = tile[...]
        for k in range(per_chunk):
            gathered = jnp.where(lane == i * per_chunk + k, sums[k * block : (k + 1) * block], gathered)
        tile[...] = gathered
        panel_high, panel_low = split(panel)
        both = matmul(panel_high, root_ref[...])
        snap[at, :] = both[:, :snaps] + both[:, snaps:] + matmul(panel_low, root_ref[:, :snaps])
        out_copy(i).start()

    residual_ref[...] = tile[...].T[: rows // block] - STEP_SIZE * force_ref[...]

    @pl.loop(0, chunks)
    def _(i):
        out_copy(i).wait()


def final_call(pieces, step_index, place, snapshots, image, force, inverse_count):
    rows, snaps = snapshots.shape
    block = force.shape[1]
    share = snaps // PARTS
    vmem = pl.BlockSpec(memory_space=pltpu.VMEM)
    hbm = pl.BlockSpec(memory_space=pl.ANY)
    return pl.pallas_call(
        functools.partial(final_kernel, inverse_count),
        out_shape=(
            jax.ShapeDtypeStruct((rows, snaps), F32),
            jax.ShapeDtypeStruct((STEPS, snaps), F32),
            jax.ShapeDtypeStruct(force.shape, F32),
        ),
        in_specs=[pl.BlockSpec(memory_space=pltpu.SMEM)] + [vmem] * 7 + [hbm],
        out_specs=[hbm, vmem, vmem],
        scratch_shapes=[
            pltpu.VMEM((rows, snaps), F32),
            pltpu.VMEM((PARTS, share + 8, snaps), F32),
            pltpu.VMEM((PARTS, share, snaps), F32),
            pltpu.VMEM((snaps, 2 * snaps), BF16),
            pltpu.VMEM((1, snaps), F32),
            pltpu.VMEM((1, snaps), F32),
            pltpu.VMEM((block, block), F32),
            pltpu.SemaphoreType.DMA((rows // CHUNK + 1,)),
        ],
        compiler_params=pltpu.CompilerParams(vmem_limit_bytes=LIMIT),
        name="final",
    )(place, *pieces, step_index, force, image, snapshots)


def shifted(value, axis, steps):
    count = lax.axis_size(axis)
    pairs = [(source, (source + steps) % count) for source in range(count)]
    return lax.ppermute(value, axis, pairs)


def from_behind(shard, axis, by):
    devices = lax.axis_size(axis)
    pairs = [(i, i + by) for i in range(devices) if 0 <= i + by < devices]
    return lax.ppermute(shard, axis, pairs)


def partner(value, axis, bit):
    count = lax.axis_size(axis)
    return lax.ppermute(value, axis, [(i, i ^ bit) for i in range(count)])


def reduce_packed(keep_first, send_first, keep_second, send_second):
    core, x, y = ("zone", 1), ("zone", 2), ("rows", 1)
    first = keep_first + partner(send_first, *core)
    second = keep_second + partner(send_second, *core)
    for way_first, way_second in ((x, y), (y, x)):
        half = first.shape[0] // 2
        first = first[:half] + partner(first[half:], *way_first)
        second = second[:half] + partner(second[half:], *way_second)
    edge = first.shape[1]
    value = jnp.concatenate([first, second], 1)
    for axis, least in (("rows", 2), ("zone", 4)):
        bit = least
        while bit < lax.axis_size(axis):
            value = value + partner(value, axis, bit)
            bit *= 2
    first, second = value[:, :edge], value[:, edge:]
    for way_first, way_second in ((y, x), (x, y)):
        first = jnp.concatenate([first, partner(first, *way_first)], 0)
        second = jnp.concatenate([second, partner(second, *way_second)], 0)
    return first, partner(first, *core), second, partner(second, *core)


def shards(snapshots, tangent, pattern, forcing, step_index):
    rows, snaps = snapshots.shape
    blocks = pattern.shape[0]
    block = rows // blocks
    edge = HALO * block
    inverse_count = 1.0 / (rows * lax.axis_size("rows") * lax.axis_size("zone"))
    place = (lax.axis_index("zone") & 3) | ((lax.axis_index("rows") & 1) << 2)
    place = jnp.reshape(place, (1,)).astype(jnp.int32)
    force = forcing.reshape(blocks, block)
    head, tail = snapshots[:edge], snapshots[rows - edge :]
    rows_prev = shifted(tail, "rows", 1)
    rows_next = shifted(head, "rows", -1)
    field, turned, gram, load = gram_call(snapshots, force)
    head, tail, load = lax.optimization_barrier((head, tail, load))
    halos = (rows_prev, rows_next, from_behind(tail, "zone", 1), from_behind(head, "zone", -1))
    image, *packed = tangent_call(field, turned, halos, tangent, pattern, force, gram, load, place)
    pieces = reduce_packed(*packed)
    basis, coefficients, residual = final_call(
        pieces, step_index.reshape(1, snaps), place, snapshots, image, force, inverse_count
    )
    return basis, coefficients, residual.reshape(rows)


def solution(mesh):
    in_specs = (
        P(("rows", "zone"), None),
        P(("rows", "zone"), None),
        P(("rows", "zone"), None),
        P(("rows", "zone")),
        P(),
    )
    out_specs = (P(("rows", "zone"), None), P(), P(("rows", "zone")))
    return jax.shard_map(shards, mesh=mesh, in_specs=in_specs, out_specs=out_specs, check_vma=False)
```

```python
import functools

import jax
import jax.numpy as jnp
from jax import lax
from jax.experimental import pallas as pl
from jax.experimental.pallas import tpu as pltpu
from jax.sharding import PartitionSpec as P

HALO = 4
STEPS = 3
STEP_SIZE = 0.25
CHUNK = 1024
LIMIT = 56 * 1024 * 1024
F32 = jnp.float32
BF16 = jnp.bfloat16
HIGHEST = lax.Precision.HIGHEST


def split(value):
    high = value.astype(BF16)
    low = (value - high.astype(F32)).astype(BF16)
    return high, low


def contract_rows(left, right):
    return lax.dot_general(left, right, (((0,), (0,)), ((), ())), preferred_element_type=F32)


def matmul(left, right, precision=None):
    return lax.dot_general(
        left, right, (((1,), (0,)), ((), ())), preferred_element_type=F32, precision=precision
    )


def halves(value):
    half = value.shape[1] // 2
    return jnp.concatenate([value[:, :half], value[:, half:]], 0)


def whole(value):
    half = value.shape[0] // 2
    return jnp.concatenate([value[:half], value[half:]], 1)


def force_product(panel, force):
    columns = force.T
    block = force.shape[1]
    total = jnp.zeros((1, panel.shape[1]), F32)
    for k in range(force.shape[0]):
        total += jnp.sum(panel[k * block : (k + 1) * block] * columns[:, k : k + 1], 0, keepdims=True)
    return total


def gram_kernel(snap_ref, force_ref, field_ref, turned_ref, gram_ref, load_ref):
    panel = snap_ref[...]
    snaps = panel.shape[1]
    high, low = split(panel)
    turned = high.T
    field_ref[:, :snaps] = high
    field_ref[:, snaps:] = low
    turned_ref[:snaps, :] = turned
    turned_ref[snaps:, :] = low.T
    gram = matmul(turned, jnp.concatenate([high, low], 1))
    load = force_product(panel, force_ref[...])

    @pl.when(pl.program_id(0) == 0)
    def _():
        gram_ref[...] = gram
        load_ref[...] = load

    @pl.when(pl.program_id(0) > 0)
    def _():
        gram_ref[...] += gram
        load_ref[...] += load


def gram_call(snapshots, force):
    rows, snaps = snapshots.shape
    block = force.shape[1]
    return pl.pallas_call(
        gram_kernel,
        out_shape=(
            jax.ShapeDtypeStruct((rows, 2 * snaps), BF16),
            jax.ShapeDtypeStruct((2 * snaps, rows), BF16),
            jax.ShapeDtypeStruct((snaps, 2 * snaps), F32),
            jax.ShapeDtypeStruct((1, snaps), F32),
        ),
        grid=(rows // CHUNK,),
        in_specs=[
            pl.BlockSpec((CHUNK, snaps), lambda i: (i, 0)),
            pl.BlockSpec((CHUNK // block, block), lambda i: (i, 0)),
        ],
        out_specs=[
            pl.BlockSpec((CHUNK, 2 * snaps), lambda i: (i, 0)),
            pl.BlockSpec((2 * snaps, CHUNK), lambda i: (0, i)),
            pl.BlockSpec((snaps, 2 * snaps), lambda i: (0, 0)),
            pl.BlockSpec((1, snaps), lambda i: (0, 0)),
        ],
        compiler_params=pltpu.CompilerParams(vmem_limit_bytes=LIMIT),
        cost_estimate=pl.CostEstimate(
            flops=4 * rows * snaps * snaps, bytes_accessed=12 * rows * snaps, transcendentals=0
        ),
        name="gram",
    )(snapshots, force)


def tangent_kernel(
    pattern_ref,
    field_any,
    prev_any,
    next_any,
    left_any,
    right_any,
    turned_ref,
    tangent_ref,
    force_ref,
    gram_ref,
    load_ref,
    image_ref,
    pack_ref,
    field,
    edges,
    mixed,
    rest,
    load,
    sems,
):
    step = pl.program_id(0)
    chunks = pl.num_programs(0) - 1
    rows = chunks * CHUNK
    snaps = image_ref.shape[1]
    block_count, coupled = pattern_ref.shape
    block = rows // block_count
    edge = HALO * block
    per_chunk = CHUNK // block

    @pl.when(step == 0)
    def _():
        copies = [pltpu.make_async_copy(field_any, field.at[pl.ds(0, rows), :], sems.at[4])]
        for i, ref in enumerate((prev_any, next_any, left_any, right_any)):
            copies.append(pltpu.make_async_copy(ref, edges.at[pl.ds(i * edge, edge), :], sems.at[i]))
        for copy in reversed(copies):
            copy.start()
        for i in range(4):
            copies[1 + i].wait()
            high, low = split(edges[i * edge : (i + 1) * edge, :])
            at = pl.ds(rows + i * edge, edge)
            field[at, :snaps] = high
            field[at, snaps:] = low
        mixed[...] = jnp.zeros_like(mixed)
        rest[...] = jnp.zeros_like(rest)
        load[...] = load_ref[...]
        copies[0].wait()

    @pl.when(step < chunks)
    def _():
        images = []
        for k in range(per_chunk):
            g = step * per_chunk + k
            picked = []
            for e in range(coupled):
                code = pattern_ref[g, e]
                source = lax.div(code, block_count)
                pick = lax.rem(code, block_count)
                tail = (source == 1) | (source == 3)
                base = jnp.where(source == 0, 0, block_count + (source - 1) * HALO)
                place = base + jnp.where(tail, pick - (block_count - HALO), pick)
                picked.append(field[pl.ds(pl.multiple_of(place * block, block), block), :])
            own = slice(k * block, (k + 1) * block)
            both = matmul(tangent_ref[own, :], jnp.concatenate(picked, 0))
            image = STEP_SIZE * (both[:, :snaps] + both[:, snaps:])
            image_ref[own, :] = image
            images.append(image)
        image = jnp.concatenate(images, 0)
        load[...] += force_product(image, force_ref[...])
        high, low = split(image)
        high_turned = high.T
        panels = turned_ref[...]
        mixed[...] += matmul(jnp.concatenate([panels, high_turned], 0), high)
        rest[...] += matmul(jnp.concatenate([panels[:snaps], high_turned], 0), low)

    @pl.when(step == chunks)
    def _():
        gram = gram_ref[:, :snaps] + gram_ref[:, snaps:] + gram_ref[:, snaps:].T
        cross = mixed[:snaps] + mixed[snaps : 2 * snaps] + rest[:snaps]
        square = mixed[2 * snaps :] + rest[snaps:] + rest[snaps:].T
        row = lax.broadcasted_iota(jnp.int32, (snaps, snaps), 0)
        column = lax.broadcasted_iota(jnp.int32, (snaps, snaps), 1)
        diagonal = jnp.sum(jnp.where(row == column, square, 0.0), 0, keepdims=True)
        first = halves(jnp.where(row <= column, gram, square))
        second = halves(cross)
        vectors = jnp.concatenate([halves(load[...]), halves(diagonal), jnp.zeros((4, snaps // 2), F32)], 0)
        share = 2 * snaps // pack_ref.shape[0]
        for k in range(pack_ref.shape[0]):
            own = slice(k * share, (k + 1) * share)
            pack_ref[k, :share, :] = first[own]
            pack_ref[k, share : 2 * share, :] = second[own]
            pack_ref[k, 2 * share :, :] = vectors


def tangent_call(field, turned, halos, tangent, pattern, force, gram, load, devices):
    rows = tangent.shape[0]
    snaps = gram.shape[0]
    block = force.shape[1]
    chunks = rows // CHUNK
    share = 2 * snaps // devices
    hbm = pl.BlockSpec(memory_space=pl.ANY)
    last = lambda i: jnp.minimum(i, chunks - 1)
    piece = (devices, 2 * share + 8, snaps // 2)
    return pl.pallas_call(
        tangent_kernel,
        out_shape=(jax.ShapeDtypeStruct((rows, snaps), F32), jax.ShapeDtypeStruct(piece, F32)),
        grid_spec=pltpu.PrefetchScalarGridSpec(
            num_scalar_prefetch=1,
            grid=(chunks + 1,),
            in_specs=[
                hbm,
                hbm,
                hbm,
                hbm,
                hbm,
                pl.BlockSpec((2 * snaps, CHUNK), lambda i, _: (0, last(i))),
                pl.BlockSpec((CHUNK, tangent.shape[1]), lambda i, _: (last(i), 0)),
                pl.BlockSpec((CHUNK // block, block), lambda i, _: (last(i), 0)),
                pl.BlockSpec((snaps, 2 * snaps), lambda i, _: (0, 0)),
                pl.BlockSpec((1, snaps), lambda i, _: (0, 0)),
            ],
            out_specs=[
                pl.BlockSpec((CHUNK, snaps), lambda i, _: (last(i), 0)),
                pl.BlockSpec(piece, lambda i, _: (0, 0, 0)),
            ],
            scratch_shapes=[
                pltpu.VMEM((rows + 4 * HALO * block, 2 * snaps), BF16),
                pltpu.VMEM((4 * HALO * block, snaps), F32),
                pltpu.VMEM((3 * snaps, snaps), F32),
                pltpu.VMEM((2 * snaps, snaps), F32),
                pltpu.VMEM((1, snaps), F32),
                pltpu.SemaphoreType.DMA((5,)),
            ],
        ),
        compiler_params=pltpu.CompilerParams(vmem_limit_bytes=LIMIT),
        name="tangent",
    )(pattern, field, *halos, turned, tangent, force, gram, load)


def inverse_factors(blocks):
    size = blocks[0].shape[0]
    groups = size // 8
    lane = lax.broadcasted_iota(jnp.int32, (8, size), 1)
    sub = lax.broadcasted_iota(jnp.int32, (8, size), 0)
    spread = lambda value: jnp.broadcast_to(value, (8, size))
    count = len(blocks)
    rows = [[value[8 * g : 8 * g + 8, :] for g in range(groups)] for value in blocks]
    done = [[] for _ in blocks]
    for g in range(groups):
        first = 8 * g
        inside = (lane >= first) & (lane < first + 8)
        unit = jnp.where(lane == sub + first, 1.0, 0.0)
        columns = [
            [spread(rows[m][g][:, first + j : first + j + 1]) for j in range(8)] for m in range(count)
        ]
        work = [jnp.where(inside, unit, rows[m][g]) for m in range(count)]
        kept = [jnp.zeros((8, size), F32) for _ in range(count)]
        for j in range(8):
            for m in range(count):
                pivot = spread(columns[m][j][j : j + 1, :])
                inverse = 1.0 / pivot
                root = lax.rsqrt(pivot)
                root = root * (1.5 - 0.5 * pivot * root * root)
                mine = sub == j
                for k in range(j + 1, 8):
                    scaled = spread(columns[m][k][j : j + 1, :]) * inverse
                    columns[m][k] = jnp.where(mine, scaled, columns[m][k] - columns[m][j] * scaled)
                row = spread(work[m][j : j + 1, :])
                kept[m] = jnp.where(mine, row * root, kept[m])
                scaled = row * inverse
                work[m] = jnp.where(mine, scaled, work[m] - columns[m][j] * scaled)
        for m in range(count):
            done[m].append(jnp.where(lane < first + 8, kept[m], 0.0))
            pivots = [spread(work[m][j : j + 1, :]) for j in range(8)]
            for i in range(g + 1, groups):
                old = rows[m][i]
                new = jnp.where(inside, 0.0, old)
                for j in range(8):
                    new = new - spread(old[:, first + j : first + j + 1]) * pivots[j]
                rows[m][i] = new
    return [jnp.concatenate(values, 0) for values in done]


def dot_last(left, right):
    return lax.dot_general(
        left, right, (((1,), (1,)), ((), ())), preferred_element_type=F32, precision=HIGHEST
    )


def reduced_system(inverse_count, pack, index):
    pieces, depth, half = pack.shape
    snaps = 2 * half
    share = 2 * snaps // pieces
    packed = whole(jnp.concatenate([pack[k, :share, :] for k in range(pieces)], 0)) * inverse_count
    cross = whole(jnp.concatenate([pack[k, share : 2 * share, :] for k in range(pieces)], 0)) * inverse_count
    vectors = pack[0, 2 * share :, :] * inverse_count
    load = whole(vectors[0:2])
    diagonal = whole(vectors[2:4])
    row = lax.broadcasted_iota(jnp.int32, (snaps, snaps), 0)
    column = lax.broadcasted_iota(jnp.int32, (snaps, snaps), 1)
    turned = packed.T
    gram = jnp.where(row <= column, packed, turned)
    square = jnp.where(row > column, packed, jnp.where(row == column, diagonal, turned))
    project = gram + cross.T
    normal = project + cross + square

    pair = (gram, normal)
    upper = inverse_factors([value[:half, :half] for value in pair])
    below = [dot_last(value[half:, :half], inv) for value, inv in zip(pair, upper)]
    rest = [value[half:, half:] - dot_last(low, low) for value, low in zip(pair, below)]
    lower = inverse_factors(rest)
    inverses = []
    for top, low, bottom in zip(upper, below, lower):
        corner = -matmul(bottom, matmul(low, top, HIGHEST), HIGHEST)
        inverses.append(
            jnp.concatenate(
                [
                    jnp.concatenate([top, jnp.zeros((half, half), F32)], 1),
                    jnp.concatenate([corner, bottom], 1),
                ],
                0,
            )
        )
    gram_inverse, normal_inverse = inverses
    root = gram_inverse.T

    across = lambda matrix, vector: jnp.sum(matrix * vector, 1, keepdims=True)
    down = lambda matrix, vector: jnp.sum(matrix * vector, 0, keepdims=True)
    state = jnp.where(index == jnp.max(index), 1.0, 0.0)
    eye = jnp.where(row == column, 1.0, 0.0)
    history = []
    for _ in range(STEPS):
        old = state
        right = down(eye, across(project, state)) + STEP_SIZE * load
        state = down(normal_inverse, across(normal_inverse, right))
        history.append(down(root, across(gram, state)))
    return root, history, state - old, state


def final_kernel(
    inverse_count,
    pack_ref,
    index_ref,
    force_ref,
    snap_any,
    image_any,
    basis_any,
    coeff_ref,
    residual_ref,
    snap,
    image,
    root_ref,
    change_ref,
    state_ref,
    tile,
    sems,
):
    rows, snaps = snap.shape
    block = force_ref.shape[1]
    chunks = rows // CHUNK
    per_chunk = CHUNK // block
    copies = [
        pltpu.make_async_copy(snap_any, snap, sems.at[chunks]),
        pltpu.make_async_copy(image_any, image, sems.at[chunks + 1]),
    ]
    for copy in copies:
        copy.start()
    root, history, change, state = reduced_system(inverse_count, pack_ref, index_ref[...])
    high, low = split(root)
    root_ref[:, :snaps] = high
    root_ref[:, snaps:] = low
    for n in range(STEPS):
        coeff_ref[n : n + 1, :] = history[n]
    change_ref[...] = change
    state_ref[...] = state
    for copy in copies:
        copy.wait()
    tile[...] = jnp.zeros_like(tile)
    lane = lax.broadcasted_iota(jnp.int32, (block, block), 1)

    def out_copy(i):
        at = pl.ds(pl.multiple_of(i * CHUNK, CHUNK), CHUNK)
        return pltpu.make_async_copy(snap.at[at, :], basis_any.at[at, :], sems.at[i])

    @pl.loop(0, chunks)
    def _(i):
        at = pl.ds(pl.multiple_of(i * CHUNK, CHUNK), CHUNK)
        panel = snap[at, :]
        sums = jnp.sum(panel * change_ref[...] + image[at, :] * state_ref[...], 1, keepdims=True)
        gathered = tile[...]
        for k in range(per_chunk):
            gathered = jnp.where(lane == i * per_chunk + k, sums[k * block : (k + 1) * block], gathered)
        tile[...] = gathered
        panel_high, panel_low = split(panel)
        both = matmul(panel_high, root_ref[...])
        snap[at, :] = both[:, :snaps] + both[:, snaps:] + matmul(panel_low, root_ref[:, :snaps])
        out_copy(i).start()

    residual_ref[...] = tile[...].T[: rows // block] - STEP_SIZE * force_ref[...]

    @pl.loop(0, chunks)
    def _(i):
        out_copy(i).wait()


def final_call(pack, step_index, snapshots, image, force, inverse_count):
    rows, snaps = snapshots.shape
    block = force.shape[1]
    vmem = pl.BlockSpec(memory_space=pltpu.VMEM)
    hbm = pl.BlockSpec(memory_space=pl.ANY)
    return pl.pallas_call(
        functools.partial(final_kernel, inverse_count),
        out_shape=(
            jax.ShapeDtypeStruct((rows, snaps), F32),
            jax.ShapeDtypeStruct((STEPS, snaps), F32),
            jax.ShapeDtypeStruct(force.shape, F32),
        ),
        in_specs=[vmem, vmem, vmem, hbm, hbm],
        out_specs=[hbm, vmem, vmem],
        scratch_shapes=[
            pltpu.VMEM((rows, snaps), F32),
            pltpu.VMEM((rows, snaps), F32),
            pltpu.VMEM((snaps, 2 * snaps), BF16),
            pltpu.VMEM((1, snaps), F32),
            pltpu.VMEM((1, snaps), F32),
            pltpu.VMEM((block, block), F32),
            pltpu.SemaphoreType.DMA((rows // CHUNK + 2,)),
        ],
        compiler_params=pltpu.CompilerParams(vmem_limit_bytes=LIMIT),
        name="final",
    )(pack, step_index, force, snapshots, image)


def shifted(value, axis, steps):
    count = lax.axis_size(axis)
    pairs = [(source, (source + steps) % count) for source in range(count)]
    return lax.ppermute(value, axis, pairs)


def from_behind(shard, axis, by):
    devices = lax.axis_size(axis)
    pairs = [(i, i + by) for i in range(devices) if 0 <= i + by < devices]
    return lax.ppermute(shard, axis, pairs)


def exchange(value, axis):
    return lax.all_to_all(value, axis, 0, 0, tiled=True)


def reduce_pieces(pack):
    zones, lines = lax.axis_size("zone"), lax.axis_size("rows")
    value = pack.reshape((zones, lines) + pack.shape[1:])
    value = exchange(value, "zone").sum(0)
    value = exchange(value, "rows").sum(0)
    value = exchange(jnp.broadcast_to(value, (lines,) + value.shape), "rows")
    value = exchange(jnp.broadcast_to(value, (zones,) + value.shape), "zone")
    return value.reshape(pack.shape)


def shards(snapshots, tangent, pattern, forcing, step_index):
    rows, snaps = snapshots.shape
    blocks = pattern.shape[0]
    block = rows // blocks
    edge = HALO * block
    devices = lax.axis_size("rows") * lax.axis_size("zone")
    inverse_count = 1.0 / (rows * devices)
    force = forcing.reshape(blocks, block)
    head, tail = snapshots[:edge], snapshots[rows - edge :]
    rows_prev = shifted(tail, "rows", 1)
    rows_next = shifted(head, "rows", -1)
    field, turned, gram, load = gram_call(snapshots, force)
    head, tail, load = lax.optimization_barrier((head, tail, load))
    halos = (rows_prev, rows_next, from_behind(tail, "zone", 1), from_behind(head, "zone", -1))
    image, pack = tangent_call(field, turned, halos, tangent, pattern, force, gram, load, devices)
    basis, coefficients, residual = final_call(
        reduce_pieces(pack), step_index.reshape(1, snaps), snapshots, image, force, inverse_count
    )
    return basis, coefficients, residual.reshape(rows)


def solution(mesh):
    in_specs = (
        P(("rows", "zone"), None),
        P(("rows", "zone"), None),
        P(("rows", "zone"), None),
        P(("rows", "zone")),
        P(),
    )
    out_specs = (P(("rows", "zone"), None), P(), P(("rows", "zone")))
    return jax.shard_map(shards, mesh=mesh, in_specs=in_specs, out_specs=out_specs, check_vma=False)
```

```python
import functools

import jax
import jax.numpy as jnp
from jax import lax
from jax.experimental import pallas as pl
from jax.experimental.pallas import tpu as pltpu
from jax.sharding import PartitionSpec as P

HALO = 4
STEPS = 3
STEP_SIZE = 0.25
CHUNK = 1024
LIMIT = 56 * 1024 * 1024
PARTS = 8
F32 = jnp.float32
BF16 = jnp.bfloat16
HIGHEST = lax.Precision.HIGHEST


def split(value):
    high = value.astype(BF16)
    low = (value - high.astype(F32)).astype(BF16)
    return high, low


def contract_rows(left, right):
    return lax.dot_general(left, right, (((0,), (0,)), ((), ())), preferred_element_type=F32)


def matmul(left, right, precision=None):
    return lax.dot_general(
        left, right, (((1,), (0,)), ((), ())), preferred_element_type=F32, precision=precision
    )


def first_piece(at):
    return ((at >> 2) & 1) | (at & 2) | ((at & 1) << 2)


def second_piece(at):
    return ((at >> 2) & 1) | ((at & 1) << 1) | ((at & 2) << 1)


def second_place(piece):
    return ((piece & 1) << 2) | ((piece >> 1) & 1) | ((piece >> 1) & 2)


def force_product(panel, force):
    columns = force.T
    block = force.shape[1]
    total = jnp.zeros((1, panel.shape[1]), F32)
    for k in range(force.shape[0]):
        total += jnp.sum(panel[k * block : (k + 1) * block] * columns[:, k : k + 1], 0, keepdims=True)
    return total


def gram_kernel(snap_ref, force_ref, field_ref, turned_ref, gram_ref, load_ref):
    panel = snap_ref[...]
    snaps = panel.shape[1]
    high, low = split(panel)
    turned = high.T
    field_ref[:, :snaps] = high
    field_ref[:, snaps:] = low
    turned_ref[:snaps, :] = turned
    turned_ref[snaps:, :] = low.T
    gram = matmul(turned, jnp.concatenate([high, low], 1))
    load = force_product(panel, force_ref[...])

    @pl.when(pl.program_id(0) == 0)
    def _():
        gram_ref[...] = gram
        load_ref[...] = load

    @pl.when(pl.program_id(0) > 0)
    def _():
        gram_ref[...] += gram
        load_ref[...] += load


def gram_call(snapshots, force):
    rows, snaps = snapshots.shape
    block = force.shape[1]
    return pl.pallas_call(
        gram_kernel,
        out_shape=(
            jax.ShapeDtypeStruct((rows, 2 * snaps), BF16),
            jax.ShapeDtypeStruct((2 * snaps, rows), BF16),
            jax.ShapeDtypeStruct((snaps, 2 * snaps), F32),
            jax.ShapeDtypeStruct((1, snaps), F32),
        ),
        grid=(rows // CHUNK,),
        in_specs=[
            pl.BlockSpec((CHUNK, snaps), lambda i: (i, 0)),
            pl.BlockSpec((CHUNK // block, block), lambda i: (i, 0)),
        ],
        out_specs=[
            pl.BlockSpec((CHUNK, 2 * snaps), lambda i: (i, 0)),
            pl.BlockSpec((2 * snaps, CHUNK), lambda i: (0, i)),
            pl.BlockSpec((snaps, 2 * snaps), lambda i: (0, 0)),
            pl.BlockSpec((1, snaps), lambda i: (0, 0)),
        ],
        compiler_params=pltpu.CompilerParams(vmem_limit_bytes=LIMIT),
        cost_estimate=pl.CostEstimate(
            flops=4 * rows * snaps * snaps, bytes_accessed=12 * rows * snaps, transcendentals=0
        ),
        name="gram",
    )(snapshots, force)


def tangent_kernel(
    pattern_ref,
    place_ref,
    field_any,
    left_any,
    right_any,
    prev_any,
    next_any,
    turned_any,
    tangent_any,
    force_ref,
    gram_ref,
    load_ref,
    image_any,
    keep_first,
    send_first,
    keep_second,
    send_second,
    field,
    edges,
    turned,
    tangent,
    image,
    mixed,
    rest,
    load,
    packed,
    field_sems,
    edge_sems,
    turned_sems,
    tangent_sems,
    image_sems,
):
    rows, snaps = image.shape
    block_count, coupled = pattern_ref.shape
    block = rows // block_count
    edge = HALO * block
    chunks = rows // CHUNK
    per_chunk = CHUNK // block

    def chunk(i):
        return pl.ds(pl.multiple_of(i * CHUNK, CHUNK), CHUNK)

    def field_copy(i):
        return pltpu.make_async_copy(field_any.at[chunk(i), :], field.at[chunk(i), :], field_sems.at[i])

    def turned_copy(i):
        return pltpu.make_async_copy(turned_any.at[:, chunk(i)], turned.at[i], turned_sems.at[i])

    def tangent_copy(i):
        return pltpu.make_async_copy(tangent_any.at[chunk(i), :], tangent.at[chunk(i), :], tangent_sems.at[i])

    def image_copy(i):
        return pltpu.make_async_copy(image.at[chunk(i), :], image_any.at[chunk(i), :], image_sems.at[i])

    edge_copies = []
    for i, ref in enumerate((left_any, right_any, prev_any, next_any)):
        edge_copies.append(pltpu.make_async_copy(ref, edges.at[pl.ds(i * edge, edge), :], edge_sems.at[i]))
        edge_copies[-1].start()
    for i in range(chunks):
        field_copy(i).start()
    for i in range(chunks):
        tangent_copy(i).start()
        turned_copy(i).start()
    for i in range(4):
        edge_copies[i].wait()
        high, low = split(edges[i * edge : (i + 1) * edge, :])
        at = pl.ds(rows + i * edge, edge)
        field[at, :snaps] = high
        field[at, snaps:] = low
    mixed[...] = jnp.zeros_like(mixed)
    rest[...] = jnp.zeros_like(rest)
    load[...] = load_ref[...]
    for i in range(chunks):
        field_copy(i).wait()

    @pl.loop(0, chunks)
    def _(step):
        start = pl.multiple_of(step * CHUNK, CHUNK)
        tangent_copy(step).wait()
        turned_copy(step).wait()
        images = []
        for k in range(per_chunk):
            g = step * per_chunk + k
            picked = []
            for e in range(coupled):
                code = pattern_ref[g, e]
                source = lax.div(code, block_count)
                pick = lax.rem(code, block_count)
                tail = (source == 1) | (source == 3)
                base = jnp.where(source == 0, 0, block_count + ((source + 1) & 3) * HALO)
                at = base + jnp.where(tail, pick - (block_count - HALO), pick)
                picked.append(field[pl.ds(pl.multiple_of(at * block, block), block), :])
            own = pl.ds(pl.multiple_of(start + k * block, block), block)
            both = matmul(tangent[own, :], jnp.concatenate(picked, 0))
            part = STEP_SIZE * (both[:, :snaps] + both[:, snaps:])
            image[own, :] = part
            images.append(part)
        image_copy(step).start()
        panel = jnp.concatenate(images, 0)
        line = pl.ds(pl.multiple_of(step * per_chunk, per_chunk), per_chunk)
        load[...] += force_product(panel, force_ref[line, :])
        high, low = split(panel)
        high_turned = high.T
        panels = turned[step]
        mixed[...] += matmul(jnp.concatenate([panels, high_turned], 0), high)
        rest[...] += matmul(jnp.concatenate([panels[:snaps], high_turned], 0), low)

    gram = gram_ref[:, :snaps] + gram_ref[:, snaps:] + gram_ref[:, snaps:].T
    cross = mixed[:snaps] + mixed[snaps : 2 * snaps] + rest[:snaps]
    square = mixed[2 * snaps :] + rest[snaps:] + rest[snaps:].T
    row = lax.broadcasted_iota(jnp.int32, (snaps, snaps), 0)
    column = lax.broadcasted_iota(jnp.int32, (snaps, snaps), 1)
    diagonal = jnp.sum(jnp.where(row == column, square, 0.0), 0, keepdims=True)
    packed[0] = jnp.where(row <= column, gram, square)
    packed[1] = cross
    extra_row = lax.broadcasted_iota(jnp.int32, (8, snaps), 0)
    extra = jnp.where(extra_row == 0, load[...], jnp.where(extra_row == 1, diagonal, 0.0))
    share = snaps // PARTS
    for at in range(PARTS):
        first = keep_first if at < PARTS // 2 else send_first
        second = keep_second if at < PARTS // 2 else send_second
        slot = at % (PARTS // 2)
        begin = pl.multiple_of((place_ref[0] ^ first_piece(at)) * share, 8)
        first[slot, :share, :] = packed[0, pl.ds(begin, share), :]
        first[slot, share:, :] = extra
        begin = pl.multiple_of((place_ref[0] ^ second_piece(at)) * share, 8)
        second[slot] = packed[1, pl.ds(begin, share), :]

    @pl.loop(0, chunks)
    def _(step):
        image_copy(step).wait()


def tangent_call(field, turned, halos, tangent, pattern, force, gram, load, place):
    rows, width = tangent.shape
    snaps = gram.shape[0]
    share = snaps // PARTS
    chunks = rows // CHUNK
    edge = halos[0].shape[0]
    vmem = pl.BlockSpec(memory_space=pltpu.VMEM)
    smem = pl.BlockSpec(memory_space=pltpu.SMEM)
    hbm = pl.BlockSpec(memory_space=pl.ANY)
    first = jax.ShapeDtypeStruct((PARTS // 2, share + 8, snaps), F32)
    second = jax.ShapeDtypeStruct((PARTS // 2, share, snaps), F32)
    return pl.pallas_call(
        tangent_kernel,
        out_shape=(jax.ShapeDtypeStruct((rows, snaps), F32), first, first, second, second),
        in_specs=[smem, smem] + [hbm] * 7 + [vmem] * 3,
        out_specs=[hbm] + [vmem] * 4,
        scratch_shapes=[
            pltpu.VMEM((rows + 4 * edge, 2 * snaps), BF16),
            pltpu.VMEM((4 * edge, snaps), F32),
            pltpu.VMEM((chunks, 2 * snaps, CHUNK), BF16),
            pltpu.VMEM((rows, width), BF16),
            pltpu.VMEM((rows, snaps), F32),
            pltpu.VMEM((3 * snaps, snaps), F32),
            pltpu.VMEM((2 * snaps, snaps), F32),
            pltpu.VMEM((1, snaps), F32),
            pltpu.VMEM((2, snaps, snaps), F32),
            pltpu.SemaphoreType.DMA((chunks,)),
            pltpu.SemaphoreType.DMA((4,)),
            pltpu.SemaphoreType.DMA((chunks,)),
            pltpu.SemaphoreType.DMA((chunks,)),
            pltpu.SemaphoreType.DMA((chunks,)),
        ],
        compiler_params=pltpu.CompilerParams(vmem_limit_bytes=LIMIT),
        name="tangent",
    )(pattern, place, field, *halos, turned, tangent, force, gram, load)


def inverse_factors(blocks):
    size = blocks[0].shape[0]
    groups = size // 8
    lane = lax.broadcasted_iota(jnp.int32, (8, size), 1)
    sub = lax.broadcasted_iota(jnp.int32, (8, size), 0)
    spread = lambda value: jnp.broadcast_to(value, (8, size))
    count = len(blocks)
    rows = [[value[8 * g : 8 * g + 8, :] for g in range(groups)] for value in blocks]
    done = [[] for _ in blocks]
    for g in range(groups):
        first = 8 * g
        inside = (lane >= first) & (lane < first + 8)
        unit = jnp.where(lane == sub + first, 1.0, 0.0)
        columns = [
            [spread(rows[m][g][:, first + j : first + j + 1]) for j in range(8)] for m in range(count)
        ]
        work = [jnp.where(inside, unit, rows[m][g]) for m in range(count)]
        kept = [jnp.zeros((8, size), F32) for _ in range(count)]
        for j in range(8):
            for m in range(count):
                pivot = spread(columns[m][j][j : j + 1, :])
                inverse = 1.0 / pivot
                root = lax.rsqrt(pivot)
                root = root * (1.5 - 0.5 * pivot * root * root)
                mine = sub == j
                for k in range(j + 1, 8):
                    scaled = spread(columns[m][k][j : j + 1, :]) * inverse
                    columns[m][k] = jnp.where(mine, scaled, columns[m][k] - columns[m][j] * scaled)
                row = spread(work[m][j : j + 1, :])
                kept[m] = jnp.where(mine, row * root, kept[m])
                scaled = row * inverse
                work[m] = jnp.where(mine, scaled, work[m] - columns[m][j] * scaled)
        for m in range(count):
            done[m].append(jnp.where(lane < first + 8, kept[m], 0.0))
            pivots = [spread(work[m][j : j + 1, :]) for j in range(8)]
            for i in range(g + 1, groups):
                old = rows[m][i]
                new = jnp.where(inside, 0.0, old)
                for j in range(8):
                    new = new - spread(old[:, first + j : first + j + 1]) * pivots[j]
                rows[m][i] = new
    return [jnp.concatenate(values, 0) for values in done]


def dot_last(left, right):
    return lax.dot_general(
        left, right, (((1,), (1,)), ((), ())), preferred_element_type=F32, precision=HIGHEST
    )


def reduced_system(inverse_count, place, first, second, index):
    snaps = first.shape[2]
    share = snaps // PARTS
    half = snaps // 2
    order = [first_piece(place ^ c) for c in range(PARTS)]
    packed = jnp.concatenate([first[at, :share, :] for at in order], 0) * inverse_count
    load = first[0, share : share + 1, :] * inverse_count
    diagonal = first[0, share + 1 : share + 2, :] * inverse_count
    order = [second_place(place ^ c) for c in range(PARTS)]
    cross = jnp.concatenate([second[at] for at in order], 0) * inverse_count
    row = lax.broadcasted_iota(jnp.int32, (snaps, snaps), 0)
    column = lax.broadcasted_iota(jnp.int32, (snaps, snaps), 1)
    turned = packed.T
    gram = jnp.where(row <= column, packed, turned)
    square = jnp.where(row > column, packed, jnp.where(row == column, diagonal, turned))
    project = gram + cross.T
    normal = project + cross + square

    pair = (gram, normal)
    upper = inverse_factors([value[:half, :half] for value in pair])
    below = [dot_last(value[half:, :half], inv) for value, inv in zip(pair, upper)]
    rest = [value[half:, half:] - dot_last(low, low) for value, low in zip(pair, below)]
    lower = inverse_factors(rest)
    inverses = []
    for top, low, bottom in zip(upper, below, lower):
        corner = -matmul(bottom, matmul(low, top, HIGHEST), HIGHEST)
        inverses.append(
            jnp.concatenate(
                [
                    jnp.concatenate([top, jnp.zeros((half, half), F32)], 1),
                    jnp.concatenate([corner, bottom], 1),
                ],
                0,
            )
        )
    gram_inverse, normal_inverse = inverses
    root = gram_inverse.T

    across = lambda matrix, vector: jnp.sum(matrix * vector, 1, keepdims=True)
    down = lambda matrix, vector: jnp.sum(matrix * vector, 0, keepdims=True)
    state = jnp.where(index == jnp.max(index), 1.0, 0.0)
    eye = jnp.where(row == column, 1.0, 0.0)
    history = []
    for _ in range(STEPS):
        old = state
        right = down(eye, across(project, state)) + STEP_SIZE * load
        state = down(normal_inverse, across(normal_inverse, right))
        history.append(down(root, across(gram, state)))
    return root, history, state - old, state


def final_kernel(
    inverse_count,
    place_ref,
    first_low,
    first_high,
    second_low,
    second_high,
    index_ref,
    force_ref,
    snap_any,
    image_any,
    basis_any,
    coeff_ref,
    residual_ref,
    snap,
    image,
    first,
    second,
    root_ref,
    change_ref,
    state_ref,
    tile,
    snap_sems,
    image_sems,
    basis_sems,
):
    rows, snaps = snap.shape
    block = force_ref.shape[1]
    chunks = rows // CHUNK
    per_chunk = CHUNK // block

    def chunk(i):
        return pl.ds(pl.multiple_of(i * CHUNK, CHUNK), CHUNK)

    def snap_copy(i):
        return pltpu.make_async_copy(snap_any.at[chunk(i), :], snap.at[chunk(i), :], snap_sems.at[i])

    def image_copy(i):
        return pltpu.make_async_copy(image_any.at[chunk(i), :], image.at[chunk(i), :], image_sems.at[i])

    def out_copy(i):
        return pltpu.make_async_copy(snap.at[chunk(i), :], basis_any.at[chunk(i), :], basis_sems.at[i])

    for i in range(chunks):
        snap_copy(i).start()
        image_copy(i).start()
    first[: PARTS // 2] = first_low[...]
    first[PARTS // 2 :] = first_high[...]
    second[: PARTS // 2] = second_low[...]
    second[PARTS // 2 :] = second_high[...]
    root, history, change, state = reduced_system(inverse_count, place_ref[0], first, second, index_ref[...])
    high, low = split(root)
    root_ref[:, :snaps] = high
    root_ref[:, snaps:] = low
    for n in range(STEPS):
        coeff_ref[n : n + 1, :] = history[n]
    change_ref[...] = change
    state_ref[...] = state
    tile[...] = jnp.zeros_like(tile)
    lane = lax.broadcasted_iota(jnp.int32, (block, block), 1)

    @pl.loop(0, chunks)
    def _(i):
        snap_copy(i).wait()
        image_copy(i).wait()
        at = chunk(i)
        panel = snap[at, :]
        sums = jnp.sum(panel * change_ref[...] + image[at, :] * state_ref[...], 1, keepdims=True)
        gathered = tile[...]
        for k in range(per_chunk):
            gathered = jnp.where(lane == i * per_chunk + k, sums[k * block : (k + 1) * block], gathered)
        tile[...] = gathered
        panel_high, panel_low = split(panel)
        both = matmul(panel_high, root_ref[...])
        snap[at, :] = both[:, :snaps] + both[:, snaps:] + matmul(panel_low, root_ref[:, :snaps])
        out_copy(i).start()

    residual_ref[...] = tile[...].T[: rows // block] - STEP_SIZE * force_ref[...]

    @pl.loop(0, chunks)
    def _(i):
        out_copy(i).wait()


def final_call(pieces, step_index, place, snapshots, image, force, inverse_count):
    rows, snaps = snapshots.shape
    block = force.shape[1]
    share = snaps // PARTS
    chunks = rows // CHUNK
    vmem = pl.BlockSpec(memory_space=pltpu.VMEM)
    hbm = pl.BlockSpec(memory_space=pl.ANY)
    return pl.pallas_call(
        functools.partial(final_kernel, inverse_count),
        out_shape=(
            jax.ShapeDtypeStruct((rows, snaps), F32),
            jax.ShapeDtypeStruct((STEPS, snaps), F32),
            jax.ShapeDtypeStruct(force.shape, F32),
        ),
        in_specs=[pl.BlockSpec(memory_space=pltpu.SMEM)] + [vmem] * 6 + [hbm, hbm],
        out_specs=[hbm, vmem, vmem],
        scratch_shapes=[
            pltpu.VMEM((rows, snaps), F32),
            pltpu.VMEM((rows, snaps), F32),
            pltpu.VMEM((PARTS, share + 8, snaps), F32),
            pltpu.VMEM((PARTS, share, snaps), F32),
            pltpu.VMEM((snaps, 2 * snaps), BF16),
            pltpu.VMEM((1, snaps), F32),
            pltpu.VMEM((1, snaps), F32),
            pltpu.VMEM((block, block), F32),
            pltpu.SemaphoreType.DMA((chunks,)),
            pltpu.SemaphoreType.DMA((chunks,)),
            pltpu.SemaphoreType.DMA((chunks,)),
        ],
        compiler_params=pltpu.CompilerParams(vmem_limit_bytes=LIMIT),
        name="final",
    )(place, *pieces, step_index, force, snapshots, image)


def shifted(value, axis, steps):
    count = lax.axis_size(axis)
    pairs = [(source, (source + steps) % count) for source in range(count)]
    return lax.ppermute(value, axis, pairs)


def from_behind(shard, axis, by):
    devices = lax.axis_size(axis)
    pairs = [(i, i + by) for i in range(devices) if 0 <= i + by < devices]
    return lax.ppermute(shard, axis, pairs)


def partner(value, axis, bit):
    count = lax.axis_size(axis)
    return lax.ppermute(value, axis, [(i, i ^ bit) for i in range(count)])


def reduce_packed(keep_first, send_first, keep_second, send_second):
    core, x, y = ("zone", 1), ("zone", 2), ("rows", 1)
    first = keep_first + partner(send_first, *core)
    second = keep_second + partner(send_second, *core)
    for way_first, way_second in ((x, y), (y, x)):
        half = first.shape[0] // 2
        first = first[:half] + partner(first[half:], *way_first)
        second = second[:half] + partner(second[half:], *way_second)
    edge = first.shape[1]
    value = jnp.concatenate([first, second], 1)
    for axis, least in (("rows", 2), ("zone", 4)):
        bit = least
        while bit < lax.axis_size(axis):
            value = value + partner(value, axis, bit)
            bit *= 2
    first, second = value[:, :edge], value[:, edge:]
    for way_first, way_second in ((y, x), (x, y)):
        first = jnp.concatenate([first, partner(first, *way_first)], 0)
        second = jnp.concatenate([second, partner(second, *way_second)], 0)
    return first, partner(first, *core), second, partner(second, *core)


def shards(snapshots, tangent, pattern, forcing, step_index):
    rows, snaps = snapshots.shape
    blocks = pattern.shape[0]
    block = rows // blocks
    edge = HALO * block
    inverse_count = 1.0 / (rows * lax.axis_size("rows") * lax.axis_size("zone"))
    place = (lax.axis_index("zone") & 3) | ((lax.axis_index("rows") & 1) << 2)
    place = jnp.reshape(place, (1,)).astype(jnp.int32)
    force = forcing.reshape(blocks, block)
    head, tail = snapshots[:edge], snapshots[rows - edge :]
    rows_prev = shifted(tail, "rows", 1)
    rows_next = shifted(head, "rows", -1)
    field, turned, gram, load = gram_call(snapshots, force)
    halos = (from_behind(tail, "zone", 1), from_behind(head, "zone", -1), rows_prev, rows_next)
    image, *packed = tangent_call(field, turned, halos, tangent, pattern, force, gram, load, place)
    pieces = reduce_packed(*packed)
    basis, coefficients, residual = final_call(
        pieces, step_index.reshape(1, snaps), place, snapshots, image, force, inverse_count
    )
    return basis, coefficients, residual.reshape(rows)


def solution(mesh):
    in_specs = (
        P(("rows", "zone"), None),
        P(("rows", "zone"), None),
        P(("rows", "zone"), None),
        P(("rows", "zone")),
        P(),
    )
    out_specs = (P(("rows", "zone"), None), P(), P(("rows", "zone")))
    return jax.shard_map(shards, mesh=mesh, in_specs=in_specs, out_specs=out_specs, check_vma=False)
```

```python
import functools

import jax
import jax.numpy as jnp
from jax import lax
from jax.experimental import pallas as pl
from jax.experimental.pallas import tpu as pltpu
from jax.sharding import PartitionSpec as P

HALO = 4
STEPS = 3
STEP_SIZE = 0.25
CHUNK = 1024
MIB = 1024 * 1024
PARTS = 8
F32 = jnp.float32
BF16 = jnp.bfloat16
HIGHEST = lax.Precision.HIGHEST


def split(value):
    high = value.astype(BF16)
    low = (value - high.astype(F32)).astype(BF16)
    return high, low


def contract_rows(left, right):
    return lax.dot_general(left, right, (((0,), (0,)), ((), ())), preferred_element_type=F32)


def matmul(left, right, precision=None):
    return lax.dot_general(
        left, right, (((1,), (0,)), ((), ())), preferred_element_type=F32, precision=precision
    )


def first_piece(at):
    return ((at >> 2) & 1) | (at & 2) | ((at & 1) << 2)


def second_piece(at):
    return ((at >> 2) & 1) | ((at & 1) << 1) | ((at & 2) << 1)


def second_place(piece):
    return ((piece & 1) << 2) | ((piece >> 1) & 1) | ((piece >> 1) & 2)


def force_product(panel, force):
    columns = force.T
    block = force.shape[1]
    total = jnp.zeros((1, panel.shape[1]), F32)
    for k in range(force.shape[0]):
        total += jnp.sum(panel[k * block : (k + 1) * block] * columns[:, k : k + 1], 0, keepdims=True)
    return total


def gram_kernel(snap_ref, force_ref, gram_ref, load_ref):
    rows = snap_ref.shape[0]
    per_chunk = CHUNK // force_ref.shape[1]
    gram_ref[...] = jnp.zeros_like(gram_ref)
    load_ref[...] = jnp.zeros_like(load_ref)

    @pl.loop(0, rows // CHUNK)
    def _(i):
        panel = snap_ref[pl.ds(pl.multiple_of(i * CHUNK, CHUNK), CHUNK), :]
        high, low = split(panel)
        gram_ref[...] += matmul(high.T, jnp.concatenate([high, low], 1))
        line = pl.ds(pl.multiple_of(i * per_chunk, per_chunk), per_chunk)
        load_ref[...] += force_product(panel, force_ref[line, :])


def gram_call(snapshots, force):
    rows, snaps = snapshots.shape
    vmem = pl.BlockSpec(memory_space=pltpu.VMEM)
    return pl.pallas_call(
        gram_kernel,
        out_shape=(
            jax.ShapeDtypeStruct((snaps, 2 * snaps), F32),
            jax.ShapeDtypeStruct((1, snaps), F32),
        ),
        in_specs=[vmem, vmem],
        out_specs=[vmem, vmem],
        compiler_params=pltpu.CompilerParams(vmem_limit_bytes=10 * MIB),
        cost_estimate=pl.CostEstimate(
            flops=4 * rows * snaps * snaps, bytes_accessed=4 * rows * snaps, transcendentals=0
        ),
        name="gram",
    )(snapshots, force)


def tangent_kernel(
    pattern_ref,
    place_ref,
    snap,
    left_ref,
    right_ref,
    prev_ref,
    next_ref,
    tangent_any,
    force_ref,
    gram_ref,
    load_ref,
    image,
    keep_first,
    send_first,
    keep_second,
    send_second,
    field,
    mixed,
    rest,
    load,
    packed,
    tangent,
    sems,
):
    rows, snaps = image.shape
    block_count, coupled = pattern_ref.shape
    block = rows // block_count
    edge = HALO * block
    chunks = rows // CHUNK
    per_chunk = CHUNK // block

    def tangent_copy(i):
        at = pl.ds(pl.multiple_of(i * CHUNK, CHUNK), CHUNK)
        return pltpu.make_async_copy(tangent_any.at[at, :], tangent.at[at, :], sems.at[i])

    for i in range(chunks):
        tangent_copy(i).start()

    def enter(at, value):
        high, low = split(value)
        field[at, :snaps] = high
        field[at, snaps:] = low

    @pl.loop(0, chunks)
    def _(i):
        at = pl.ds(pl.multiple_of(i * CHUNK, CHUNK), CHUNK)
        enter(at, snap[at, :])

    for i, ref in enumerate((left_ref, right_ref, prev_ref, next_ref)):
        enter(pl.ds(rows + i * edge, edge), ref[...])
    mixed[...] = jnp.zeros_like(mixed)
    rest[...] = jnp.zeros_like(rest)
    load[...] = load_ref[...]

    @pl.loop(0, chunks)
    def _(step):
        start = pl.multiple_of(step * CHUNK, CHUNK)
        here = field[pl.ds(start, CHUNK), :]
        panels = [here[:, :snaps].T, here[:, snaps:].T]
        tangent_copy(step).wait()
        images = []
        for k in range(per_chunk):
            g = step * per_chunk + k
            picked = []
            for e in range(coupled):
                code = pattern_ref[g, e]
                source = lax.div(code, block_count)
                pick = lax.rem(code, block_count)
                tail = (source == 1) | (source == 3)
                base = jnp.where(source == 0, 0, block_count + ((source + 1) & 3) * HALO)
                at = base + jnp.where(tail, pick - (block_count - HALO), pick)
                picked.append(field[pl.ds(pl.multiple_of(at * block, block), block), :])
            own = pl.ds(pl.multiple_of(start + k * block, block), block)
            both = matmul(tangent[own, :], jnp.concatenate(picked, 0))
            part = STEP_SIZE * (both[:, :snaps] + both[:, snaps:])
            image[own, :] = part
            images.append(part)
        panel = jnp.concatenate(images, 0)
        line = pl.ds(pl.multiple_of(step * per_chunk, per_chunk), per_chunk)
        load[...] += force_product(panel, force_ref[line, :])
        high, low = split(panel)
        high_turned = high.T
        mixed[...] += matmul(jnp.concatenate([*panels, high_turned], 0), high)
        rest[...] += matmul(jnp.concatenate([panels[0], high_turned], 0), low)

    gram = gram_ref[:, :snaps] + gram_ref[:, snaps:] + gram_ref[:, snaps:].T
    cross = mixed[:snaps] + mixed[snaps : 2 * snaps] + rest[:snaps]
    square = mixed[2 * snaps :] + rest[snaps:] + rest[snaps:].T
    row = lax.broadcasted_iota(jnp.int32, (snaps, snaps), 0)
    column = lax.broadcasted_iota(jnp.int32, (snaps, snaps), 1)
    diagonal = jnp.sum(jnp.where(row == column, square, 0.0), 0, keepdims=True)
    packed[0] = jnp.where(row <= column, gram, square)
    packed[1] = cross
    extra_row = lax.broadcasted_iota(jnp.int32, (8, snaps), 0)
    extra = jnp.where(extra_row == 0, load[...], jnp.where(extra_row == 1, diagonal, 0.0))
    share = snaps // PARTS
    for at in range(PARTS):
        first = keep_first if at < PARTS // 2 else send_first
        second = keep_second if at < PARTS // 2 else send_second
        slot = at % (PARTS // 2)
        begin = pl.multiple_of((place_ref[0] ^ first_piece(at)) * share, 8)
        first[slot, :share, :] = packed[0, pl.ds(begin, share), :]
        first[slot, share:, :] = extra
        begin = pl.multiple_of((place_ref[0] ^ second_piece(at)) * share, 8)
        second[slot] = packed[1, pl.ds(begin, share), :]


def tangent_call(snapshots, halos, tangent, pattern, force, gram, load, place):
    rows, snaps = snapshots.shape
    share = snaps // PARTS
    edge = halos[0].shape[0]
    vmem = pl.BlockSpec(memory_space=pltpu.VMEM)
    smem = pl.BlockSpec(memory_space=pltpu.SMEM)
    first = jax.ShapeDtypeStruct((PARTS // 2, share + 8, snaps), F32)
    second = jax.ShapeDtypeStruct((PARTS // 2, share, snaps), F32)
    return pl.pallas_call(
        tangent_kernel,
        out_shape=(jax.ShapeDtypeStruct((rows, snaps), F32), first, first, second, second),
        in_specs=[smem, smem] + [vmem] * 5 + [pl.BlockSpec(memory_space=pl.ANY)] + [vmem] * 3,
        out_specs=[vmem] * 5,
        scratch_shapes=[
            pltpu.VMEM((rows + 4 * edge, 2 * snaps), BF16),
            pltpu.VMEM((3 * snaps, snaps), F32),
            pltpu.VMEM((2 * snaps, snaps), F32),
            pltpu.VMEM((1, snaps), F32),
            pltpu.VMEM((2, snaps, snaps), F32),
            pltpu.VMEM(tangent.shape, BF16),
            pltpu.SemaphoreType.DMA((rows // CHUNK,)),
        ],
        compiler_params=pltpu.CompilerParams(vmem_limit_bytes=40 * MIB),
        name="tangent",
    )(pattern, place, snapshots, *halos, tangent, force, gram, load)


def inverse_factors(blocks):
    size = blocks[0].shape[0]
    groups = size // 8
    lane = lax.broadcasted_iota(jnp.int32, (8, size), 1)
    sub = lax.broadcasted_iota(jnp.int32, (8, size), 0)
    spread = lambda value: jnp.broadcast_to(value, (8, size))
    count = len(blocks)
    rows = [[value[8 * g : 8 * g + 8, :] for g in range(groups)] for value in blocks]
    done = [[] for _ in blocks]
    for g in range(groups):
        first = 8 * g
        inside = (lane >= first) & (lane < first + 8)
        unit = jnp.where(lane == sub + first, 1.0, 0.0)
        columns = [
            [spread(rows[m][g][:, first + j : first + j + 1]) for j in range(8)] for m in range(count)
        ]
        work = [jnp.where(inside, unit, rows[m][g]) for m in range(count)]
        kept = [jnp.zeros((8, size), F32) for _ in range(count)]
        for j in range(8):
            for m in range(count):
                pivot = spread(columns[m][j][j : j + 1, :])
                inverse = 1.0 / pivot
                root = lax.rsqrt(pivot)
                root = root * (1.5 - 0.5 * pivot * root * root)
                mine = sub == j
                for k in range(j + 1, 8):
                    scaled = spread(columns[m][k][j : j + 1, :]) * inverse
                    columns[m][k] = jnp.where(mine, scaled, columns[m][k] - columns[m][j] * scaled)
                row = spread(work[m][j : j + 1, :])
                kept[m] = jnp.where(mine, row * root, kept[m])
                scaled = row * inverse
                work[m] = jnp.where(mine, scaled, work[m] - columns[m][j] * scaled)
        for m in range(count):
            done[m].append(jnp.where(lane < first + 8, kept[m], 0.0))
            pivots = [spread(work[m][j : j + 1, :]) for j in range(8)]
            for i in range(g + 1, groups):
                old = rows[m][i]
                new = jnp.where(inside, 0.0, old)
                for j in range(8):
                    new = new - spread(old[:, first + j : first + j + 1]) * pivots[j]
                rows[m][i] = new
    return [jnp.concatenate(values, 0) for values in done]


def dot_last(left, right):
    return lax.dot_general(
        left, right, (((1,), (1,)), ((), ())), preferred_element_type=F32, precision=HIGHEST
    )


def reduced_system(inverse_count, place, first, second, index):
    snaps = first.shape[2]
    share = snaps // PARTS
    half = snaps // 2
    order = [first_piece(place ^ c) for c in range(PARTS)]
    packed = jnp.concatenate([first[at, :share, :] for at in order], 0) * inverse_count
    load = first[0, share : share + 1, :] * inverse_count
    diagonal = first[0, share + 1 : share + 2, :] * inverse_count
    order = [second_place(place ^ c) for c in range(PARTS)]
    cross = jnp.concatenate([second[at] for at in order], 0) * inverse_count
    row = lax.broadcasted_iota(jnp.int32, (snaps, snaps), 0)
    column = lax.broadcasted_iota(jnp.int32, (snaps, snaps), 1)
    turned = packed.T
    gram = jnp.where(row <= column, packed, turned)
    square = jnp.where(row > column, packed, jnp.where(row == column, diagonal, turned))
    project = gram + cross.T
    normal = project + cross + square

    pair = (gram, normal)
    upper = inverse_factors([value[:half, :half] for value in pair])
    below = [dot_last(value[half:, :half], inv) for value, inv in zip(pair, upper)]
    rest = [value[half:, half:] - dot_last(low, low) for value, low in zip(pair, below)]
    lower = inverse_factors(rest)
    inverses = []
    for top, low, bottom in zip(upper, below, lower):
        corner = -matmul(bottom, matmul(low, top, HIGHEST), HIGHEST)
        inverses.append(
            jnp.concatenate(
                [
                    jnp.concatenate([top, jnp.zeros((half, half), F32)], 1),
                    jnp.concatenate([corner, bottom], 1),
                ],
                0,
            )
        )
    gram_inverse, normal_inverse = inverses
    root = gram_inverse.T

    across = lambda matrix, vector: jnp.sum(matrix * vector, 1, keepdims=True)
    down = lambda matrix, vector: jnp.sum(matrix * vector, 0, keepdims=True)
    state = jnp.where(index == jnp.max(index), 1.0, 0.0)
    eye = jnp.where(row == column, 1.0, 0.0)
    history = []
    for _ in range(STEPS):
        old = state
        right = down(eye, across(project, state)) + STEP_SIZE * load
        state = down(normal_inverse, across(normal_inverse, right))
        history.append(down(root, across(gram, state)))
    return root, history, state - old, state


def final_kernel(
    inverse_count,
    place_ref,
    first_low,
    first_high,
    second_low,
    second_high,
    index_ref,
    force_ref,
    snap,
    image,
    basis_any,
    coeff_ref,
    residual_ref,
    first,
    second,
    root_ref,
    change_ref,
    state_ref,
    tile,
    basis,
    sems,
):
    rows, snaps = snap.shape
    block = force_ref.shape[1]
    chunks = rows // CHUNK
    per_chunk = CHUNK // block

    def chunk(i):
        return pl.ds(pl.multiple_of(i * CHUNK, CHUNK), CHUNK)

    def out_copy(i):
        return pltpu.make_async_copy(basis.at[i % 2], basis_any.at[chunk(i), :], sems.at[i % 2])

    first[: PARTS // 2] = first_low[...]
    first[PARTS // 2 :] = first_high[...]
    second[: PARTS // 2] = second_low[...]
    second[PARTS // 2 :] = second_high[...]
    root, history, change, state = reduced_system(inverse_count, place_ref[0], first, second, index_ref[...])
    high, low = split(root)
    root_ref[:, :snaps] = high
    root_ref[:, snaps:] = low
    for n in range(STEPS):
        coeff_ref[n : n + 1, :] = history[n]
    change_ref[...] = change
    state_ref[...] = state
    tile[...] = jnp.zeros_like(tile)
    lane = lax.broadcasted_iota(jnp.int32, (block, block), 1)

    @pl.loop(0, chunks)
    def _(i):
        at = chunk(i)
        panel = snap[at, :]
        sums = jnp.sum(panel * change_ref[...] + image[at, :] * state_ref[...], 1, keepdims=True)
        gathered = tile[...]
        for k in range(per_chunk):
            gathered = jnp.where(lane == i * per_chunk + k, sums[k * block : (k + 1) * block], gathered)
        tile[...] = gathered
        panel_high, panel_low = split(panel)
        both = matmul(panel_high, root_ref[...])

        @pl.when(i >= 2)
        def _():
            out_copy(i - 2).wait()

        basis[i % 2] = both[:, :snaps] + both[:, snaps:] + matmul(panel_low, root_ref[:, :snaps])
        out_copy(i).start()

    residual_ref[...] = tile[...].T[: rows // block] - STEP_SIZE * force_ref[...]

    for i in range(chunks - 2, chunks):
        out_copy(i).wait()


def final_call(pieces, step_index, place, snapshots, image, force, inverse_count):
    rows, snaps = snapshots.shape
    block = force.shape[1]
    share = snaps // PARTS
    vmem = pl.BlockSpec(memory_space=pltpu.VMEM)
    hbm = pl.BlockSpec(memory_space=pl.ANY)
    return pl.pallas_call(
        functools.partial(final_kernel, inverse_count),
        out_shape=(
            jax.ShapeDtypeStruct((rows, snaps), F32),
            jax.ShapeDtypeStruct((STEPS, snaps), F32),
            jax.ShapeDtypeStruct(force.shape, F32),
        ),
        in_specs=[pl.BlockSpec(memory_space=pltpu.SMEM)] + [vmem] * 8,
        out_specs=[hbm, vmem, vmem],
        scratch_shapes=[
            pltpu.VMEM((PARTS, share + 8, snaps), F32),
            pltpu.VMEM((PARTS, share, snaps), F32),
            pltpu.VMEM((snaps, 2 * snaps), BF16),
            pltpu.VMEM((1, snaps), F32),
            pltpu.VMEM((1, snaps), F32),
            pltpu.VMEM((block, block), F32),
            pltpu.VMEM((2, CHUNK, snaps), F32),
            pltpu.SemaphoreType.DMA((2,)),
        ],
        compiler_params=pltpu.CompilerParams(vmem_limit_bytes=12 * MIB),
        name="final",
    )(place, *pieces, step_index, force, snapshots, image)


def shifted(value, axis, steps):
    count = lax.axis_size(axis)
    pairs = [(source, (source + steps) % count) for source in range(count)]
    return lax.ppermute(value, axis, pairs)


def from_behind(shard, axis, by):
    devices = lax.axis_size(axis)
    pairs = [(i, i + by) for i in range(devices) if 0 <= i + by < devices]
    return lax.ppermute(shard, axis, pairs)


def partner(value, axis, bit):
    count = lax.axis_size(axis)
    return lax.ppermute(value, axis, [(i, i ^ bit) for i in range(count)])


def reduce_packed(keep_first, send_first, keep_second, send_second):
    core, x, y = ("zone", 1), ("zone", 2), ("rows", 1)
    first = keep_first + partner(send_first, *core)
    second = keep_second + partner(send_second, *core)
    for way_first, way_second in ((x, y), (y, x)):
        half = first.shape[0] // 2
        first = first[:half] + partner(first[half:], *way_first)
        second = second[:half] + partner(second[half:], *way_second)
    edge = first.shape[1]
    value = jnp.concatenate([first, second], 1)
    for axis, least in (("rows", 2), ("zone", 4)):
        bit = least
        while bit < lax.axis_size(axis):
            value = value + partner(value, axis, bit)
            bit *= 2
    first, second = value[:, :edge], value[:, edge:]
    for way_first, way_second in ((y, x), (x, y)):
        first = jnp.concatenate([first, partner(first, *way_first)], 0)
        second = jnp.concatenate([second, partner(second, *way_second)], 0)
    return first, partner(first, *core), second, partner(second, *core)


def shards(snapshots, tangent, pattern, forcing, step_index):
    rows, snaps = snapshots.shape
    blocks = pattern.shape[0]
    block = rows // blocks
    edge = HALO * block
    inverse_count = 1.0 / (rows * lax.axis_size("rows") * lax.axis_size("zone"))
    place = (lax.axis_index("zone") & 3) | ((lax.axis_index("rows") & 1) << 2)
    place = jnp.reshape(place, (1,)).astype(jnp.int32)
    force = forcing.reshape(blocks, block)
    head, tail = snapshots[:edge], snapshots[rows - edge :]
    rows_prev = shifted(tail, "rows", 1)
    rows_next = shifted(head, "rows", -1)
    gram, load = gram_call(snapshots, force)
    halos = (from_behind(tail, "zone", 1), from_behind(head, "zone", -1), rows_prev, rows_next)
    image, *packed = tangent_call(snapshots, halos, tangent, pattern, force, gram, load, place)
    pieces = reduce_packed(*packed)
    basis, coefficients, residual = final_call(
        pieces, step_index.reshape(1, snaps), place, snapshots, image, force, inverse_count
    )
    return basis, coefficients, residual.reshape(rows)


def solution(mesh):
    in_specs = (
        P(("rows", "zone"), None),
        P(("rows", "zone"), None),
        P(("rows", "zone"), None),
        P(("rows", "zone")),
        P(),
    )
    out_specs = (P(("rows", "zone"), None), P(), P(("rows", "zone")))
    return jax.shard_map(shards, mesh=mesh, in_specs=in_specs, out_specs=out_specs, check_vma=False)
```

```python
import functools

import jax
import jax.numpy as jnp
from jax import lax
from jax.experimental import pallas as pl
from jax.experimental.pallas import tpu as pltpu
from jax.sharding import PartitionSpec as P

HALO = 4
STEPS = 3
STEP_SIZE = 0.25
CHUNK = 1024
MIB = 1024 * 1024
PARTS = 8
F32 = jnp.float32
BF16 = jnp.bfloat16
HIGHEST = lax.Precision.HIGHEST


def split(value):
    high = value.astype(BF16)
    low = (value - high.astype(F32)).astype(BF16)
    return high, low


def contract_rows(left, right):
    return lax.dot_general(left, right, (((0,), (0,)), ((), ())), preferred_element_type=F32)


def matmul(left, right, precision=None):
    return lax.dot_general(
        left, right, (((1,), (0,)), ((), ())), preferred_element_type=F32, precision=precision
    )


def piece_at(position):
    return ((position >> 2) & 1) | (position & 2) | ((position & 1) << 2)


def force_product(panel, force):
    columns = force.T
    block = force.shape[1]
    total = jnp.zeros((1, panel.shape[1]), F32)
    for k in range(force.shape[0]):
        total += jnp.sum(panel[k * block : (k + 1) * block] * columns[:, k : k + 1], 0, keepdims=True)
    return total


def gram_kernel(snap_ref, force_ref, field_ref, turned_ref, gram_ref, load_ref):
    rows = snap_ref.shape[0]
    per_chunk = CHUNK // force_ref.shape[1]
    gram_ref[...] = jnp.zeros_like(gram_ref)
    load_ref[...] = jnp.zeros_like(load_ref)

    @pl.loop(0, rows // CHUNK)
    def _(i):
        at = pl.ds(pl.multiple_of(i * CHUNK, CHUNK), CHUNK)
        panel = snap_ref[at, :]
        snaps = panel.shape[1]
        high, low = split(panel)
        turned = high.T
        field_ref[at, :snaps] = high
        field_ref[at, snaps:] = low
        turned_ref[i, :snaps, :] = turned
        turned_ref[i, snaps:, :] = low.T
        gram_ref[...] += matmul(turned, jnp.concatenate([high, low], 1))
        line = pl.ds(pl.multiple_of(i * per_chunk, per_chunk), per_chunk)
        load_ref[...] += force_product(panel, force_ref[line, :])


def gram_call(snapshots, force):
    rows, snaps = snapshots.shape
    vmem = pl.BlockSpec(memory_space=pltpu.VMEM)
    return pl.pallas_call(
        gram_kernel,
        out_shape=(
            jax.ShapeDtypeStruct((rows, 2 * snaps), BF16),
            jax.ShapeDtypeStruct((rows // CHUNK, 2 * snaps, CHUNK), BF16),
            jax.ShapeDtypeStruct((snaps, 2 * snaps), F32),
            jax.ShapeDtypeStruct((1, snaps), F32),
        ),
        in_specs=[vmem, vmem],
        out_specs=[vmem] * 4,
        compiler_params=pltpu.CompilerParams(vmem_limit_bytes=10 * MIB),
        cost_estimate=pl.CostEstimate(
            flops=4 * rows * snaps * snaps, bytes_accessed=4 * rows * snaps, transcendentals=0
        ),
        name="gram",
    )(snapshots, force)


def tangent_kernel(
    pattern_ref,
    place_ref,
    field,
    turned,
    left_ref,
    right_ref,
    prev_ref,
    next_ref,
    tangent_any,
    force_ref,
    gram_ref,
    load_ref,
    image,
    keep_ref,
    send_ref,
    halo,
    mixed,
    rest,
    load,
    packed,
    tangent,
    sems,
):
    rows, snaps = image.shape
    block_count, coupled = pattern_ref.shape
    block = rows // block_count
    edge = HALO * block
    chunks = rows // CHUNK
    per_chunk = CHUNK // block

    def tangent_copy(i):
        at = pl.ds(pl.multiple_of(i * CHUNK, CHUNK), CHUNK)
        return pltpu.make_async_copy(tangent_any.at[at, :], tangent.at[at, :], sems.at[i])

    for i in range(chunks):
        tangent_copy(i).start()

    for i, ref in enumerate((left_ref, right_ref, prev_ref, next_ref)):
        high, low = split(ref[...])
        at = pl.ds(i * edge, edge)
        halo[at, :snaps] = high
        halo[at, snaps:] = low
    mixed[...] = jnp.zeros_like(mixed)
    rest[...] = jnp.zeros_like(rest)
    load[...] = load_ref[...]

    @pl.loop(0, chunks)
    def _(step):
        start = pl.multiple_of(step * CHUNK, CHUNK)
        tangent_copy(step).wait()
        images = []
        for k in range(per_chunk):
            g = step * per_chunk + k
            picked = []
            for e in range(coupled):
                code = pattern_ref[g, e]
                source = lax.div(code, block_count)
                pick = lax.rem(code, block_count)
                here = source == 0
                tail = (source == 1) | (source == 3)
                beyond = ((source + 1) & 3) * HALO + jnp.where(tail, pick - (block_count - HALO), pick)
                beyond = jnp.where(here, 0, beyond)
                inner = field[pl.ds(pl.multiple_of(pick * block, block), block), :]
                outer = halo[pl.ds(pl.multiple_of(beyond * block, block), block), :]
                picked.append(lax.select(here, inner, outer))
            own = pl.ds(pl.multiple_of(start + k * block, block), block)
            both = matmul(tangent[own, :], jnp.concatenate(picked, 0))
            part = STEP_SIZE * (both[:, :snaps] + both[:, snaps:])
            image[own, :] = part
            images.append(part)
        panel = jnp.concatenate(images, 0)
        line = pl.ds(pl.multiple_of(step * per_chunk, per_chunk), per_chunk)
        load[...] += force_product(panel, force_ref[line, :])
        high, low = split(panel)
        high_turned = high.T
        panels = turned[step]
        mixed[...] += matmul(jnp.concatenate([panels, high_turned], 0), high)
        rest[...] += matmul(jnp.concatenate([panels[:snaps], high_turned], 0), low)

    gram = gram_ref[:, :snaps] + gram_ref[:, snaps:] + gram_ref[:, snaps:].T
    cross = mixed[:snaps] + mixed[snaps : 2 * snaps] + rest[:snaps]
    square = mixed[2 * snaps :] + rest[snaps:] + rest[snaps:].T
    row = lax.broadcasted_iota(jnp.int32, (snaps, snaps), 0)
    column = lax.broadcasted_iota(jnp.int32, (snaps, snaps), 1)
    diagonal = jnp.sum(jnp.where(row == column, square, 0.0), 0, keepdims=True)
    packed[0] = jnp.where(row <= column, gram, square)
    packed[1] = cross
    extra_row = lax.broadcasted_iota(jnp.int32, (8, snaps), 0)
    extra = jnp.where(extra_row == 0, load[...], jnp.where(extra_row == 1, diagonal, 0.0))
    share = snaps // PARTS
    for at in range(PARTS):
        out = keep_ref if at < PARTS // 2 else send_ref
        slot = at % (PARTS // 2)
        begin = pl.multiple_of((place_ref[0] ^ piece_at(at)) * share, 8)
        out[slot, :share, :] = packed[0, pl.ds(begin, share), :]
        out[slot, share : 2 * share, :] = packed[1, pl.ds(begin, share), :]
        out[slot, 2 * share :, :] = extra


def tangent_call(field, turned, halos, tangent, pattern, force, gram, load, place):
    rows = tangent.shape[0]
    snaps = gram.shape[0]
    share = snaps // PARTS
    edge = halos[0].shape[0]
    vmem = pl.BlockSpec(memory_space=pltpu.VMEM)
    smem = pl.BlockSpec(memory_space=pltpu.SMEM)
    packed = jax.ShapeDtypeStruct((PARTS // 2, 2 * share + 8, snaps), F32)
    return pl.pallas_call(
        tangent_kernel,
        out_shape=(jax.ShapeDtypeStruct((rows, snaps), F32), packed, packed),
        in_specs=[smem, smem] + [vmem] * 6 + [pl.BlockSpec(memory_space=pl.ANY)] + [vmem] * 3,
        out_specs=[vmem] * 3,
        scratch_shapes=[
            pltpu.VMEM((4 * edge, 2 * snaps), BF16),
            pltpu.VMEM((3 * snaps, snaps), F32),
            pltpu.VMEM((2 * snaps, snaps), F32),
            pltpu.VMEM((1, snaps), F32),
            pltpu.VMEM((2, snaps, snaps), F32),
            pltpu.VMEM(tangent.shape, BF16),
            pltpu.SemaphoreType.DMA((rows // CHUNK,)),
        ],
        compiler_params=pltpu.CompilerParams(vmem_limit_bytes=18 * MIB),
        name="tangent",
    )(pattern, place, field, turned, *halos, tangent, force, gram, load)


def inverse_factors(blocks):
    size = blocks[0].shape[0]
    groups = size // 8
    lane = lax.broadcasted_iota(jnp.int32, (8, size), 1)
    sub = lax.broadcasted_iota(jnp.int32, (8, size), 0)
    spread = lambda value: jnp.broadcast_to(value, (8, size))
    count = len(blocks)
    rows = [[value[8 * g : 8 * g + 8, :] for g in range(groups)] for value in blocks]
    done = [[] for _ in blocks]
    for g in range(groups):
        first = 8 * g
        inside = (lane >= first) & (lane < first + 8)
        unit = jnp.where(lane == sub + first, 1.0, 0.0)
        columns = [
            [spread(rows[m][g][:, first + j : first + j + 1]) for j in range(8)] for m in range(count)
        ]
        work = [jnp.where(inside, unit, rows[m][g]) for m in range(count)]
        kept = [jnp.zeros((8, size), F32) for _ in range(count)]
        for j in range(8):
            for m in range(count):
                pivot = spread(columns[m][j][j : j + 1, :])
                inverse = 1.0 / pivot
                root = lax.rsqrt(pivot)
                root = root * (1.5 - 0.5 * pivot * root * root)
                mine = sub == j
                for k in range(j + 1, 8):
                    scaled = spread(columns[m][k][j : j + 1, :]) * inverse
                    columns[m][k] = jnp.where(mine, scaled, columns[m][k] - columns[m][j] * scaled)
                row = spread(work[m][j : j + 1, :])
                kept[m] = jnp.where(mine, row * root, kept[m])
                scaled = row * inverse
                work[m] = jnp.where(mine, scaled, work[m] - columns[m][j] * scaled)
        for m in range(count):
            done[m].append(jnp.where(lane < first + 8, kept[m], 0.0))
            pivots = [spread(work[m][j : j + 1, :]) for j in range(8)]
            for i in range(g + 1, groups):
                old = rows[m][i]
                new = jnp.where(inside, 0.0, old)
                for j in range(8):
                    new = new - spread(old[:, first + j : first + j + 1]) * pivots[j]
                rows[m][i] = new
    return [jnp.concatenate(values, 0) for values in done]


def dot_last(left, right):
    return lax.dot_general(
        left, right, (((1,), (1,)), ((), ())), preferred_element_type=F32, precision=HIGHEST
    )


def reduced_system(inverse_count, place, pack, index):
    snaps = pack.shape[2]
    share = snaps // PARTS
    half = snaps // 2
    order = [piece_at(place ^ c) for c in range(PARTS)]
    packed = jnp.concatenate([pack[at, :share, :] for at in order], 0) * inverse_count
    cross = jnp.concatenate([pack[at, share : 2 * share, :] for at in order], 0) * inverse_count
    load = pack[0, 2 * share : 2 * share + 1, :] * inverse_count
    diagonal = pack[0, 2 * share + 1 : 2 * share + 2, :] * inverse_count
    row = lax.broadcasted_iota(jnp.int32, (snaps, snaps), 0)
    column = lax.broadcasted_iota(jnp.int32, (snaps, snaps), 1)
    turned = packed.T
    gram = jnp.where(row <= column, packed, turned)
    square = jnp.where(row > column, packed, jnp.where(row == column, diagonal, turned))
    project = gram + cross.T
    normal = project + cross + square

    pair = (gram, normal)
    upper = inverse_factors([value[:half, :half] for value in pair])
    below = [dot_last(value[half:, :half], inv) for value, inv in zip(pair, upper)]
    rest = [value[half:, half:] - dot_last(low, low) for value, low in zip(pair, below)]
    lower = inverse_factors(rest)
    inverses = []
    for top, low, bottom in zip(upper, below, lower):
        corner = -matmul(bottom, matmul(low, top, HIGHEST), HIGHEST)
        inverses.append(
            jnp.concatenate(
                [
                    jnp.concatenate([top, jnp.zeros((half, half), F32)], 1),
                    jnp.concatenate([corner, bottom], 1),
                ],
                0,
            )
        )
    gram_inverse, normal_inverse = inverses
    root = gram_inverse.T

    across = lambda matrix, vector: jnp.sum(matrix * vector, 1, keepdims=True)
    down = lambda matrix, vector: jnp.sum(matrix * vector, 0, keepdims=True)
    state = jnp.where(index == jnp.max(index), 1.0, 0.0)
    eye = jnp.where(row == column, 1.0, 0.0)
    history = []
    for _ in range(STEPS):
        old = state
        right = down(eye, across(project, state)) + STEP_SIZE * load
        state = down(normal_inverse, across(normal_inverse, right))
        history.append(down(root, across(gram, state)))
    return root, history, state - old, state


def final_kernel(
    inverse_count,
    place_ref,
    low_ref,
    high_ref,
    index_ref,
    force_ref,
    snap,
    image,
    basis_any,
    coeff_ref,
    residual_ref,
    pack,
    root_ref,
    change_ref,
    state_ref,
    tile,
    basis,
    sems,
):
    rows, snaps = snap.shape
    block = force_ref.shape[1]
    chunks = rows // CHUNK
    per_chunk = CHUNK // block

    def chunk(i):
        return pl.ds(pl.multiple_of(i * CHUNK, CHUNK), CHUNK)

    def out_copy(i):
        return pltpu.make_async_copy(basis.at[chunk(i), :], basis_any.at[chunk(i), :], sems.at[i])

    pack[: PARTS // 2] = low_ref[...]
    pack[PARTS // 2 :] = high_ref[...]
    root, history, change, state = reduced_system(inverse_count, place_ref[0], pack, index_ref[...])
    high, low = split(root)
    root_ref[:, :snaps] = high
    root_ref[:, snaps:] = low
    for n in range(STEPS):
        coeff_ref[n : n + 1, :] = history[n]
    change_ref[...] = change
    state_ref[...] = state
    tile[...] = jnp.zeros_like(tile)
    lane = lax.broadcasted_iota(jnp.int32, (block, block), 1)

    @pl.loop(0, chunks)
    def _(i):
        at = chunk(i)
        panel = snap[at, :]
        sums = jnp.sum(panel * change_ref[...] + image[at, :] * state_ref[...], 1, keepdims=True)
        gathered = tile[...]
        for k in range(per_chunk):
            gathered = jnp.where(lane == i * per_chunk + k, sums[k * block : (k + 1) * block], gathered)
        tile[...] = gathered
        panel_high, panel_low = split(panel)
        both = matmul(panel_high, root_ref[...])
        basis[at, :] = both[:, :snaps] + both[:, snaps:] + matmul(panel_low, root_ref[:, :snaps])
        out_copy(i).start()

    residual_ref[...] = tile[...].T[: rows // block] - STEP_SIZE * force_ref[...]

    @pl.loop(0, chunks)
    def _(i):
        out_copy(i).wait()


def final_call(pieces, step_index, place, snapshots, image, force, inverse_count):
    rows, snaps = snapshots.shape
    block = force.shape[1]
    share = snaps // PARTS
    vmem = pl.BlockSpec(memory_space=pltpu.VMEM)
    hbm = pl.BlockSpec(memory_space=pl.ANY)
    return pl.pallas_call(
        functools.partial(final_kernel, inverse_count),
        out_shape=(
            jax.ShapeDtypeStruct((rows, snaps), F32),
            jax.ShapeDtypeStruct((STEPS, snaps), F32),
            jax.ShapeDtypeStruct(force.shape, F32),
        ),
        in_specs=[pl.BlockSpec(memory_space=pltpu.SMEM)] + [vmem] * 6,
        out_specs=[hbm, vmem, vmem],
        scratch_shapes=[
            pltpu.VMEM((PARTS, 2 * share + 8, snaps), F32),
            pltpu.VMEM((snaps, 2 * snaps), BF16),
            pltpu.VMEM((1, snaps), F32),
            pltpu.VMEM((1, snaps), F32),
            pltpu.VMEM((block, block), F32),
            pltpu.VMEM((rows, snaps), F32),
            pltpu.SemaphoreType.DMA((rows // CHUNK,)),
        ],
        compiler_params=pltpu.CompilerParams(vmem_limit_bytes=18 * MIB),
        name="final",
    )(place, *pieces, step_index, force, snapshots, image)


def shifted(value, axis, steps):
    count = lax.axis_size(axis)
    pairs = [(source, (source + steps) % count) for source in range(count)]
    return lax.ppermute(value, axis, pairs)


def from_behind(shard, axis, by):
    devices = lax.axis_size(axis)
    pairs = [(i, i + by) for i in range(devices) if 0 <= i + by < devices]
    return lax.ppermute(shard, axis, pairs)


def partner(value, axis, bit):
    count = lax.axis_size(axis)
    return lax.ppermute(value, axis, [(i, i ^ bit) for i in range(count)])


def reduce_packed(keep, send):
    core, x, y = ("zone", 1), ("zone", 2), ("rows", 1)
    value = keep + partner(send, *core)
    for way in (x, y):
        half = value.shape[0] // 2
        value = value[:half] + partner(value[half:], *way)
    for axis, bit in (("rows", 2), ("zone", 4)):
        while bit < lax.axis_size(axis):
            value = value + partner(value, axis, bit)
            bit *= 2
    for way in (y, x):
        value = jnp.concatenate([value, partner(value, *way)], 0)
    return value, partner(value, *core)


def shards(snapshots, tangent, pattern, forcing, step_index):
    rows, snaps = snapshots.shape
    blocks = pattern.shape[0]
    block = rows // blocks
    edge = HALO * block
    inverse_count = 1.0 / (rows * lax.axis_size("rows") * lax.axis_size("zone"))
    place = (lax.axis_index("zone") & 3) | ((lax.axis_index("rows") & 1) << 2)
    place = jnp.reshape(place, (1,)).astype(jnp.int32)
    force = forcing.reshape(blocks, block)
    head, tail = snapshots[:edge], snapshots[rows - edge :]
    rows_prev = shifted(tail, "rows", 1)
    rows_next = shifted(head, "rows", -1)
    field, turned, gram, load = gram_call(snapshots, force)
    halos = (from_behind(tail, "zone", 1), from_behind(head, "zone", -1), rows_prev, rows_next)
    image, *packed = tangent_call(field, turned, halos, tangent, pattern, force, gram, load, place)
    pieces = reduce_packed(*packed)
    basis, coefficients, residual = final_call(
        pieces, step_index.reshape(1, snaps), place, snapshots, image, force, inverse_count
    )
    return basis, coefficients, residual.reshape(rows)


def solution(mesh):
    in_specs = (
        P(("rows", "zone"), None),
        P(("rows", "zone"), None),
        P(("rows", "zone"), None),
        P(("rows", "zone")),
        P(),
    )
    out_specs = (P(("rows", "zone"), None), P(), P(("rows", "zone")))
    return jax.shard_map(shards, mesh=mesh, in_specs=in_specs, out_specs=out_specs, check_vma=False)
```

```python
import functools

import jax
import jax.numpy as jnp
from jax import lax
from jax.experimental import pallas as pl
from jax.experimental.pallas import tpu as pltpu
from jax.sharding import PartitionSpec as P

HALO = 4
STEPS = 3
STEP_SIZE = 0.25
CHUNK = 1024
MIB = 1024 * 1024
PARTS = 8
F32 = jnp.float32
BF16 = jnp.bfloat16
HIGHEST = lax.Precision.HIGHEST


def split(value):
    high = value.astype(BF16)
    low = (value - high.astype(F32)).astype(BF16)
    return high, low


def contract_rows(left, right):
    return lax.dot_general(left, right, (((0,), (0,)), ((), ())), preferred_element_type=F32)


def matmul(left, right, precision=None):
    return lax.dot_general(
        left, right, (((1,), (0,)), ((), ())), preferred_element_type=F32, precision=precision
    )


def piece_at(position):
    return ((position >> 2) & 1) | (position & 2) | ((position & 1) << 2)


def force_product(panel, force):
    columns = force.T
    block = force.shape[1]
    total = jnp.zeros((1, panel.shape[1]), F32)
    for k in range(force.shape[0]):
        total += jnp.sum(panel[k * block : (k + 1) * block] * columns[:, k : k + 1], 0, keepdims=True)
    return total


def gram_kernel(snap_ref, force_ref, field_ref, turned_ref, gram_ref, load_ref):
    rows = snap_ref.shape[0]
    per_chunk = CHUNK // force_ref.shape[1]
    gram_ref[...] = jnp.zeros_like(gram_ref)
    load_ref[...] = jnp.zeros_like(load_ref)

    @pl.loop(0, rows // CHUNK)
    def _(i):
        at = pl.ds(pl.multiple_of(i * CHUNK, CHUNK), CHUNK)
        panel = snap_ref[at, :]
        snaps = panel.shape[1]
        high, low = split(panel)
        turned = high.T
        field_ref[at, :snaps] = high
        field_ref[at, snaps:] = low
        turned_ref[i, :snaps, :] = turned
        turned_ref[i, snaps:, :] = low.T
        gram_ref[...] += matmul(turned, jnp.concatenate([high, low], 1))
        line = pl.ds(pl.multiple_of(i * per_chunk, per_chunk), per_chunk)
        load_ref[...] += force_product(panel, force_ref[line, :])


def gram_call(snapshots, force):
    rows, snaps = snapshots.shape
    vmem = pl.BlockSpec(memory_space=pltpu.VMEM)
    return pl.pallas_call(
        gram_kernel,
        out_shape=(
            jax.ShapeDtypeStruct((rows, 2 * snaps), BF16),
            jax.ShapeDtypeStruct((rows // CHUNK, 2 * snaps, CHUNK), BF16),
            jax.ShapeDtypeStruct((snaps, 2 * snaps), F32),
            jax.ShapeDtypeStruct((1, snaps), F32),
        ),
        in_specs=[vmem, vmem],
        out_specs=[vmem] * 4,
        compiler_params=pltpu.CompilerParams(vmem_limit_bytes=10 * MIB),
        cost_estimate=pl.CostEstimate(
            flops=4 * rows * snaps * snaps, bytes_accessed=4 * rows * snaps, transcendentals=0
        ),
        name="gram",
    )(snapshots, force)


def tangent_kernel(
    pattern_ref,
    place_ref,
    field,
    turned,
    left_ref,
    right_ref,
    prev_ref,
    next_ref,
    tangent_any,
    force_ref,
    gram_ref,
    load_ref,
    image,
    keep_ref,
    send_ref,
    halo,
    mixed,
    rest,
    load,
    packed,
    tangent,
    sems,
):
    rows, snaps = image.shape
    block_count, coupled = pattern_ref.shape
    block = rows // block_count
    edge = HALO * block
    chunks = rows // CHUNK
    per_chunk = CHUNK // block

    def tangent_copy(i):
        at = pl.ds(pl.multiple_of(i * CHUNK, CHUNK), CHUNK)
        return pltpu.make_async_copy(tangent_any.at[at, :], tangent.at[at, :], sems.at[i])

    for i in range(chunks):
        tangent_copy(i).start()

    for i, ref in enumerate((left_ref, right_ref, prev_ref, next_ref)):
        high, low = split(ref[...])
        at = pl.ds(i * edge, edge)
        halo[at, :snaps] = high
        halo[at, snaps:] = low
    mixed[...] = jnp.zeros_like(mixed)
    rest[...] = jnp.zeros_like(rest)
    load[...] = load_ref[...]

    @pl.loop(0, chunks)
    def _(step):
        start = pl.multiple_of(step * CHUNK, CHUNK)
        tangent_copy(step).wait()
        images = []
        for k in range(per_chunk):
            g = step * per_chunk + k
            picked = []
            for e in range(coupled):
                code = pattern_ref[g, e]
                source = lax.div(code, block_count)
                pick = lax.rem(code, block_count)
                here = source == 0
                tail = (source == 1) | (source == 3)
                beyond = ((source + 1) & 3) * HALO + jnp.where(tail, pick - (block_count - HALO), pick)
                beyond = jnp.where(here, 0, beyond)
                inner = field[pl.ds(pl.multiple_of(pick * block, block), block), :]
                outer = halo[pl.ds(pl.multiple_of(beyond * block, block), block), :]
                picked.append(lax.select(here, inner, outer))
            own = pl.ds(pl.multiple_of(start + k * block, block), block)
            both = matmul(tangent[own, :], jnp.concatenate(picked, 0))
            part = STEP_SIZE * (both[:, :snaps] + both[:, snaps:])
            image[own, :] = part
            images.append(part)
        panel = jnp.concatenate(images, 0)
        line = pl.ds(pl.multiple_of(step * per_chunk, per_chunk), per_chunk)
        load[...] += force_product(panel, force_ref[line, :])
        high, low = split(panel)
        high_turned = high.T
        panels = turned[step]
        mixed[...] += matmul(jnp.concatenate([panels, high_turned], 0), high)
        rest[...] += matmul(jnp.concatenate([panels[:snaps], high_turned], 0), low)

    gram = gram_ref[:, :snaps] + gram_ref[:, snaps:] + gram_ref[:, snaps:].T
    cross = mixed[:snaps] + mixed[snaps : 2 * snaps] + rest[:snaps]
    square = mixed[2 * snaps :] + rest[snaps:] + rest[snaps:].T
    row = lax.broadcasted_iota(jnp.int32, (snaps, snaps), 0)
    column = lax.broadcasted_iota(jnp.int32, (snaps, snaps), 1)
    diagonal = jnp.sum(jnp.where(row == column, square, 0.0), 0, keepdims=True)
    packed[0] = jnp.where(row <= column, gram, square)
    packed[1] = cross
    extra_row = lax.broadcasted_iota(jnp.int32, (8, snaps), 0)
    extra = jnp.where(extra_row == 0, load[...], jnp.where(extra_row == 1, diagonal, 0.0))
    share = snaps // PARTS
    for at in range(PARTS):
        out = keep_ref if at < PARTS // 2 else send_ref
        slot = at % (PARTS // 2)
        begin = pl.multiple_of((place_ref[0] ^ piece_at(at)) * share, 8)
        out[slot, :share, :] = packed[0, pl.ds(begin, share), :]
        out[slot, share : 2 * share, :] = packed[1, pl.ds(begin, share), :]
        out[slot, 2 * share :, :] = extra


def tangent_call(field, turned, halos, tangent, pattern, force, gram, load, place):
    rows = tangent.shape[0]
    snaps = gram.shape[0]
    share = snaps // PARTS
    edge = halos[0].shape[0]
    vmem = pl.BlockSpec(memory_space=pltpu.VMEM)
    smem = pl.BlockSpec(memory_space=pltpu.SMEM)
    packed = jax.ShapeDtypeStruct((PARTS // 2, 2 * share + 8, snaps), F32)
    return pl.pallas_call(
        tangent_kernel,
        out_shape=(jax.ShapeDtypeStruct((rows, snaps), F32), packed, packed),
        in_specs=[smem, smem] + [vmem] * 6 + [pl.BlockSpec(memory_space=pl.ANY)] + [vmem] * 3,
        out_specs=[vmem] * 3,
        scratch_shapes=[
            pltpu.VMEM((4 * edge, 2 * snaps), BF16),
            pltpu.VMEM((3 * snaps, snaps), F32),
            pltpu.VMEM((2 * snaps, snaps), F32),
            pltpu.VMEM((1, snaps), F32),
            pltpu.VMEM((2, snaps, snaps), F32),
            pltpu.VMEM(tangent.shape, BF16),
            pltpu.SemaphoreType.DMA((rows // CHUNK,)),
        ],
        compiler_params=pltpu.CompilerParams(vmem_limit_bytes=18 * MIB),
        name="tangent",
    )(pattern, place, field, turned, *halos, tangent, force, gram, load)


def reciprocal(value):
    result = pl.reciprocal(value, approx=True)
    for _ in range(2):
        result = result * (2.0 - value * result)
    return result


def inverse_factors(blocks):
    size = blocks[0].shape[0]
    groups = size // 8
    lane = lax.broadcasted_iota(jnp.int32, (8, size), 1)
    sub = lax.broadcasted_iota(jnp.int32, (8, size), 0)
    spread = lambda value: jnp.broadcast_to(value, (8, size))
    count = len(blocks)
    rows = [[value[8 * g : 8 * g + 8, :] for g in range(groups)] for value in blocks]
    done = [[] for _ in blocks]
    for g in range(groups):
        first = 8 * g
        inside = (lane >= first) & (lane < first + 8)
        unit = jnp.where(lane == sub + first, 1.0, 0.0)
        columns = [
            [spread(rows[m][g][:, first + j : first + j + 1]) for j in range(8)] for m in range(count)
        ]
        work = [jnp.where(inside, unit, rows[m][g]) for m in range(count)]
        kept = [jnp.zeros((8, size), F32) for _ in range(count)]
        pivots = [spread(columns[m][0][0:1, :]) for m in range(count)]
        for j in range(8):
            mine = sub == j
            for m in range(count):
                pivot, column = pivots[m], columns[m][j]
                inverse = reciprocal(pivot)
                tops = [spread(columns[m][k][j : j + 1, :]) for k in range(j + 1, 8)]
                if j < 7:
                    below = spread(column[j + 1 : j + 2, :]) * tops[0]
                    pivots[m] = spread(columns[m][j + 1][j + 1 : j + 2, :]) - below * inverse
                for k in range(j + 1, 8):
                    top = tops[k - j - 1]
                    step = jnp.where(mine, -top, column * top)
                    columns[m][k] = jnp.where(mine, 0.0, columns[m][k]) - step * inverse
                row = spread(work[m][j : j + 1, :])
                step = jnp.where(mine, -row, column * row)
                work[m] = jnp.where(mine, 0.0, work[m]) - step * inverse
                root = lax.rsqrt(pivot)
                root = root * (1.5 - 0.5 * pivot * root * root)
                kept[m] = jnp.where(mine, row * root, kept[m])
        for m in range(count):
            done[m].append(jnp.where(lane < first + 8, kept[m], 0.0))
            solved = [spread(work[m][j : j + 1, :]) for j in range(8)]
            for i in range(g + 1, groups):
                old = rows[m][i]
                terms = [spread(old[:, first + j : first + j + 1]) * solved[j] for j in range(8)]
                while len(terms) > 1:
                    terms = [a + b for a, b in zip(terms[::2], terms[1::2])]
                rows[m][i] = jnp.where(inside, 0.0, old) - terms[0]
    return [jnp.concatenate(values, 0) for values in done]


def dot_last(left, right):
    return lax.dot_general(
        left, right, (((1,), (1,)), ((), ())), preferred_element_type=F32, precision=HIGHEST
    )


def reduced_system(inverse_count, place, pack, index):
    snaps = pack.shape[2]
    share = snaps // PARTS
    half = snaps // 2
    order = [piece_at(place ^ c) for c in range(PARTS)]
    packed = jnp.concatenate([pack[at, :share, :] for at in order], 0) * inverse_count
    cross = jnp.concatenate([pack[at, share : 2 * share, :] for at in order], 0) * inverse_count
    load = pack[0, 2 * share : 2 * share + 1, :] * inverse_count
    diagonal = pack[0, 2 * share + 1 : 2 * share + 2, :] * inverse_count
    row = lax.broadcasted_iota(jnp.int32, (snaps, snaps), 0)
    column = lax.broadcasted_iota(jnp.int32, (snaps, snaps), 1)
    turned = packed.T
    gram = jnp.where(row <= column, packed, turned)
    square = jnp.where(row > column, packed, jnp.where(row == column, diagonal, turned))
    project = gram + cross.T
    normal = project + cross + square

    pair = (gram, normal)
    upper = inverse_factors([value[:half, :half] for value in pair])
    below = [dot_last(value[half:, :half], inv) for value, inv in zip(pair, upper)]
    rest = [value[half:, half:] - dot_last(low, low) for value, low in zip(pair, below)]
    lower = inverse_factors(rest)
    inverses = []
    for top, low, bottom in zip(upper, below, lower):
        corner = -matmul(bottom, matmul(low, top, HIGHEST), HIGHEST)
        inverses.append(
            jnp.concatenate(
                [
                    jnp.concatenate([top, jnp.zeros((half, half), F32)], 1),
                    jnp.concatenate([corner, bottom], 1),
                ],
                0,
            )
        )
    gram_inverse, normal_inverse = inverses
    root = gram_inverse.T

    across = lambda matrix, vector: jnp.sum(matrix * vector, 1, keepdims=True)
    down = lambda matrix, vector: jnp.sum(matrix * vector, 0, keepdims=True)
    state = jnp.where(index == jnp.max(index), 1.0, 0.0)
    eye = jnp.where(row == column, 1.0, 0.0)
    history = []
    for _ in range(STEPS):
        old = state
        right = down(eye, across(project, state)) + STEP_SIZE * load
        state = down(normal_inverse, across(normal_inverse, right))
        history.append(down(root, across(gram, state)))
    return root, history, state - old, state


def final_kernel(
    inverse_count,
    place_ref,
    low_ref,
    high_ref,
    index_ref,
    force_ref,
    snap,
    image,
    basis_any,
    coeff_ref,
    residual_ref,
    pack,
    root_ref,
    change_ref,
    state_ref,
    tile,
    basis,
    sems,
):
    rows, snaps = snap.shape
    block = force_ref.shape[1]
    chunks = rows // CHUNK
    per_chunk = CHUNK // block

    def chunk(i):
        return pl.ds(pl.multiple_of(i * CHUNK, CHUNK), CHUNK)

    def out_copy(i):
        return pltpu.make_async_copy(basis.at[chunk(i), :], basis_any.at[chunk(i), :], sems.at[i])

    pack[: PARTS // 2] = low_ref[...]
    pack[PARTS // 2 :] = high_ref[...]
    root, history, change, state = reduced_system(inverse_count, place_ref[0], pack, index_ref[...])
    high, low = split(root)
    root_ref[:, :snaps] = high
    root_ref[:, snaps:] = low
    for n in range(STEPS):
        coeff_ref[n : n + 1, :] = history[n]
    change_ref[...] = change
    state_ref[...] = state
    tile[...] = jnp.zeros_like(tile)
    lane = lax.broadcasted_iota(jnp.int32, (block, block), 1)

    @pl.loop(0, chunks)
    def _(i):
        at = chunk(i)
        panel = snap[at, :]
        sums = jnp.sum(panel * change_ref[...] + image[at, :] * state_ref[...], 1, keepdims=True)
        gathered = tile[...]
        for k in range(per_chunk):
            gathered = jnp.where(lane == i * per_chunk + k, sums[k * block : (k + 1) * block], gathered)
        tile[...] = gathered
        panel_high, panel_low = split(panel)
        both = matmul(panel_high, root_ref[...])
        basis[at, :] = both[:, :snaps] + both[:, snaps:] + matmul(panel_low, root_ref[:, :snaps])
        out_copy(i).start()

    residual_ref[...] = tile[...].T[: rows // block] - STEP_SIZE * force_ref[...]

    @pl.loop(0, chunks)
    def _(i):
        out_copy(i).wait()


def final_call(pieces, step_index, place, snapshots, image, force, inverse_count):
    rows, snaps = snapshots.shape
    block = force.shape[1]
    share = snaps // PARTS
    vmem = pl.BlockSpec(memory_space=pltpu.VMEM)
    hbm = pl.BlockSpec(memory_space=pl.ANY)
    return pl.pallas_call(
        functools.partial(final_kernel, inverse_count),
        out_shape=(
            jax.ShapeDtypeStruct((rows, snaps), F32),
            jax.ShapeDtypeStruct((STEPS, snaps), F32),
            jax.ShapeDtypeStruct(force.shape, F32),
        ),
        in_specs=[pl.BlockSpec(memory_space=pltpu.SMEM)] + [vmem] * 6,
        out_specs=[hbm, vmem, vmem],
        scratch_shapes=[
            pltpu.VMEM((PARTS, 2 * share + 8, snaps), F32),
            pltpu.VMEM((snaps, 2 * snaps), BF16),
            pltpu.VMEM((1, snaps), F32),
            pltpu.VMEM((1, snaps), F32),
            pltpu.VMEM((block, block), F32),
            pltpu.VMEM((rows, snaps), F32),
            pltpu.SemaphoreType.DMA((rows // CHUNK,)),
        ],
        compiler_params=pltpu.CompilerParams(vmem_limit_bytes=18 * MIB),
        name="final",
    )(place, *pieces, step_index, force, snapshots, image)


def shifted(value, axis, steps):
    count = lax.axis_size(axis)
    pairs = [(source, (source + steps) % count) for source in range(count)]
    return lax.ppermute(value, axis, pairs)


def from_behind(shard, axis, by):
    devices = lax.axis_size(axis)
    pairs = [(i, i + by) for i in range(devices) if 0 <= i + by < devices]
    return lax.ppermute(shard, axis, pairs)


def partner(value, axis, bit):
    count = lax.axis_size(axis)
    return lax.ppermute(value, axis, [(i, i ^ bit) for i in range(count)])


def across(value, line_bit, zone_bit):
    zones = lax.axis_size("zone")
    count = zones * lax.axis_size("rows")
    pairs = [(i, (i // zones ^ line_bit) * zones + (i % zones ^ zone_bit)) for i in range(count)]
    return lax.ppermute(value, ("rows", "zone"), pairs)


def reduce_packed(keep, send):
    value = keep + partner(send, "zone", 1)
    ways = ((1, 0), (0, 2), (1, 2))
    others = [across(value[at + 1 : at + 2], *way) for at, way in enumerate(ways)]
    value = value[:1] + others[0] + others[1] + others[2]
    for axis, bit in (("rows", 2), ("zone", 4)):
        while bit < lax.axis_size(axis):
            value = value + partner(value, axis, bit)
            bit *= 2
    value = jnp.concatenate([value] + [across(value, *way) for way in ways], 0)
    return value, partner(value, "zone", 1)


def shards(snapshots, tangent, pattern, forcing, step_index):
    rows, snaps = snapshots.shape
    blocks = pattern.shape[0]
    block = rows // blocks
    edge = HALO * block
    inverse_count = 1.0 / (rows * lax.axis_size("rows") * lax.axis_size("zone"))
    place = (lax.axis_index("zone") & 3) | ((lax.axis_index("rows") & 1) << 2)
    place = jnp.reshape(place, (1,)).astype(jnp.int32)
    force = forcing.reshape(blocks, block)
    head, tail = snapshots[:edge], snapshots[rows - edge :]
    rows_prev = shifted(tail, "rows", 1)
    rows_next = shifted(head, "rows", -1)
    field, turned, gram, load = gram_call(snapshots, force)
    halos = (from_behind(tail, "zone", 1), from_behind(head, "zone", -1), rows_prev, rows_next)
    image, *packed = tangent_call(field, turned, halos, tangent, pattern, force, gram, load, place)
    pieces = reduce_packed(*packed)
    basis, coefficients, residual = final_call(
        pieces, step_index.reshape(1, snaps), place, snapshots, image, force, inverse_count
    )
    return basis, coefficients, residual.reshape(rows)


def solution(mesh):
    in_specs = (
        P(("rows", "zone"), None),
        P(("rows", "zone"), None),
        P(("rows", "zone"), None),
        P(("rows", "zone")),
        P(),
    )
    out_specs = (P(("rows", "zone"), None), P(), P(("rows", "zone")))
    return jax.shard_map(shards, mesh=mesh, in_specs=in_specs, out_specs=out_specs, check_vma=False)
```

```python
import functools

import jax
import jax.numpy as jnp
from jax import lax
from jax.experimental import pallas as pl
from jax.experimental.pallas import tpu as pltpu
from jax.sharding import PartitionSpec as P

HALO = 4
STEPS = 3
STEP_SIZE = 0.25
CHUNK = 1024
MIB = 1024 * 1024
PARTS = 8
F32 = jnp.float32
BF16 = jnp.bfloat16
HIGHEST = lax.Precision.HIGHEST


def split(value):
    high = value.astype(BF16)
    low = (value - high.astype(F32)).astype(BF16)
    return high, low


def contract_rows(left, right):
    return lax.dot_general(left, right, (((0,), (0,)), ((), ())), preferred_element_type=F32)


def matmul(left, right, precision=None):
    return lax.dot_general(
        left, right, (((1,), (0,)), ((), ())), preferred_element_type=F32, precision=precision
    )


def piece_at(position):
    return ((position >> 2) & 1) | (position & 2) | ((position & 1) << 2)


def force_product(panel, force):
    columns = force.T
    block = force.shape[1]
    total = jnp.zeros((1, panel.shape[1]), F32)
    for k in range(force.shape[0]):
        total += jnp.sum(panel[k * block : (k + 1) * block] * columns[:, k : k + 1], 0, keepdims=True)
    return total


def gram_kernel(snap_ref, force_ref, field_ref, turned_ref, gram_ref, load_ref):
    rows = snap_ref.shape[0]
    per_chunk = CHUNK // force_ref.shape[1]
    gram_ref[...] = jnp.zeros_like(gram_ref)
    load_ref[...] = jnp.zeros_like(load_ref)

    @pl.loop(0, rows // CHUNK)
    def _(i):
        at = pl.ds(pl.multiple_of(i * CHUNK, CHUNK), CHUNK)
        panel = snap_ref[at, :]
        snaps = panel.shape[1]
        high, low = split(panel)
        turned = high.T
        field_ref[at, :snaps] = high
        field_ref[at, snaps:] = low
        turned_ref[i, :snaps, :] = turned
        turned_ref[i, snaps:, :] = low.T
        gram_ref[...] += matmul(turned, jnp.concatenate([high, low], 1))
        line = pl.ds(pl.multiple_of(i * per_chunk, per_chunk), per_chunk)
        load_ref[...] += force_product(panel, force_ref[line, :])


def gram_call(snapshots, force):
    rows, snaps = snapshots.shape
    vmem = pl.BlockSpec(memory_space=pltpu.VMEM)
    return pl.pallas_call(
        gram_kernel,
        out_shape=(
            jax.ShapeDtypeStruct((rows, 2 * snaps), BF16),
            jax.ShapeDtypeStruct((rows // CHUNK, 2 * snaps, CHUNK), BF16),
            jax.ShapeDtypeStruct((snaps, 2 * snaps), F32),
            jax.ShapeDtypeStruct((1, snaps), F32),
        ),
        in_specs=[vmem, vmem],
        out_specs=[vmem] * 4,
        compiler_params=pltpu.CompilerParams(vmem_limit_bytes=10 * MIB),
        cost_estimate=pl.CostEstimate(
            flops=4 * rows * snaps * snaps, bytes_accessed=4 * rows * snaps, transcendentals=0
        ),
        name="gram",
    )(snapshots, force)


def tangent_kernel(
    pattern_ref,
    place_ref,
    field,
    turned,
    left_ref,
    prev_ref,
    right_ref,
    next_ref,
    tangent_any,
    force_ref,
    gram_ref,
    load_ref,
    image,
    keep_ref,
    send_ref,
    halo,
    mixed,
    rest,
    load,
    packed,
    tangent,
    sems,
):
    rows, snaps = image.shape
    block_count, coupled = pattern_ref.shape
    block = rows // block_count
    edge = HALO * block
    chunks = rows // CHUNK
    per_chunk = CHUNK // block

    def tangent_copy(i):
        at = pl.ds(pl.multiple_of(i * CHUNK, CHUNK), CHUNK)
        return pltpu.make_async_copy(tangent_any.at[at, :], tangent.at[at, :], sems.at[i])

    for i in range(chunks):
        tangent_copy(i).start()

    for i, ref in enumerate((left_ref, right_ref, prev_ref, next_ref)):
        high, low = split(ref[...])
        at = pl.ds(i * edge, edge)
        halo[at, :snaps] = high
        halo[at, snaps:] = low
    mixed[...] = jnp.zeros_like(mixed)
    rest[...] = jnp.zeros_like(rest)
    load[...] = load_ref[...]

    @pl.loop(0, chunks)
    def _(step):
        start = pl.multiple_of(step * CHUNK, CHUNK)
        tangent_copy(step).wait()
        images = []
        for k in range(per_chunk):
            g = step * per_chunk + k
            picked = []
            for e in range(coupled):
                code = pattern_ref[g, e]
                source = lax.div(code, block_count)
                pick = lax.rem(code, block_count)
                here = source == 0
                tail = (source == 1) | (source == 3)
                beyond = ((source + 1) & 3) * HALO + jnp.where(tail, pick - (block_count - HALO), pick)
                beyond = jnp.where(here, 0, beyond)
                inner = field[pl.ds(pl.multiple_of(pick * block, block), block), :]
                outer = halo[pl.ds(pl.multiple_of(beyond * block, block), block), :]
                picked.append(lax.select(here, inner, outer))
            own = pl.ds(pl.multiple_of(start + k * block, block), block)
            both = matmul(tangent[own, :], jnp.concatenate(picked, 0))
            part = STEP_SIZE * (both[:, :snaps] + both[:, snaps:])
            image[own, :] = part
            images.append(part)
        panel = jnp.concatenate(images, 0)
        line = pl.ds(pl.multiple_of(step * per_chunk, per_chunk), per_chunk)
        load[...] += force_product(panel, force_ref[line, :])
        high, low = split(panel)
        high_turned = high.T
        panels = turned[step]
        mixed[...] += matmul(jnp.concatenate([panels, high_turned], 0), high)
        rest[...] += matmul(jnp.concatenate([panels[:snaps], high_turned], 0), low)

    gram = gram_ref[:, :snaps] + gram_ref[:, snaps:] + gram_ref[:, snaps:].T
    cross = mixed[:snaps] + mixed[snaps : 2 * snaps] + rest[:snaps]
    square = mixed[2 * snaps :] + rest[snaps:] + rest[snaps:].T
    row = lax.broadcasted_iota(jnp.int32, (snaps, snaps), 0)
    column = lax.broadcasted_iota(jnp.int32, (snaps, snaps), 1)
    diagonal = jnp.sum(jnp.where(row == column, square, 0.0), 0, keepdims=True)
    packed[0] = jnp.where(row <= column, gram, square)
    packed[1] = cross
    extra_row = lax.broadcasted_iota(jnp.int32, (8, snaps), 0)
    extra = jnp.where(extra_row == 0, load[...], jnp.where(extra_row == 1, diagonal, 0.0))
    share = snaps // PARTS
    for at in range(PARTS):
        out = keep_ref if at < PARTS // 2 else send_ref
        slot = at % (PARTS // 2)
        begin = pl.multiple_of((place_ref[0] ^ piece_at(at)) * share, 8)
        out[slot, :share, :] = packed[0, pl.ds(begin, share), :]
        out[slot, share : 2 * share, :] = packed[1, pl.ds(begin, share), :]
        out[slot, 2 * share :, :] = extra


def tangent_call(field, turned, halos, tangent, pattern, force, gram, load, place):
    rows = tangent.shape[0]
    snaps = gram.shape[0]
    share = snaps // PARTS
    edge = halos[0].shape[0]
    vmem = pl.BlockSpec(memory_space=pltpu.VMEM)
    smem = pl.BlockSpec(memory_space=pltpu.SMEM)
    packed = jax.ShapeDtypeStruct((PARTS // 2, 2 * share + 8, snaps), F32)
    return pl.pallas_call(
        tangent_kernel,
        out_shape=(jax.ShapeDtypeStruct((rows, snaps), F32), packed, packed),
        in_specs=[smem, smem] + [vmem] * 6 + [pl.BlockSpec(memory_space=pl.ANY)] + [vmem] * 3,
        out_specs=[vmem] * 3,
        scratch_shapes=[
            pltpu.VMEM((4 * edge, 2 * snaps), BF16),
            pltpu.VMEM((3 * snaps, snaps), F32),
            pltpu.VMEM((2 * snaps, snaps), F32),
            pltpu.VMEM((1, snaps), F32),
            pltpu.VMEM((2, snaps, snaps), F32),
            pltpu.VMEM(tangent.shape, BF16),
            pltpu.SemaphoreType.DMA((rows // CHUNK,)),
        ],
        compiler_params=pltpu.CompilerParams(vmem_limit_bytes=18 * MIB),
        name="tangent",
    )(pattern, place, field, turned, *halos, tangent, force, gram, load)


def inverse_factors(blocks):
    size = blocks[0].shape[0]
    groups = size // 8
    lane = lax.broadcasted_iota(jnp.int32, (8, size), 1)
    sub = lax.broadcasted_iota(jnp.int32, (8, size), 0)
    spread = lambda value: jnp.broadcast_to(value, (8, size))
    count = len(blocks)
    rows = [[value[8 * g : 8 * g + 8, :] for g in range(groups)] for value in blocks]
    done = [[] for _ in blocks]
    for g in range(groups):
        first = 8 * g
        inside = (lane >= first) & (lane < first + 8)
        unit = jnp.where(lane == sub + first, 1.0, 0.0)
        columns = [
            [spread(rows[m][g][:, first + j : first + j + 1]) for j in range(8)] for m in range(count)
        ]
        work = [jnp.where(inside, unit, rows[m][g]) for m in range(count)]
        kept = [jnp.zeros((8, size), F32) for _ in range(count)]
        for j in range(8):
            for m in range(count):
                pivot = spread(columns[m][j][j : j + 1, :])
                inverse = 1.0 / pivot
                root = lax.rsqrt(pivot)
                root = root * (1.5 - 0.5 * pivot * root * root)
                mine = sub == j
                for k in range(j + 1, 8):
                    scaled = spread(columns[m][k][j : j + 1, :]) * inverse
                    columns[m][k] = jnp.where(mine, scaled, columns[m][k] - columns[m][j] * scaled)
                row = spread(work[m][j : j + 1, :])
                kept[m] = jnp.where(mine, row * root, kept[m])
                scaled = row * inverse
                work[m] = jnp.where(mine, scaled, work[m] - columns[m][j] * scaled)
        for m in range(count):
            done[m].append(jnp.where(lane < first + 8, kept[m], 0.0))
            if g + 1 < groups:
                old = rows[m][g + 1]
                new = jnp.where(inside, 0.0, old)
                for j in range(8):
                    new = new - spread(old[:, first + j : first + j + 1]) * spread(work[m][j : j + 1, :])
                rows[m][g + 1] = new
            if g + 2 < groups:
                panel = [jnp.zeros((8, size), F32)] * groups
                panel[g] = work[m]
                old = jnp.concatenate(rows[m][g + 2 :], 0)
                wide = jnp.concatenate([inside] * (groups - g - 2), 0)
                change = matmul(jnp.where(wide, old, 0.0), jnp.concatenate(panel, 0), HIGHEST)
                new = jnp.where(wide, 0.0, old) - change
                rows[m][g + 2 :] = [new[8 * i : 8 * i + 8, :] for i in range(groups - g - 2)]
    return [jnp.concatenate(values, 0) for values in done]


def dot_last(left, right):
    return lax.dot_general(
        left, right, (((1,), (1,)), ((), ())), preferred_element_type=F32, precision=HIGHEST
    )


def reduced_system(inverse_count, place, pack, index):
    snaps = pack.shape[2]
    share = snaps // PARTS
    half = snaps // 2
    order = [piece_at(place ^ c) for c in range(PARTS)]
    packed = jnp.concatenate([pack[at, :share, :] for at in order], 0) * inverse_count
    cross = jnp.concatenate([pack[at, share : 2 * share, :] for at in order], 0) * inverse_count
    load = pack[0, 2 * share : 2 * share + 1, :] * inverse_count
    diagonal = pack[0, 2 * share + 1 : 2 * share + 2, :] * inverse_count
    row = lax.broadcasted_iota(jnp.int32, (snaps, snaps), 0)
    column = lax.broadcasted_iota(jnp.int32, (snaps, snaps), 1)
    turned = packed.T
    gram = jnp.where(row <= column, packed, turned)
    square = jnp.where(row > column, packed, jnp.where(row == column, diagonal, turned))
    project = gram + cross.T
    normal = project + cross + square

    pair = (gram, normal)
    upper = inverse_factors([value[:half, :half] for value in pair])
    below = [dot_last(value[half:, :half], inv) for value, inv in zip(pair, upper)]
    rest = [value[half:, half:] - dot_last(low, low) for value, low in zip(pair, below)]
    lower = inverse_factors(rest)
    inverses = []
    for top, low, bottom in zip(upper, below, lower):
        corner = -matmul(bottom, matmul(low, top, HIGHEST), HIGHEST)
        inverses.append(
            jnp.concatenate(
                [
                    jnp.concatenate([top, jnp.zeros((half, half), F32)], 1),
                    jnp.concatenate([corner, bottom], 1),
                ],
                0,
            )
        )
    gram_inverse, normal_inverse = inverses
    root = gram_inverse.T

    across = lambda matrix, vector: jnp.sum(matrix * vector, 1, keepdims=True)
    down = lambda matrix, vector: jnp.sum(matrix * vector, 0, keepdims=True)
    state = jnp.where(index == jnp.max(index), 1.0, 0.0)
    eye = jnp.where(row == column, 1.0, 0.0)
    history = []
    for _ in range(STEPS):
        old = state
        right = down(eye, across(project, state)) + STEP_SIZE * load
        state = down(normal_inverse, across(normal_inverse, right))
        history.append(down(root, across(gram, state)))
    return root, history, state - old, state


def final_kernel(
    inverse_count,
    place_ref,
    low_ref,
    high_ref,
    index_ref,
    force_ref,
    snap,
    image,
    basis_any,
    coeff_ref,
    residual_ref,
    pack,
    root_ref,
    change_ref,
    state_ref,
    tile,
    basis,
    sems,
):
    rows, snaps = snap.shape
    block = force_ref.shape[1]
    chunks = rows // CHUNK
    per_chunk = CHUNK // block

    def chunk(i):
        return pl.ds(pl.multiple_of(i * CHUNK, CHUNK), CHUNK)

    def out_copy(i):
        return pltpu.make_async_copy(basis.at[chunk(i), :], basis_any.at[chunk(i), :], sems.at[i])

    pack[: PARTS // 2] = low_ref[...]
    pack[PARTS // 2 :] = high_ref[...]
    root, history, change, state = reduced_system(inverse_count, place_ref[0], pack, index_ref[...])
    high, low = split(root)
    root_ref[:, :snaps] = high
    root_ref[:, snaps:] = low
    for n in range(STEPS):
        coeff_ref[n : n + 1, :] = history[n]
    change_ref[...] = change
    state_ref[...] = state
    tile[...] = jnp.zeros_like(tile)
    lane = lax.broadcasted_iota(jnp.int32, (block, block), 1)

    @pl.loop(0, chunks)
    def _(i):
        at = chunk(i)
        panel = snap[at, :]
        sums = jnp.sum(panel * change_ref[...] + image[at, :] * state_ref[...], 1, keepdims=True)
        gathered = tile[...]
        for k in range(per_chunk):
            gathered = jnp.where(lane == i * per_chunk + k, sums[k * block : (k + 1) * block], gathered)
        tile[...] = gathered
        panel_high, panel_low = split(panel)
        both = matmul(panel_high, root_ref[...])
        basis[at, :] = both[:, :snaps] + both[:, snaps:] + matmul(panel_low, root_ref[:, :snaps])
        out_copy(i).start()

    residual_ref[...] = tile[...].T[: rows // block] - STEP_SIZE * force_ref[...]

    @pl.loop(0, chunks)
    def _(i):
        out_copy(i).wait()


def final_call(pieces, step_index, place, snapshots, image, force, inverse_count):
    rows, snaps = snapshots.shape
    block = force.shape[1]
    share = snaps // PARTS
    vmem = pl.BlockSpec(memory_space=pltpu.VMEM)
    hbm = pl.BlockSpec(memory_space=pl.ANY)
    return pl.pallas_call(
        functools.partial(final_kernel, inverse_count),
        out_shape=(
            jax.ShapeDtypeStruct((rows, snaps), F32),
            jax.ShapeDtypeStruct((STEPS, snaps), F32),
            jax.ShapeDtypeStruct(force.shape, F32),
        ),
        in_specs=[pl.BlockSpec(memory_space=pltpu.SMEM)] + [vmem] * 6,
        out_specs=[hbm, vmem, vmem],
        scratch_shapes=[
            pltpu.VMEM((PARTS, 2 * share + 8, snaps), F32),
            pltpu.VMEM((snaps, 2 * snaps), BF16),
            pltpu.VMEM((1, snaps), F32),
            pltpu.VMEM((1, snaps), F32),
            pltpu.VMEM((block, block), F32),
            pltpu.VMEM((rows, snaps), F32),
            pltpu.SemaphoreType.DMA((rows // CHUNK,)),
        ],
        compiler_params=pltpu.CompilerParams(vmem_limit_bytes=18 * MIB),
        name="final",
    )(place, *pieces, step_index, force, snapshots, image)


def shifted(value, axis, steps):
    count = lax.axis_size(axis)
    pairs = [(source, (source + steps) % count) for source in range(count)]
    return lax.ppermute(value, axis, pairs)


def from_behind(shard, axis, by):
    devices = lax.axis_size(axis)
    pairs = [(i, i + by) for i in range(devices) if 0 <= i + by < devices]
    return lax.ppermute(shard, axis, pairs)


def partner(value, axis, bit):
    count = lax.axis_size(axis)
    return lax.ppermute(value, axis, [(i, i ^ bit) for i in range(count)])


def across(value, line_bit, zone_bit):
    zones = lax.axis_size("zone")
    count = zones * lax.axis_size("rows")
    pairs = [(i, (i // zones ^ line_bit) * zones + (i % zones ^ zone_bit)) for i in range(count)]
    return lax.ppermute(value, ("rows", "zone"), pairs)


def reduce_packed(keep, send):
    value = keep + partner(send, "zone", 1)
    ways = ((1, 0), (0, 2), (1, 2))
    others = [across(value[at + 1 : at + 2], *way) for at, way in enumerate(ways)]
    value = value[:1] + others[0] + others[1] + others[2]
    for axis, bit in (("rows", 2), ("zone", 4)):
        while bit < lax.axis_size(axis):
            value = value + partner(value, axis, bit)
            bit *= 2
    value = jnp.concatenate([value] + [across(value, *way) for way in ways], 0)
    return value, partner(value, "zone", 1)


def shards(snapshots, tangent, pattern, forcing, step_index):
    rows, snaps = snapshots.shape
    blocks = pattern.shape[0]
    block = rows // blocks
    edge = HALO * block
    inverse_count = 1.0 / (rows * lax.axis_size("rows") * lax.axis_size("zone"))
    place = (lax.axis_index("zone") & 3) | ((lax.axis_index("rows") & 1) << 2)
    place = jnp.reshape(place, (1,)).astype(jnp.int32)
    force = forcing.reshape(blocks, block)
    head, tail = snapshots[:edge], snapshots[rows - edge :]
    rows_prev = shifted(tail, "rows", 1)
    rows_next = shifted(head, "rows", -1)
    field, turned, gram, load = gram_call(snapshots, force)
    halos = (from_behind(tail, "zone", 1), rows_prev, from_behind(head, "zone", -1), rows_next)
    image, *packed = tangent_call(field, turned, halos, tangent, pattern, force, gram, load, place)
    pieces = reduce_packed(*packed)
    basis, coefficients, residual = final_call(
        pieces, step_index.reshape(1, snaps), place, snapshots, image, force, inverse_count
    )
    return basis, coefficients, residual.reshape(rows)


def solution(mesh):
    in_specs = (
        P(("rows", "zone"), None),
        P(("rows", "zone"), None),
        P(("rows", "zone"), None),
        P(("rows", "zone")),
        P(),
    )
    out_specs = (P(("rows", "zone"), None), P(), P(("rows", "zone")))
    return jax.shard_map(shards, mesh=mesh, in_specs=in_specs, out_specs=out_specs, check_vma=False)
```

```python
import functools

import jax
import jax.numpy as jnp
from jax import lax
from jax.experimental import pallas as pl
from jax.experimental.pallas import tpu as pltpu
from jax.sharding import PartitionSpec as P

HALO = 4
STEPS = 3
STEP_SIZE = 0.25
CHUNK = 1024
MIB = 1024 * 1024
PARTS = 8
F32 = jnp.float32
BF16 = jnp.bfloat16
HIGHEST = lax.Precision.HIGHEST


def split(value):
    high = value.astype(BF16)
    low = (value - high.astype(F32)).astype(BF16)
    return high, low


def contract_rows(left, right):
    return lax.dot_general(left, right, (((0,), (0,)), ((), ())), preferred_element_type=F32)


def matmul(left, right, precision=None):
    return lax.dot_general(
        left, right, (((1,), (0,)), ((), ())), preferred_element_type=F32, precision=precision
    )


def piece_at(position):
    return ((position >> 2) & 1) | (position & 2) | ((position & 1) << 2)


def force_product(panel, force):
    columns = force.T
    block = force.shape[1]
    total = jnp.zeros((1, panel.shape[1]), F32)
    for k in range(force.shape[0]):
        total += jnp.sum(panel[k * block : (k + 1) * block] * columns[:, k : k + 1], 0, keepdims=True)
    return total


def gram_kernel(snap_ref, force_ref, field_ref, turned_ref, gram_ref, load_ref):
    rows = snap_ref.shape[0]
    per_chunk = CHUNK // force_ref.shape[1]
    gram_ref[...] = jnp.zeros_like(gram_ref)
    load_ref[...] = jnp.zeros_like(load_ref)

    @pl.loop(0, rows // CHUNK)
    def _(i):
        at = pl.ds(pl.multiple_of(i * CHUNK, CHUNK), CHUNK)
        panel = snap_ref[at, :]
        snaps = panel.shape[1]
        high, low = split(panel)
        turned = high.T
        field_ref[at, :snaps] = high
        field_ref[at, snaps:] = low
        turned_ref[i, :snaps, :] = turned
        turned_ref[i, snaps:, :] = low.T
        gram_ref[...] += matmul(turned, jnp.concatenate([high, low], 1))
        line = pl.ds(pl.multiple_of(i * per_chunk, per_chunk), per_chunk)
        load_ref[...] += force_product(panel, force_ref[line, :])


def gram_call(snapshots, force):
    rows, snaps = snapshots.shape
    vmem = pl.BlockSpec(memory_space=pltpu.VMEM)
    return pl.pallas_call(
        gram_kernel,
        out_shape=(
            jax.ShapeDtypeStruct((rows, 2 * snaps), BF16),
            jax.ShapeDtypeStruct((rows // CHUNK, 2 * snaps, CHUNK), BF16),
            jax.ShapeDtypeStruct((snaps, 2 * snaps), F32),
            jax.ShapeDtypeStruct((1, snaps), F32),
        ),
        in_specs=[vmem, vmem],
        out_specs=[vmem] * 4,
        compiler_params=pltpu.CompilerParams(vmem_limit_bytes=10 * MIB),
        cost_estimate=pl.CostEstimate(
            flops=4 * rows * snaps * snaps, bytes_accessed=4 * rows * snaps, transcendentals=0
        ),
        name="gram",
    )(snapshots, force)


def tangent_kernel(
    pattern_ref,
    place_ref,
    field,
    turned,
    left_ref,
    prev_ref,
    right_ref,
    next_ref,
    tangent_any,
    force_ref,
    gram_ref,
    load_ref,
    image,
    keep_ref,
    send_ref,
    halo,
    mixed,
    rest,
    load,
    packed,
    tangent,
    sems,
):
    rows, snaps = image.shape
    block_count, coupled = pattern_ref.shape
    block = rows // block_count
    edge = HALO * block
    chunks = rows // CHUNK
    per_chunk = CHUNK // block

    def tangent_copy(i):
        at = pl.ds(pl.multiple_of(i * CHUNK, CHUNK), CHUNK)
        return pltpu.make_async_copy(tangent_any.at[at, :], tangent.at[at, :], sems.at[i])

    for i in range(chunks):
        tangent_copy(i).start()

    for i, ref in enumerate((left_ref, right_ref, prev_ref, next_ref)):
        high, low = split(ref[...])
        at = pl.ds(i * edge, edge)
        halo[at, :snaps] = high
        halo[at, snaps:] = low
    mixed[...] = jnp.zeros_like(mixed)
    rest[...] = jnp.zeros_like(rest)
    load[...] = load_ref[...]

    @pl.loop(0, chunks)
    def _(step):
        start = pl.multiple_of(step * CHUNK, CHUNK)
        tangent_copy(step).wait()
        images = []
        for k in range(per_chunk):
            g = step * per_chunk + k
            picked = []
            for e in range(coupled):
                code = pattern_ref[g, e]
                source = lax.div(code, block_count)
                pick = lax.rem(code, block_count)
                here = source == 0
                tail = (source == 1) | (source == 3)
                beyond = ((source + 1) & 3) * HALO + jnp.where(tail, pick - (block_count - HALO), pick)
                beyond = jnp.where(here, 0, beyond)
                inner = field[pl.ds(pl.multiple_of(pick * block, block), block), :]
                outer = halo[pl.ds(pl.multiple_of(beyond * block, block), block), :]
                picked.append(lax.select(here, inner, outer))
            own = pl.ds(pl.multiple_of(start + k * block, block), block)
            both = matmul(tangent[own, :], jnp.concatenate(picked, 0))
            part = STEP_SIZE * (both[:, :snaps] + both[:, snaps:])
            image[own, :] = part
            images.append(part)
        panel = jnp.concatenate(images, 0)
        line = pl.ds(pl.multiple_of(step * per_chunk, per_chunk), per_chunk)
        load[...] += force_product(panel, force_ref[line, :])
        high, low = split(panel)
        high_turned = high.T
        panels = turned[step]
        mixed[...] += matmul(jnp.concatenate([panels, high_turned], 0), high)
        rest[...] += matmul(jnp.concatenate([panels[:snaps], high_turned], 0), low)

    gram = gram_ref[:, :snaps] + gram_ref[:, snaps:] + gram_ref[:, snaps:].T
    cross = mixed[:snaps] + mixed[snaps : 2 * snaps] + rest[:snaps]
    square = mixed[2 * snaps :] + rest[snaps:] + rest[snaps:].T
    row = lax.broadcasted_iota(jnp.int32, (snaps, snaps), 0)
    column = lax.broadcasted_iota(jnp.int32, (snaps, snaps), 1)
    diagonal = jnp.sum(jnp.where(row == column, square, 0.0), 0, keepdims=True)
    packed[0] = jnp.where(row <= column, gram, square)
    packed[1] = cross
    extra_row = lax.broadcasted_iota(jnp.int32, (8, snaps), 0)
    extra = jnp.where(extra_row == 0, load[...], jnp.where(extra_row == 1, diagonal, 0.0))
    share = snaps // PARTS
    for at in range(PARTS):
        out = keep_ref if at < PARTS // 2 else send_ref
        slot = at % (PARTS // 2)
        begin = pl.multiple_of((place_ref[0] ^ piece_at(at)) * share, 8)
        out[slot, :share, :] = packed[0, pl.ds(begin, share), :]
        out[slot, share : 2 * share, :] = packed[1, pl.ds(begin, share), :]
        out[slot, 2 * share :, :] = extra


def tangent_call(field, turned, halos, tangent, pattern, force, gram, load, place):
    rows = tangent.shape[0]
    snaps = gram.shape[0]
    share = snaps // PARTS
    edge = halos[0].shape[0]
    vmem = pl.BlockSpec(memory_space=pltpu.VMEM)
    smem = pl.BlockSpec(memory_space=pltpu.SMEM)
    packed = jax.ShapeDtypeStruct((PARTS // 2, 2 * share + 8, snaps), F32)
    return pl.pallas_call(
        tangent_kernel,
        out_shape=(jax.ShapeDtypeStruct((rows, snaps), F32), packed, packed),
        in_specs=[smem, smem] + [vmem] * 6 + [pl.BlockSpec(memory_space=pl.ANY)] + [vmem] * 3,
        out_specs=[vmem] * 3,
        scratch_shapes=[
            pltpu.VMEM((4 * edge, 2 * snaps), BF16),
            pltpu.VMEM((3 * snaps, snaps), F32),
            pltpu.VMEM((2 * snaps, snaps), F32),
            pltpu.VMEM((1, snaps), F32),
            pltpu.VMEM((2, snaps, snaps), F32),
            pltpu.VMEM(tangent.shape, BF16),
            pltpu.SemaphoreType.DMA((rows // CHUNK,)),
        ],
        compiler_params=pltpu.CompilerParams(vmem_limit_bytes=18 * MIB),
        name="tangent",
    )(pattern, place, field, turned, *halos, tangent, force, gram, load)


def reciprocal(value):
    result = pl.reciprocal(value, approx=True)
    for _ in range(2):
        result = result * (2.0 - value * result)
    return result


def inverse_factors(blocks):
    size = blocks[0].shape[0]
    groups = size // 8
    lane = lax.broadcasted_iota(jnp.int32, (8, size), 1)
    sub = lax.broadcasted_iota(jnp.int32, (8, size), 0)
    spread = lambda value: jnp.broadcast_to(value, (8, size))
    count = len(blocks)
    rows = [[value[8 * g : 8 * g + 8, :] for g in range(groups)] for value in blocks]
    done = [[] for _ in blocks]
    for g in range(groups):
        first = 8 * g
        inside = (lane >= first) & (lane < first + 8)
        unit = jnp.where(lane == sub + first, 1.0, 0.0)
        columns = [
            [spread(rows[m][g][:, first + j : first + j + 1]) for j in range(8)] for m in range(count)
        ]
        work = [jnp.where(inside, unit, rows[m][g]) for m in range(count)]
        kept = [jnp.zeros((8, size), F32) for _ in range(count)]
        pivots = [spread(columns[m][0][0:1, :]) for m in range(count)]
        for j in range(8):
            mine = sub == j
            for m in range(count):
                pivot, column = pivots[m], columns[m][j]
                inverse = reciprocal(pivot)
                tops = [spread(columns[m][k][j : j + 1, :]) for k in range(j + 1, 8)]
                if j < 7:
                    below = spread(column[j + 1 : j + 2, :]) * tops[0]
                    pivots[m] = spread(columns[m][j + 1][j + 1 : j + 2, :]) - below * inverse
                for k in range(j + 1, 8):
                    top = tops[k - j - 1]
                    step = jnp.where(mine, -top, column * top)
                    columns[m][k] = jnp.where(mine, 0.0, columns[m][k]) - step * inverse
                row = spread(work[m][j : j + 1, :])
                step = jnp.where(mine, -row, column * row)
                work[m] = jnp.where(mine, 0.0, work[m]) - step * inverse
                root = lax.rsqrt(pivot)
                root = root * (1.5 - 0.5 * pivot * root * root)
                kept[m] = jnp.where(mine, row * root, kept[m])
        for m in range(count):
            done[m].append(jnp.where(lane < first + 8, kept[m], 0.0))
            if g + 1 < groups:
                old = rows[m][g + 1]
                new = jnp.where(inside, 0.0, old)
                for j in range(8):
                    new = new - spread(old[:, first + j : first + j + 1]) * spread(work[m][j : j + 1, :])
                rows[m][g + 1] = new
            if g + 2 < groups:
                panel = [jnp.zeros((8, size), F32)] * groups
                panel[g] = work[m]
                old = jnp.concatenate(rows[m][g + 2 :], 0)
                wide = jnp.concatenate([inside] * (groups - g - 2), 0)
                change = matmul(jnp.where(wide, old, 0.0), jnp.concatenate(panel, 0), HIGHEST)
                new = jnp.where(wide, 0.0, old) - change
                rows[m][g + 2 :] = [new[8 * i : 8 * i + 8, :] for i in range(groups - g - 2)]
    return [jnp.concatenate(values, 0) for values in done]


def dot_last(left, right):
    return lax.dot_general(
        left, right, (((1,), (1,)), ((), ())), preferred_element_type=F32, precision=HIGHEST
    )


def reduced_system(inverse_count, place, pack, index):
    snaps = pack.shape[2]
    share = snaps // PARTS
    half = snaps // 2
    order = [piece_at(place ^ c) for c in range(PARTS)]
    packed = jnp.concatenate([pack[at, :share, :] for at in order], 0) * inverse_count
    cross = jnp.concatenate([pack[at, share : 2 * share, :] for at in order], 0) * inverse_count
    load = pack[0, 2 * share : 2 * share + 1, :] * inverse_count
    diagonal = pack[0, 2 * share + 1 : 2 * share + 2, :] * inverse_count
    row = lax.broadcasted_iota(jnp.int32, (snaps, snaps), 0)
    column = lax.broadcasted_iota(jnp.int32, (snaps, snaps), 1)
    turned = packed.T
    gram = jnp.where(row <= column, packed, turned)
    square = jnp.where(row > column, packed, jnp.where(row == column, diagonal, turned))
    project = gram + cross.T
    normal = project + cross + square

    pair = (gram, normal)
    upper = inverse_factors([value[:half, :half] for value in pair])
    below = [dot_last(value[half:, :half], inv) for value, inv in zip(pair, upper)]
    rest = [value[half:, half:] - dot_last(low, low) for value, low in zip(pair, below)]
    lower = inverse_factors(rest)
    inverses = []
    for top, low, bottom in zip(upper, below, lower):
        corner = -matmul(bottom, matmul(low, top, HIGHEST), HIGHEST)
        inverses.append(
            jnp.concatenate(
                [
                    jnp.concatenate([top, jnp.zeros((half, half), F32)], 1),
                    jnp.concatenate([corner, bottom], 1),
                ],
                0,
            )
        )
    gram_inverse, normal_inverse = inverses
    root = gram_inverse.T

    across = lambda matrix, vector: jnp.sum(matrix * vector, 1, keepdims=True)
    down = lambda matrix, vector: jnp.sum(matrix * vector, 0, keepdims=True)
    state = jnp.where(index == jnp.max(index), 1.0, 0.0)
    eye = jnp.where(row == column, 1.0, 0.0)
    history = []
    for _ in range(STEPS):
        old = state
        right = down(eye, across(project, state)) + STEP_SIZE * load
        state = down(normal_inverse, across(normal_inverse, right))
        history.append(down(root, across(gram, state)))
    return root, history, state - old, state


def final_kernel(
    inverse_count,
    place_ref,
    low_ref,
    high_ref,
    index_ref,
    force_ref,
    snap,
    image,
    basis_any,
    coeff_ref,
    residual_ref,
    pack,
    root_ref,
    change_ref,
    state_ref,
    tile,
    basis,
    sems,
):
    rows, snaps = snap.shape
    block = force_ref.shape[1]
    chunks = rows // CHUNK
    per_chunk = CHUNK // block

    def chunk(i):
        return pl.ds(pl.multiple_of(i * CHUNK, CHUNK), CHUNK)

    def out_copy(i):
        return pltpu.make_async_copy(basis.at[chunk(i), :], basis_any.at[chunk(i), :], sems.at[i])

    pack[: PARTS // 2] = low_ref[...]
    pack[PARTS // 2 :] = high_ref[...]
    root, history, change, state = reduced_system(inverse_count, place_ref[0], pack, index_ref[...])
    high, low = split(root)
    root_ref[:, :snaps] = high
    root_ref[:, snaps:] = low
    for n in range(STEPS):
        coeff_ref[n : n + 1, :] = history[n]
    change_ref[...] = change
    state_ref[...] = state
    tile[...] = jnp.zeros_like(tile)
    lane = lax.broadcasted_iota(jnp.int32, (block, block), 1)

    @pl.loop(0, chunks)
    def _(i):
        at = chunk(i)
        panel = snap[at, :]
        sums = jnp.sum(panel * change_ref[...] + image[at, :] * state_ref[...], 1, keepdims=True)
        gathered = tile[...]
        for k in range(per_chunk):
            gathered = jnp.where(lane == i * per_chunk + k, sums[k * block : (k + 1) * block], gathered)
        tile[...] = gathered
        panel_high, panel_low = split(panel)
        both = matmul(panel_high, root_ref[...])
        basis[at, :] = both[:, :snaps] + both[:, snaps:] + matmul(panel_low, root_ref[:, :snaps])
        out_copy(i).start()

    residual_ref[...] = tile[...].T[: rows // block] - STEP_SIZE * force_ref[...]

    @pl.loop(0, chunks)
    def _(i):
        out_copy(i).wait()


def final_call(pieces, step_index, place, snapshots, image, force, inverse_count):
    rows, snaps = snapshots.shape
    block = force.shape[1]
    share = snaps // PARTS
    vmem = pl.BlockSpec(memory_space=pltpu.VMEM)
    hbm = pl.BlockSpec(memory_space=pl.ANY)
    return pl.pallas_call(
        functools.partial(final_kernel, inverse_count),
        out_shape=(
            jax.ShapeDtypeStruct((rows, snaps), F32),
            jax.ShapeDtypeStruct((STEPS, snaps), F32),
            jax.ShapeDtypeStruct(force.shape, F32),
        ),
        in_specs=[pl.BlockSpec(memory_space=pltpu.SMEM)] + [vmem] * 6,
        out_specs=[hbm, vmem, vmem],
        scratch_shapes=[
            pltpu.VMEM((PARTS, 2 * share + 8, snaps), F32),
            pltpu.VMEM((snaps, 2 * snaps), BF16),
            pltpu.VMEM((1, snaps), F32),
            pltpu.VMEM((1, snaps), F32),
            pltpu.VMEM((block, block), F32),
            pltpu.VMEM((rows, snaps), F32),
            pltpu.SemaphoreType.DMA((rows // CHUNK,)),
        ],
        compiler_params=pltpu.CompilerParams(vmem_limit_bytes=18 * MIB),
        name="final",
    )(place, *pieces, step_index, force, snapshots, image)


def shifted(value, axis, steps):
    count = lax.axis_size(axis)
    pairs = [(source, (source + steps) % count) for source in range(count)]
    return lax.ppermute(value, axis, pairs)


def from_behind(shard, axis, by):
    devices = lax.axis_size(axis)
    pairs = [(i, i + by) for i in range(devices) if 0 <= i + by < devices]
    return lax.ppermute(shard, axis, pairs)


def partner(value, axis, bit):
    count = lax.axis_size(axis)
    return lax.ppermute(value, axis, [(i, i ^ bit) for i in range(count)])


def across(value, line_bit, zone_bit):
    zones = lax.axis_size("zone")
    count = zones * lax.axis_size("rows")
    pairs = [(i, (i // zones ^ line_bit) * zones + (i % zones ^ zone_bit)) for i in range(count)]
    return lax.ppermute(value, ("rows", "zone"), pairs)


def reduce_packed(keep, send):
    value = keep + partner(send, "zone", 1)
    ways = ((1, 0), (0, 2), (1, 2))
    others = [across(value[at + 1 : at + 2], *way) for at, way in enumerate(ways)]
    value = value[:1] + others[0] + others[1] + others[2]
    for axis, bit in (("rows", 2), ("zone", 4)):
        while bit < lax.axis_size(axis):
            value = value + partner(value, axis, bit)
            bit *= 2
    value = jnp.concatenate([value] + [across(value, *way) for way in ways], 0)
    return value, partner(value, "zone", 1)


def shards(snapshots, tangent, pattern, forcing, step_index):
    rows, snaps = snapshots.shape
    blocks = pattern.shape[0]
    block = rows // blocks
    edge = HALO * block
    inverse_count = 1.0 / (rows * lax.axis_size("rows") * lax.axis_size("zone"))
    place = (lax.axis_index("zone") & 3) | ((lax.axis_index("rows") & 1) << 2)
    place = jnp.reshape(place, (1,)).astype(jnp.int32)
    force = forcing.reshape(blocks, block)
    head, tail = snapshots[:edge], snapshots[rows - edge :]
    rows_prev = shifted(tail, "rows", 1)
    rows_next = shifted(head, "rows", -1)
    field, turned, gram, load = gram_call(snapshots, force)
    halos = (from_behind(tail, "zone", 1), rows_prev, from_behind(head, "zone", -1), rows_next)
    image, *packed = tangent_call(field, turned, halos, tangent, pattern, force, gram, load, place)
    pieces = reduce_packed(*packed)
    basis, coefficients, residual = final_call(
        pieces, step_index.reshape(1, snaps), place, snapshots, image, force, inverse_count
    )
    return basis, coefficients, residual.reshape(rows)


def solution(mesh):
    in_specs = (
        P(("rows", "zone"), None),
        P(("rows", "zone"), None),
        P(("rows", "zone"), None),
        P(("rows", "zone")),
        P(),
    )
    out_specs = (P(("rows", "zone"), None), P(), P(("rows", "zone")))
    return jax.shard_map(shards, mesh=mesh, in_specs=in_specs, out_specs=out_specs, check_vma=False)
```
